128 devices in a mesh: rows: 64 (over y, z, x), grp: 2 (over core).
Axes of the slice: x: 4, y: 4, z: 4, core: 2. Of those that a mesh axis runs over, the one named last changes fastest.
Arguments:
- start_basis: bfloat16 [65536, 64], P(('rows', 'grp')), may hold values from -6 to 6
- kernel_blocks: bfloat16 [11776, 256, 256], P(('rows', 'grp')), may hold values from -0.0390625 to 0.0390625
- block_row: int32 [11776], P(('rows', 'grp')), may hold values from 0 to 255, as said below
- block_col: int32 [11776], P(('rows', 'grp')), may hold values from 0 to 255, as said below
- block_count: int32 [128], P(('rows', 'grp')), may hold values from 1 to 92, as said below
Outputs:
- embedding: float32 [65536, 64], P(('rows', 'grp'))
- projected: float32 [64, 64], replicated
The draws below stay inside these ranges and needn't reach their ends.
Inputs may be any that keep to these rules, and one draw needn't show every extreme that they name: block_count[d] is the number of live slots of device d, its first ones; device 0 has all 92 live and the last device has 1. `block_row`: each slot's row block is one of its own device's 2 row blocks. `block_col`: each slot's column block is at least its row block; among one device's live slots at most 1 have their column block on any one device, the last device's live slots all lie on itself, and device 0 has a live slot whose column block lies on the last device.
All inputs are finite; a program needn't handle non-finite values.
Results may differ from the reference program's by a relative error of at most 0.0034.
Values may be sent and summed in bfloat16 or wider, within the bound.
No kernel may reach another device: no remote copies, remote signals or barrier semaphores. Data moves between devices by JAX's collectives and lax.ppermute only.
A program may use at most 128 MiB of HBM per device.

```python
import jax
import jax.numpy as jnp
from jax import lax

B = 256
C = 64
ITERS = 2
RB_DEV = 2
SLOTS = 92
ROW_BLOCKS = 256
TOTAL_ROWS = 65536
TOTAL_SLOTS = 11776


def layout(key):
    devices = TOTAL_SLOTS // SLOTS
    device_ids = jnp.arange(devices, dtype=jnp.int32)
    base_count = (SLOTS * (devices - device_ids) + devices - 1) // devices
    cut_count = jax.random.randint(jax.random.fold_in(key, 11), (devices,), 0, max(1, SLOTS // 8) + 1)
    cut_count = jnp.where((device_ids == 0) | (device_ids == devices - 1), 0, cut_count)
    live_count = jnp.maximum(base_count - cut_count, 1)
    slot_ids = jnp.arange(SLOTS, dtype=jnp.int32)
    alive_mask = slot_ids[None, :] < live_count[:, None]
    random_keys = jax.random.randint(jax.random.fold_in(key, 12), (devices, SLOTS), 0, 1 << 19)
    scores = (jnp.where(alive_mask, 0, 1 << 20) + random_keys) * SLOTS + slot_ids[None, :]
    sort_order = jnp.argsort(scores, axis=1, stable=True)
    live_rank = jnp.argsort(sort_order, axis=1, stable=True).astype(jnp.int32)
    reach_span = devices - device_ids
    offset = jax.random.randint(jax.random.fold_in(key, 13), (devices,), 0, 1 << 20) % reach_span
    offset = jnp.where(device_ids == 0, devices - 1, offset)
    target_dev = device_ids[:, None] + (live_rank + offset[:, None]) % reach_span[:, None]
    row_local = jax.random.randint(jax.random.fold_in(key, 14), (devices, SLOTS), 0, RB_DEV)
    col_pick = jax.random.randint(jax.random.fold_in(key, 15), (devices, SLOTS), 0, 1 << 20)
    self_target = target_dev == device_ids[:, None]
    col_local = jnp.where(self_target, row_local + col_pick % (RB_DEV - row_local), col_pick % RB_DEV)
    row_ids = device_ids[:, None] * RB_DEV + row_local
    col_ids = target_dev * RB_DEV + col_local
    return (row_ids.reshape(-1).astype(jnp.int32), col_ids.reshape(-1).astype(jnp.int32), live_count.astype(jnp.int32))


def draw_block_row(key, part):
    return layout(key)[0]


def draw_block_col(key, part):
    return layout(key)[1]


def draw_block_count(key, part):
    return layout(key)[2]


def shard_levels(key, extent, shards, smallest, high):
    factor_of = 1.0
    for axis_at, blocks in shards:
        steps = jax.random.uniform(jax.random.fold_in(jax.random.fold_in(key, 6), axis_at), (blocks,), jnp.float32, smallest / len(shards), high / len(shards))
        factor_of = factor_of * jnp.repeat(jnp.exp(steps), extent[axis_at] // blocks).reshape((-1,) + (1,) * (len(extent) - 1 - axis_at))
    return factor_of


def centred(rng, dims, deviation, bound, pieces=(), kind=jnp.bfloat16):
    entries = deviation * jax.random.normal(rng, dims, jnp.float32)
    if pieces:
        entries = entries * shard_levels(rng, dims, pieces, -0.22, 0.18)
    return jnp.clip(entries, -bound, bound).astype(kind)


def setup_inputs(seed: int = 0) -> dict:
    streams_of = jax.random.split(jax.random.key(seed), 6)
    start_basis = centred(streams_of[0], (TOTAL_ROWS, C), 1.0, 6.0, ((0, 128),))
    kernel_blocks = centred(streams_of[1], (TOTAL_SLOTS, B, B), (B * SLOTS) ** -0.5, 0.0390625, ((0, 128),))
    block_row = draw_block_row(jax.random.fold_in(streams_of[5], 71), 0)
    block_col = draw_block_col(jax.random.fold_in(streams_of[5], 71), 0)
    block_count = draw_block_count(jax.random.fold_in(streams_of[5], 71), 0)
    return dict(start_basis=start_basis, kernel_blocks=kernel_blocks, block_row=block_row, block_col=block_col, block_count=block_count)


def image_of(kernel_blocks, block_row, block_col, block_count, basis):
    devices = TOTAL_SLOTS // SLOTS
    basis_tiles = basis.reshape(ROW_BLOCKS, B, C)
    stacked = kernel_blocks.reshape(devices, SLOTS, B, B)
    row_lists = block_row.reshape(devices, SLOTS)
    col_lists = block_col.reshape(devices, SLOTS)

    def visit(running, inputs):
        blocks, row_ids, col_ids, live_total = inputs
        alive_mask = (jnp.arange(SLOTS, dtype=jnp.int32) < live_total).astype(jnp.float32)[:, None, None]
        blocks_wide = blocks.astype(jnp.float32)
        forward = jnp.einsum('sij,sjc->sic', blocks_wide, basis_tiles[col_ids].astype(jnp.float32), precision=lax.Precision.HIGHEST)
        mirrored = jnp.einsum('sji,sjc->sic', blocks_wide, basis_tiles[row_ids].astype(jnp.float32), precision=lax.Precision.HIGHEST).astype(jnp.bfloat16)
        mirrored = lax.optimization_barrier(mirrored).astype(jnp.float32)
        running = running.at[row_ids].add(forward * alive_mask).at[col_ids].add(mirrored * alive_mask)
        return (running, None)
    running, _ = lax.scan(visit, jnp.zeros((ROW_BLOCKS, B, C), jnp.float32), (stacked, row_lists, col_lists, block_count))
    return running.reshape(TOTAL_ROWS, C)

def reference(start_basis, kernel_blocks, block_row, block_col, block_count):
    basis = start_basis
    result = None
    projected = None
    for iteration in range(ITERS):
        image_rows = image_of(kernel_blocks, block_row, block_col, block_count, basis)
        gram_part = jnp.dot(image_rows.T, image_rows, precision=lax.Precision.HIGHEST) / TOTAL_ROWS
        if iteration == ITERS - 1:
            projected = jnp.dot(basis.astype(jnp.float32).T, image_rows, precision=lax.Precision.HIGHEST) / TOTAL_ROWS
        lower_factor = jnp.linalg.cholesky(gram_part)
        inverse = jax.scipy.linalg.solve_triangular(lower_factor, jnp.eye(C, dtype=jnp.float32), lower=True)
        result = jnp.dot(image_rows, inverse.T, precision=lax.Precision.HIGHEST)
        basis = result.astype(jnp.bfloat16)
    return (result, projected)
```

```python
import functools

import jax
import jax.numpy as jnp
from jax import lax
from jax.experimental import pallas as pl
from jax.experimental.pallas import tpu as pltpu
from jax.sharding import PartitionSpec as P

AXES = ("rows", "grp")
HIGHEST = lax.Precision.HIGHEST
CHUNK = 4
NT = (((1,), (1,)), ((), ()))
VMEM = pl.BlockSpec(memory_space=pltpu.VMEM)
SMEM = pl.BlockSpec(memory_space=pltpu.SMEM)
ANY = pl.BlockSpec(memory_space=pl.ANY)


def block_copies(blocks_ref, held, sems):
    chunks = blocks_ref.shape[0] // CHUNK
    return [
        pltpu.make_async_copy(
            blocks_ref.at[pl.ds(i * CHUNK, CHUNK)], held.at[pl.ds(i * CHUNK, CHUNK)], sems.at[i]
        )
        for i in range(chunks)
    ]


def wait_chunk(blocks_ref, held, sems, i):
    at = pl.ds(i * CHUNK, CHUNK)
    pltpu.make_async_copy(blocks_ref.at[at], held.at[at], sems.at[i]).wait()


def mirror_blocks(me, row_ref, col_ref, count_ref, tiles_ref, blocks_ref, held, sems, out_ref):
    live = count_ref[0]
    row_blocks = tiles_ref.shape[0]

    def visit(i, carry):
        wait_chunk(blocks_ref, held, sems, i)
        for j in range(CHUNK):
            s = i * CHUNK + j
            local = row_ref[s] - me * row_blocks
            place = jnp.where(s < live, col_ref[s] // row_blocks, 0)
            product = jnp.dot(tiles_ref[local], held[s], preferred_element_type=jnp.float32)
            out_ref[place] = product.astype(out_ref.dtype)
        return carry

    lax.fori_loop(0, held.shape[0] // CHUNK, visit, 0)


def place_tiles(me, wanted_ref, tiles_ref, out_ref):
    def visit(d, carry):
        @pl.when(wanted_ref[d] >= 0)
        def _():
            out_ref[d] = tiles_ref[wanted_ref[d]]

        return carry

    lax.fori_loop(0, me, visit, 0)


def first_kernel(me_ref, row_ref, col_ref, count_ref, basis_ref, blocks_ref, out_ref, tiles_ref, held, sems):
    for copy in block_copies(blocks_ref, held, sems):
        copy.start()
    row_blocks, _, size = tiles_ref.shape
    for j in range(row_blocks):
        rows = basis_ref[j * size : (j + 1) * size, :].astype(jnp.float32)
        tiles_ref[j] = rows.T.astype(tiles_ref.dtype)
    mirror_blocks(me_ref[0], row_ref, col_ref, count_ref, tiles_ref, blocks_ref, held, sems, out_ref)


def place_kernel(me_ref, wanted_ref, tiles_ref, given_ref, out_ref):
    del given_ref
    place_tiles(me_ref[0], wanted_ref, tiles_ref, out_ref)


def fold(square):
    half = square.shape[0] // 2
    return jnp.concatenate([square[:half], square[half:]], axis=1)


def unfold(folded):
    half = folded.shape[1] // 2
    return jnp.concatenate([folded[:, :half], folded[:, half:]], axis=0)


def image_kernel(
    with_projection, me_ref, row_ref, col_ref, count_ref, wanted_ref, tiles_ref, arrived_ref, blocks_ref,
    image_ref, sums_ref, held, sems,
):
    for copy in block_copies(blocks_ref, held, sems):
        copy.start()
    me, live = me_ref[0], count_ref[0]
    row_blocks = tiles_ref.shape[0]
    image_ref[...] = jnp.zeros_like(image_ref)

    def add_mirror(d, carry):
        @pl.when(wanted_ref[d] >= 0)
        def _():
            image_ref[wanted_ref[d]] += arrived_ref[d].astype(jnp.float32)

        return carry

    lax.fori_loop(0, me + 1, add_mirror, 0)

    def visit(i, carry):
        wait_chunk(blocks_ref, held, sems, i)
        for j in range(CHUNK):
            s = i * CHUNK + j
            local = row_ref[s] - me * row_blocks
            column = col_ref[s]
            owner = column // row_blocks
            tile = jnp.where(owner == me, tiles_ref[column - owner * row_blocks], arrived_ref[owner])
            tile = jnp.where(s < live, tile, jnp.zeros_like(tile))
            image_ref[local] += lax.dot_general(tile, held[s], NT, preferred_element_type=jnp.float32)
        return carry

    lax.fori_loop(0, held.shape[0] // CHUNK, visit, 0)

    def summed(left_ref):
        total = None
        for j in range(row_blocks):
            term = lax.dot_general(
                left_ref[j].astype(jnp.float32), image_ref[j], NT, precision=HIGHEST,
                preferred_element_type=jnp.float32,
            )
            total = term if total is None else total + term
        return fold(total)

    parts = [summed(image_ref)] + ([summed(tiles_ref)] if with_projection else [])
    half = sums_ref.shape[1] // len(parts)
    for c in range(2):
        for k, part in enumerate(parts):
            sums_ref[c, k * half : (k + 1) * half, :] = part[c * half : (c + 1) * half, :]


def inverse_factor(gram):
    n = gram.shape[0]
    row_at = lax.broadcasted_iota(jnp.int32, (n, n), 0)
    col_at = lax.broadcasted_iota(jnp.int32, (n, n), 1)
    identity = (row_at == col_at).astype(jnp.float32)
    work = jnp.concatenate([gram, identity], axis=1)
    at = lax.broadcasted_iota(jnp.int32, (n, 1), 0)
    scale = jnp.zeros((n, 1), jnp.float32)
    for k in range(n):
        row = work[k : k + 1, :]
        column = work[:, k : k + 1]
        pivot = row[:, k : k + 1]
        factor = jnp.where(at > k, column, 0.0) / pivot
        scale = jnp.where(at == k, pivot, scale)
        work = work - factor * row
    return work[:, n:] * (1.0 / jnp.sqrt(scale))


def whole_sum(core, own_ref, other_ref, k, parts):
    half = own_ref.shape[0] // parts
    own = own_ref[k * half : (k + 1) * half, :]
    other = other_ref[k * half : (k + 1) * half, :]
    first = jnp.where(core == 0, own, other)
    second = jnp.where(core == 0, other, own)
    return unfold(jnp.concatenate([first, second], axis=0))


def normal_kernel(
    total_rows, me_ref, row_ref, col_ref, count_ref, wanted_ref, own_ref, other_ref, image_ref, blocks_ref,
    out_ref, tiles_ref, held, sems,
):
    for copy in block_copies(blocks_ref, held, sems):
        copy.start()
    me = me_ref[0]
    inverse = inverse_factor(whole_sum(me % 2, own_ref, other_ref, 0, 1) / total_rows)
    for j in range(tiles_ref.shape[0]):
        tiles_ref[j] = jnp.dot(
            inverse, image_ref[j], precision=HIGHEST, preferred_element_type=jnp.float32
        ).astype(tiles_ref.dtype)
    mirror_blocks(me, row_ref, col_ref, count_ref, tiles_ref, blocks_ref, held, sems, out_ref)
    place_tiles(me, wanted_ref, tiles_ref, out_ref)


def last_kernel(total_rows, me_ref, own_ref, other_ref, image_ref, result_ref, projected_ref):
    core = me_ref[0] % 2
    inverse = inverse_factor(whole_sum(core, own_ref, other_ref, 0, 2) / total_rows)
    size = image_ref.shape[2]
    for j in range(image_ref.shape[0]):
        result = jnp.dot(inverse, image_ref[j], precision=HIGHEST, preferred_element_type=jnp.float32)
        result_ref[j * size : (j + 1) * size, :] = result.T
    projected_ref[...] = whole_sum(core, own_ref, other_ref, 1, 2) / total_rows


def sum_over_devices(halves):
    core = lax.axis_index("grp")
    swap = [(0, 1), (1, 0)]
    mine = lax.dynamic_index_in_dim(halves, core, 0, keepdims=False)
    given = lax.dynamic_index_in_dim(halves, 1 - core, 0, keepdims=False)
    mine = mine + lax.ppermute(given, "grp", swap)
    spread = jnp.broadcast_to(mine[None], (lax.axis_size("rows"),) + mine.shape)
    own = jnp.sum(lax.all_to_all(spread, "rows", 0, 0, tiled=True), axis=0)
    return own, lax.ppermute(own, "grp", swap)


def on_device(start_basis, kernel_blocks, block_row, block_col, block_count):
    devices = lax.axis_size(AXES)
    me = lax.axis_index(AXES)
    slots, size, _ = kernel_blocks.shape
    own_rows, columns = start_basis.shape
    row_blocks = own_rows // size
    total_rows = own_rows * devices
    me_array = me.reshape(1).astype(jnp.int32)

    owner = block_col // row_blocks
    alive = jnp.arange(slots, dtype=jnp.int32) < block_count[0]
    asked = jnp.max(
        jnp.where(
            (owner[None, :] == jnp.arange(devices, dtype=jnp.int32)[:, None]) & alive[None, :],
            (block_col - owner * row_blocks)[None, :],
            -1,
        ),
        axis=1,
    )
    wanted = lax.all_to_all(asked, AXES, split_axis=0, concat_axis=0, tiled=True)

    params = pltpu.CompilerParams(vmem_limit_bytes=48 * 1024 * 1024)
    scratch = [
        pltpu.VMEM(kernel_blocks.shape, kernel_blocks.dtype),
        pltpu.SemaphoreType.DMA((slots // CHUNK,)),
    ]
    tiles_shape = jax.ShapeDtypeStruct((row_blocks, columns, size), jnp.bfloat16)
    image_shape = jax.ShapeDtypeStruct((row_blocks, columns, size), jnp.float32)
    out_shape = jax.ShapeDtypeStruct((devices, columns, size), jnp.bfloat16)

    def image_of(tiles, arrived, with_projection):
        parts = 2 if with_projection else 1
        sums_shape = jax.ShapeDtypeStruct((2, parts * columns // 4, 2 * columns), jnp.float32)
        return pl.pallas_call(
            functools.partial(image_kernel, with_projection),
            out_shape=(image_shape, sums_shape),
            in_specs=[SMEM] * 5 + [VMEM] * 2 + [ANY],
            out_specs=(VMEM, VMEM),
            scratch_shapes=scratch,
            compiler_params=params,
        )(me_array, block_row, block_col, block_count, wanted, tiles, arrived, kernel_blocks)

    def exchange(outgoing):
        return lax.all_to_all(outgoing, AXES, split_axis=0, concat_axis=0, tiled=True)

    outgoing, tiles = pl.pallas_call(
        first_kernel,
        out_shape=(out_shape, tiles_shape),
        in_specs=[SMEM] * 4 + [VMEM, ANY],
        out_specs=(VMEM, VMEM),
        scratch_shapes=scratch,
        compiler_params=params,
    )(me_array, block_row, block_col, block_count, start_basis, kernel_blocks)
    outgoing = pl.pallas_call(
        place_kernel,
        out_shape=out_shape,
        in_specs=[SMEM] * 2 + [VMEM] * 2,
        out_specs=VMEM,
        input_output_aliases={3: 0},
        compiler_params=params,
    )(me_array, wanted, tiles, outgoing)
    image, sums = image_of(tiles, exchange(outgoing), False)
    own, other = sum_over_devices(sums)
    outgoing, tiles = pl.pallas_call(
        functools.partial(normal_kernel, total_rows),
        out_shape=(out_shape, tiles_shape),
        in_specs=[SMEM] * 5 + [VMEM] * 3 + [ANY],
        out_specs=(VMEM, VMEM),
        scratch_shapes=scratch,
        compiler_params=params,
    )(me_array, block_row, block_col, block_count, wanted, own, other, image, kernel_blocks)
    image, sums = image_of(tiles, exchange(outgoing), True)
    own, other = sum_over_devices(sums)
    return pl.pallas_call(
        functools.partial(last_kernel, total_rows),
        out_shape=(
            jax.ShapeDtypeStruct((own_rows, columns), jnp.float32),
            jax.ShapeDtypeStruct((columns, columns), jnp.float32),
        ),
        in_specs=[SMEM] + [VMEM] * 3,
        out_specs=(VMEM, VMEM),
        compiler_params=params,
    )(me_array, own, other, image)


def solution(mesh):
    in_specs = (
        P(AXES, None),
        P(AXES, None, None),
        P(AXES),
        P(AXES),
        P(AXES),
    )
    out_specs = (P(AXES, None), P())
    return jax.shard_map(
        on_device, mesh=mesh, in_specs=in_specs, out_specs=out_specs, check_vma=False
    )
```

```python
import functools

import jax
import jax.numpy as jnp
from jax import lax
from jax.experimental import pallas as pl
from jax.experimental.pallas import tpu as pltpu
from jax.sharding import PartitionSpec as P

AXES = ("rows", "grp")
HIGHEST = lax.Precision.HIGHEST
CHUNK = 4
PANEL = 8
ME, LIVE, FIRST = 0, 1, 2
NT = (((1,), (1,)), ((), ()))
VMEM = pl.BlockSpec(memory_space=pltpu.VMEM)
SMEM = pl.BlockSpec(memory_space=pltpu.SMEM)
ANY = pl.BlockSpec(memory_space=pl.ANY)
MIB = 1024 * 1024


def block_copy(blocks_ref, held, sems, i):
    at = pl.ds(i * CHUNK, CHUNK)
    return pltpu.make_async_copy(blocks_ref.at[at], held.at[at], sems.at[i])


def start_blocks(live, blocks_ref, held, sems):
    chunks = (live + CHUNK - 1) // CHUNK

    def start(i, carry):
        block_copy(blocks_ref, held, sems, i).start()
        return carry

    lax.fori_loop(0, chunks, start, 0)
    return chunks


def multiply_mirrors(me, table_ref, live, chunks, tiles_ref, blocks_ref, held, sems, out_ref):
    row_blocks = tiles_ref.shape[0]

    def visit(i, carry):
        block_copy(blocks_ref, held, sems, i).wait()
        for j in range(CHUNK):
            s = i * CHUNK + j
            local = table_ref[FIRST + s] - me * row_blocks
            place = jnp.where(s < live, table_ref[FIRST + held.shape[0] + s] // row_blocks, 0)
            product = jnp.dot(tiles_ref[local], held[s], preferred_element_type=jnp.float32)
            out_ref[place] = product.astype(out_ref.dtype)
        return carry

    lax.fori_loop(0, chunks, visit, 0)


def place_tiles(me, wanted_ref, tiles_ref, out_ref):
    def visit(i, carry):
        for j in range(CHUNK):
            d = jnp.minimum(i * CHUNK + j, me - 1)
            out_ref[d] = tiles_ref[jnp.maximum(wanted_ref[d], 0)]
        return carry

    lax.fori_loop(0, (me + CHUNK - 1) // CHUNK, visit, 0)


def ask_kernel(row_blocks, count_ref, col_ref, out_ref):
    devices, slots = out_ref.shape[0], col_ref.shape[1]
    column = jnp.broadcast_to(col_ref[...], (devices, slots))
    owner = column // row_blocks
    device = lax.broadcasted_iota(jnp.int32, (devices, slots), 0)
    alive = lax.broadcasted_iota(jnp.int32, (devices, slots), 1) < count_ref[0]
    block = jnp.where((owner == device) & alive, column - owner * row_blocks, -1)
    asked = jnp.max(block, axis=1, keepdims=True)
    out_ref[...] = jnp.broadcast_to(asked, (devices, out_ref.shape[2]))[:, None, :]


def first_kernel(table_ref, basis_ref, blocks_ref, out_ref, tiles_ref, held, sems):
    live = table_ref[LIVE]
    chunks = start_blocks(live, blocks_ref, held, sems)
    row_blocks, _, size = tiles_ref.shape
    for j in range(row_blocks):
        tiles_ref[j] = basis_ref[:, j * size : (j + 1) * size]
    multiply_mirrors(table_ref[ME], table_ref, live, chunks, tiles_ref, blocks_ref, held, sems, out_ref)


def place_kernel(table_ref, wanted_ref, tiles_ref, given_ref, out_ref):
    me = table_ref[ME]
    place_tiles(me, wanted_ref, tiles_ref, out_ref)

    def keep(i, carry):
        for j in range(CHUNK):
            d = jnp.minimum(me + i * CHUNK + j, out_ref.shape[0] - 1)
            out_ref[d] = given_ref[d]
        return carry

    lax.fori_loop(0, (out_ref.shape[0] - me + CHUNK - 1) // CHUNK, keep, 0)


def fold(square):
    half = square.shape[0] // 2
    return jnp.concatenate([square[:half], square[half:]], axis=1)


def unfold(folded):
    half = folded.shape[1] // 2
    return jnp.concatenate([folded[:, :half], folded[:, half:]], axis=0)


def image_kernel(
    with_projection, table_ref, wanted_ref, tiles_ref, arrived_ref, blocks_ref,
    image_ref, own_ref, given_ref, held, sems,
):
    me, live = table_ref[ME], table_ref[LIVE]
    chunks = start_blocks(live, blocks_ref, held, sems)
    row_blocks = tiles_ref.shape[0]
    image_ref[...] = jnp.zeros_like(image_ref)

    def add_mirror(d, carry):
        @pl.when(wanted_ref[d] >= 0)
        def _():
            image_ref[wanted_ref[d]] += arrived_ref[d].astype(jnp.float32)

        return carry

    lax.fori_loop(0, me + 1, add_mirror, 0)

    def visit(i, carry):
        block_copy(blocks_ref, held, sems, i).wait()
        for j in range(CHUNK):
            s = i * CHUNK + j
            local = table_ref[FIRST + s] - me * row_blocks
            column = table_ref[FIRST + held.shape[0] + s]
            owner = column // row_blocks
            tile = jnp.where(owner == me, tiles_ref[column - owner * row_blocks], arrived_ref[owner])
            tile = jnp.where(s < live, tile, jnp.zeros_like(tile))
            image_ref[local] += lax.dot_general(tile, held[s], NT, preferred_element_type=jnp.float32)
        return carry

    lax.fori_loop(0, chunks, visit, 0)

    def summed(left_ref):
        total = None
        for j in range(image_ref.shape[0]):
            term = lax.dot_general(
                left_ref[j].astype(jnp.float32), image_ref[j], NT, precision=HIGHEST,
                preferred_element_type=jnp.float32,
            )
            total = term if total is None else total + term
        return fold(total)

    parts = [summed(image_ref)] + ([summed(tiles_ref)] if with_projection else [])
    half = own_ref.shape[0] // len(parts)
    for k, folded in enumerate(parts):
        at = slice(k * half, (k + 1) * half)
        low, high = folded[:half], folded[half:]
        own_ref[at, :] = jnp.where(me % 2 == 0, low, high)
        given_ref[at, :] = jnp.where(me % 2 == 0, high, low)


def inverse_factor(gram):
    n = gram.shape[0]
    row_at = lax.broadcasted_iota(jnp.int32, (n, n), 0)
    col_at = lax.broadcasted_iota(jnp.int32, (n, n), 1)
    work = jnp.concatenate([gram, (row_at == col_at).astype(jnp.float32)], axis=1)
    at = lax.broadcasted_iota(jnp.int32, work.shape, 0)
    pivots = jnp.zeros(work.shape, jnp.float32)
    for k in range(0, n, PANEL):
        spread = [jnp.broadcast_to(work[:, k + j : k + j + 1], work.shape) for j in range(PANEL)]
        rows = [work[k + j : k + j + 1, :] for j in range(PANEL)]
        for j in range(PANEL):
            pivot = spread[j][k + j : k + j + 1, :]
            pivots = jnp.where(at == k + j, pivot, pivots)
            share = 1.0 / pivot
            scaled = rows[j] * share
            for m in range(j + 1, PANEL):
                spread[m] = spread[m] - spread[j] * (spread[m][k + j : k + j + 1, :] * share)
                rows[m] = rows[m] - spread[j][k + m : k + m + 1, :] * scaled
            rows[j] = scaled
        for j in range(PANEL):
            work = work - jnp.where(at > k + j, spread[j], 0.0) * rows[j]
    return work[:, n:] * (1.0 / jnp.sqrt(pivots[:, n:]))


def whole_sum(core, own_ref, other_ref, k, parts):
    half = own_ref.shape[0] // parts
    own = own_ref[k * half : (k + 1) * half, :]
    other = other_ref[k * half : (k + 1) * half, :]
    first = jnp.where(core == 0, own, other)
    second = jnp.where(core == 0, other, own)
    return unfold(jnp.concatenate([first, second], axis=0))


def normal_kernel(
    total_rows, table_ref, wanted_ref, own_ref, other_ref, image_ref, blocks_ref,
    out_ref, tiles_ref, held, sems,
):
    me, live = table_ref[ME], table_ref[LIVE]
    chunks = start_blocks(live, blocks_ref, held, sems)
    inverse = inverse_factor(whole_sum(me % 2, own_ref, other_ref, 0, 1) / total_rows)
    for j in range(tiles_ref.shape[0]):
        tiles_ref[j] = jnp.dot(
            inverse, image_ref[j], precision=HIGHEST, preferred_element_type=jnp.float32
        ).astype(tiles_ref.dtype)
    multiply_mirrors(me, table_ref, live, chunks, tiles_ref, blocks_ref, held, sems, out_ref)
    place_tiles(me, wanted_ref, tiles_ref, out_ref)


def last_kernel(total_rows, table_ref, own_ref, other_ref, image_ref, result_ref, projected_ref):
    core = table_ref[ME] % 2
    inverse = inverse_factor(whole_sum(core, own_ref, other_ref, 0, 2) / total_rows)
    size = image_ref.shape[2]
    for j in range(image_ref.shape[0]):
        result_ref[:, j * size : (j + 1) * size] = jnp.dot(
            inverse, image_ref[j], precision=HIGHEST, preferred_element_type=jnp.float32
        )
    projected_ref[...] = whole_sum(core, own_ref, other_ref, 1, 2) / total_rows


def sum_over_devices(mine, given):
    swap = [(0, 1), (1, 0)]
    mine = mine + lax.ppermute(given, "grp", swap)
    spread = jnp.broadcast_to(mine[None], (lax.axis_size("rows"),) + mine.shape)
    own = jnp.sum(lax.all_to_all(spread, "rows", 0, 0, tiled=True), axis=0)
    return own, lax.ppermute(own, "grp", swap)


def exchange(outgoing):
    return lax.all_to_all(outgoing, AXES, split_axis=0, concat_axis=0, tiled=True)


def on_device(start_basis, kernel_blocks, block_row, block_col, block_count):
    devices = lax.axis_size(AXES)
    me = lax.axis_index(AXES)
    slots, size, _ = kernel_blocks.shape
    own_rows, columns = start_basis.shape
    row_blocks = own_rows // size
    total_rows = own_rows * devices

    asked = pl.pallas_call(
        functools.partial(ask_kernel, row_blocks),
        out_shape=jax.ShapeDtypeStruct((devices, 1, 128), jnp.int32),
        in_specs=[SMEM, VMEM],
        out_specs=VMEM,
        name="ask",
    )(block_count, block_col[None, :])
    wanted = exchange(asked)[:, 0, 0]
    table = jnp.concatenate([me.reshape(1).astype(jnp.int32), block_count, block_row, block_col])

    params = pltpu.CompilerParams(vmem_limit_bytes=48 * MIB)
    scratch = [
        pltpu.VMEM(kernel_blocks.shape, kernel_blocks.dtype),
        pltpu.SemaphoreType.DMA((slots // CHUNK,)),
    ]
    tiles_shape = jax.ShapeDtypeStruct((row_blocks, columns, size), jnp.bfloat16)
    image_shape = jax.ShapeDtypeStruct((row_blocks, columns, size), jnp.float32)
    out_shape = jax.ShapeDtypeStruct((devices, columns, size), jnp.bfloat16)

    def image_of(tiles, arrived, with_projection):
        parts = 2 if with_projection else 1
        half = jax.ShapeDtypeStruct((parts * columns // 4, 2 * columns), jnp.float32)
        return pl.pallas_call(
            functools.partial(image_kernel, with_projection),
            out_shape=(image_shape, half, half),
            in_specs=[SMEM] * 2 + [VMEM] * 2 + [ANY],
            out_specs=(VMEM, VMEM, VMEM),
            scratch_shapes=scratch,
            compiler_params=params,
            name="image",
        )(table, wanted, tiles, arrived, kernel_blocks)

    outgoing, tiles = pl.pallas_call(
        first_kernel,
        out_shape=(out_shape, tiles_shape),
        in_specs=[SMEM] + [VMEM, ANY],
        out_specs=(VMEM, VMEM),
        scratch_shapes=scratch,
        compiler_params=params,
        name="first",
    )(table, start_basis.T, kernel_blocks)
    outgoing = pl.pallas_call(
        place_kernel,
        out_shape=out_shape,
        in_specs=[SMEM] * 2 + [VMEM] * 2,
        out_specs=VMEM,
        compiler_params=params,
        name="place",
    )(table, wanted, tiles, outgoing)
    image, own, given = image_of(tiles, exchange(outgoing), False)
    own, other = sum_over_devices(own, given)
    outgoing, tiles = pl.pallas_call(
        functools.partial(normal_kernel, total_rows),
        out_shape=(out_shape, tiles_shape),
        in_specs=[SMEM] * 2 + [VMEM] * 3 + [ANY],
        out_specs=(VMEM, VMEM),
        scratch_shapes=scratch,
        compiler_params=params,
        name="normal",
    )(table, wanted, own, other, image, kernel_blocks)
    image, own, given = image_of(tiles, exchange(outgoing), True)
    own, other = sum_over_devices(own, given)
    result, projected = pl.pallas_call(
        functools.partial(last_kernel, total_rows),
        out_shape=(
            jax.ShapeDtypeStruct((columns, own_rows), jnp.float32),
            jax.ShapeDtypeStruct((columns, columns), jnp.float32),
        ),
        in_specs=[SMEM] + [VMEM] * 3,
        out_specs=(VMEM, VMEM),
        compiler_params=params,
        name="last",
    )(table, own, other, image)
    return result.T, projected


def solution(mesh):
    in_specs = (
        P(AXES, None),
        P(AXES, None, None),
        P(AXES),
        P(AXES),
        P(AXES),
    )
    out_specs = (P(AXES, None), P())
    return jax.shard_map(
        on_device, mesh=mesh, in_specs=in_specs, out_specs=out_specs, check_vma=False
    )
```

```python
import functools

import jax
import jax.numpy as jnp
from jax import lax
from jax.experimental import pallas as pl
from jax.experimental.pallas import tpu as pltpu
from jax.sharding import PartitionSpec as P

AXES = ("rows", "grp")
HIGHEST = lax.Precision.HIGHEST
CHUNK = 4
PANEL = 8
ROWS, LANES = 8, 128
ME, LIVE, FIRST = 0, 1, 2
NT = (((1,), (1,)), ((), ()))
VMEM = pl.BlockSpec(memory_space=pltpu.VMEM)
SMEM = pl.BlockSpec(memory_space=pltpu.SMEM)
ANY = pl.BlockSpec(memory_space=pl.ANY)
MIB = 1024 * 1024


def block_copy(blocks_ref, held, sems, i):
    at = pl.ds(i * CHUNK, CHUNK)
    return pltpu.make_async_copy(blocks_ref.at[at], held.at[at], sems.at[i])


def start_blocks(live, blocks_ref, held, sems):
    chunks = (live + CHUNK - 1) // CHUNK

    def start(i, carry):
        block_copy(blocks_ref, held, sems, i).start()
        return carry

    lax.fori_loop(0, chunks, start, 0)
    return chunks


def multiply_mirrors(me, table_ref, live, chunks, tiles_ref, blocks_ref, held, sems, out_ref):
    row_blocks = tiles_ref.shape[0]

    def visit(i, carry):
        block_copy(blocks_ref, held, sems, i).wait()
        for j in range(CHUNK):
            s = i * CHUNK + j
            local = table_ref[FIRST + s] - me * row_blocks
            place = jnp.where(s < live, table_ref[FIRST + held.shape[0] + s] // row_blocks, 0)
            product = jnp.dot(tiles_ref[local], held[s], preferred_element_type=jnp.float32)
            out_ref[place] = product.astype(out_ref.dtype)
        return carry

    lax.fori_loop(0, chunks, visit, 0)


def place_tiles(start, end, wanted_ref, tiles_ref, out_ref):
    def visit(i, carry):
        for j in range(CHUNK):
            d = jnp.minimum(start + i * CHUNK + j, end - 1)
            out_ref[d] = tiles_ref[jnp.maximum(wanted_ref[d], 0)]
        return carry

    lax.fori_loop(0, (end - start + CHUNK - 1) // CHUNK, visit, 0)


def ask_kernel(row_blocks, count_ref, col_ref, out_ref):
    devices, slots = out_ref.shape[0], col_ref.shape[1]
    column = jnp.broadcast_to(col_ref[...], (devices, slots))
    owner = column // row_blocks
    device = lax.broadcasted_iota(jnp.int32, (devices, slots), 0)
    alive = lax.broadcasted_iota(jnp.int32, (devices, slots), 1) < count_ref[0]
    block = jnp.where((owner == device) & alive, column - owner * row_blocks, -1)
    asked = jnp.max(block, axis=1, keepdims=True)
    out_ref[...] = jnp.broadcast_to(asked, (devices, out_ref.shape[2]))[:, None, :]


def first_kernel(table_ref, basis_ref, blocks_ref, out_ref, tiles_ref, held, sems):
    live = table_ref[LIVE]
    chunks = start_blocks(live, blocks_ref, held, sems)
    row_blocks, _, size = tiles_ref.shape
    for j in range(row_blocks):
        tiles_ref[j] = basis_ref[:, j * size : (j + 1) * size]
    multiply_mirrors(table_ref[ME], table_ref, live, chunks, tiles_ref, blocks_ref, held, sems, out_ref)


def place_kernel(table_ref, asked_ref, tiles_ref, given_ref, out_ref, wanted_ref, sems):
    me = table_ref[ME]
    groups = sems.shape[0]
    size = out_ref.shape[0] // groups
    first = me // size

    def copy_of(g):
        at = pl.ds(g * size, size)
        return pltpu.make_async_copy(given_ref.at[at], out_ref.at[at], sems.at[g])

    def start(g, carry):
        copy_of(g).start()
        return carry

    def wait(g, carry):
        copy_of(g).wait()
        return carry

    def compact(i, carry):
        for j in range(CHUNK):
            wanted_ref[i * CHUNK + j] = asked_ref[i * CHUNK + j, 0, 0]
        return carry

    lax.fori_loop(first, groups, start, 0)
    lax.fori_loop(0, wanted_ref.shape[0] // CHUNK, compact, 0)
    place_tiles(0, first * size, wanted_ref, tiles_ref, out_ref)
    lax.fori_loop(first, groups, wait, 0)
    place_tiles(first * size, me, wanted_ref, tiles_ref, out_ref)


def row_of(k):
    return slice(k * LANES, (k + 1) * LANES)


def fold(square):
    half = square.shape[0] // 2
    row_at = lax.broadcasted_iota(jnp.int32, (half, half), 0)
    col_at = lax.broadcasted_iota(jnp.int32, (half, half), 1)
    corner = square[half:, half:]
    mixed = jnp.where(row_at >= col_at, square[:half, :half], corner)
    sides = jnp.concatenate([mixed, square[half:, :half]], axis=1)
    folded = jnp.concatenate([sides[: half // 2], sides[half // 2 :]], axis=1)
    diagonal = jnp.sum(jnp.where(row_at == col_at, corner, 0.0), axis=0, keepdims=True)
    return folded, diagonal


def unfold(folded, diagonal):
    width = folded.shape[1] // 2
    half = width // 2
    row_at = lax.broadcasted_iota(jnp.int32, (half, half), 0)
    col_at = lax.broadcasted_iota(jnp.int32, (half, half), 1)
    sides = jnp.concatenate([folded[:, :width], folded[:, width:]], axis=0)
    mixed, side = sides[:, :half], sides[:, half:]
    turned = mixed.T
    upper = jnp.where(row_at >= col_at, mixed, turned)
    corner = jnp.where(row_at < col_at, mixed, turned)
    corner = jnp.where(row_at == col_at, jnp.broadcast_to(diagonal, (half, half)), corner)
    return jnp.concatenate(
        [jnp.concatenate([upper, side.T], axis=1), jnp.concatenate([side, corner], axis=1)], axis=0
    )


def image_kernel(
    with_projection, table_ref, wanted_ref, tiles_ref, arrived_ref, blocks_ref,
    image_ref, own_ref, given_ref, held, sems,
):
    me, live = table_ref[ME], table_ref[LIVE]
    chunks = start_blocks(live, blocks_ref, held, sems)
    row_blocks = tiles_ref.shape[0]
    image_ref[...] = jnp.zeros_like(image_ref)

    def add_mirror(d, carry):
        @pl.when(wanted_ref[d] >= 0)
        def _():
            image_ref[wanted_ref[d]] += arrived_ref[d].astype(jnp.float32)

        return carry

    lax.fori_loop(0, me + 1, add_mirror, 0)

    def visit(i, carry):
        block_copy(blocks_ref, held, sems, i).wait()
        for j in range(CHUNK):
            s = i * CHUNK + j
            local = table_ref[FIRST + s] - me * row_blocks
            column = table_ref[FIRST + held.shape[0] + s]
            owner = column // row_blocks
            tile = jnp.where(owner == me, tiles_ref[column - owner * row_blocks], arrived_ref[owner])
            tile = jnp.where(s < live, tile, jnp.zeros_like(tile))
            image_ref[local] += lax.dot_general(tile, held[s], NT, preferred_element_type=jnp.float32)
        return carry

    lax.fori_loop(0, chunks, visit, 0)

    def summed(left_ref):
        total = None
        for j in range(image_ref.shape[0]):
            term = lax.dot_general(
                left_ref[j].astype(jnp.float32), image_ref[j], NT, precision=HIGHEST,
                preferred_element_type=jnp.float32,
            )
            total = term if total is None else total + term
        return total

    squares = [summed(image_ref)]
    if with_projection:
        product = summed(tiles_ref)
        squares.append((product + product.T) * 0.5)
    diagonals = []
    for k, square in enumerate(squares):
        folded, diagonal = fold(square)
        diagonals.append(diagonal)
        low, high = folded[:ROWS], folded[ROWS:]
        own, given = jnp.where(me % 2 == 0, low, high), jnp.where(me % 2 == 0, high, low)
        for r in range(ROWS):
            at = row_of(k * ROWS + r)
            own_ref[:, at] = own[r : r + 1]
            given_ref[:, at] = given[r : r + 1]
    rest = own_ref.shape[1] // LANES - 1
    missing = LANES - len(diagonals) * diagonals[0].shape[1]
    last = jnp.concatenate(diagonals + [jnp.zeros((1, missing), jnp.float32)], axis=1)
    own_ref[:, row_of(rest)] = last
    given_ref[:, row_of(rest)] = last


def inverse_factor(gram):
    n = gram.shape[0]
    row_at = lax.broadcasted_iota(jnp.int32, (n, n), 0)
    col_at = lax.broadcasted_iota(jnp.int32, (n, n), 1)
    work = jnp.concatenate([gram, (row_at == col_at).astype(jnp.float32)], axis=1)
    at = lax.broadcasted_iota(jnp.int32, work.shape, 0)
    pivots = jnp.zeros(work.shape, jnp.float32)
    for k in range(0, n, PANEL):
        spread = [jnp.broadcast_to(work[:, k + j : k + j + 1], work.shape) for j in range(PANEL)]
        rows = [work[k + j : k + j + 1, :] for j in range(PANEL)]
        for j in range(PANEL):
            pivot = spread[j][k + j : k + j + 1, :]
            pivots = jnp.where(at == k + j, pivot, pivots)
            share = 1.0 / pivot
            scaled = rows[j] * share
            for m in range(j + 1, PANEL):
                spread[m] = spread[m] - spread[j] * (spread[m][k + j : k + j + 1, :] * share)
                rows[m] = rows[m] - spread[j][k + m : k + m + 1, :] * scaled
            rows[j] = scaled
        for j in range(PANEL):
            work = work - jnp.where(at > k + j, spread[j], 0.0) * rows[j]
    return work[:, n:] * (1.0 / jnp.sqrt(pivots[:, n:]))


def whole_sum(core, own_ref, other_ref, k):
    at = [row_of(k * ROWS + r) for r in range(ROWS)]
    own = jnp.concatenate([own_ref[:, a] for a in at], axis=0)
    other = jnp.concatenate([other_ref[:, a] for a in at], axis=0)
    rest = row_of(own_ref.shape[1] // LANES - 1)
    diagonals = jnp.where(core == 0, own_ref[:, rest], other_ref[:, rest])
    first = jnp.where(core == 0, own, other)
    second = jnp.where(core == 0, other, own)
    width = LANES // 4
    return unfold(jnp.concatenate([first, second], axis=0), diagonals[:, k * width : (k + 1) * width])


def normal_kernel(
    total_rows, table_ref, wanted_ref, own_ref, other_ref, image_ref, blocks_ref,
    out_ref, tiles_ref, held, sems,
):
    me, live = table_ref[ME], table_ref[LIVE]
    chunks = start_blocks(live, blocks_ref, held, sems)
    inverse = inverse_factor(whole_sum(me % 2, own_ref, other_ref, 0) / total_rows)
    for j in range(tiles_ref.shape[0]):
        tiles_ref[j] = jnp.dot(
            inverse, image_ref[j], precision=HIGHEST, preferred_element_type=jnp.float32
        ).astype(tiles_ref.dtype)
    multiply_mirrors(me, table_ref, live, chunks, tiles_ref, blocks_ref, held, sems, out_ref)
    place_tiles(0, me, wanted_ref, tiles_ref, out_ref)


def last_kernel(total_rows, table_ref, own_ref, other_ref, image_ref, result_ref, projected_ref):
    core = table_ref[ME] % 2
    inverse = inverse_factor(whole_sum(core, own_ref, other_ref, 0) / total_rows)
    size = image_ref.shape[2]
    for j in range(image_ref.shape[0]):
        result_ref[:, j * size : (j + 1) * size] = jnp.dot(
            inverse, image_ref[j], precision=HIGHEST, preferred_element_type=jnp.float32
        )
    projected_ref[...] = whole_sum(core, own_ref, other_ref, 1) / total_rows


def spread_kernel(own_ref, given_ref, out_ref):
    chip = own_ref[...] + given_ref[...]
    for i in range(out_ref.shape[0]):
        out_ref[i] = chip


def total_kernel(parts_ref, out_ref):
    terms = [parts_ref[i] for i in range(parts_ref.shape[0])]
    while len(terms) > 1:
        terms = [a + b for a, b in zip(terms[::2], terms[1::2])] + terms[len(terms) // 2 * 2 :]
    out_ref[...] = terms[0]


def sum_over_devices(mine, given):
    swap = [(0, 1), (1, 0)]
    chips = lax.axis_size("rows")
    spread = pl.pallas_call(
        spread_kernel,
        out_shape=jax.ShapeDtypeStruct((chips,) + mine.shape, mine.dtype),
        in_specs=[VMEM] * 2,
        out_specs=VMEM,
        name="spread",
    )(mine, lax.ppermute(given, "grp", swap))
    own = pl.pallas_call(
        total_kernel,
        out_shape=jax.ShapeDtypeStruct(mine.shape, mine.dtype),
        in_specs=[VMEM],
        out_specs=VMEM,
        name="total",
    )(lax.all_to_all(spread, "rows", 0, 0, tiled=True))
    return own, lax.ppermute(own, "grp", swap)


def exchange(outgoing):
    return lax.all_to_all(outgoing, AXES, split_axis=0, concat_axis=0, tiled=True)


def on_device(start_basis, kernel_blocks, block_row, block_col, block_count):
    devices = lax.axis_size(AXES)
    me = lax.axis_index(AXES)
    slots, size, _ = kernel_blocks.shape
    own_rows, columns = start_basis.shape
    row_blocks = own_rows // size
    total_rows = own_rows * devices

    asked = pl.pallas_call(
        functools.partial(ask_kernel, row_blocks),
        out_shape=jax.ShapeDtypeStruct((devices, 1, 128), jnp.int32),
        in_specs=[SMEM, VMEM],
        out_specs=VMEM,
        name="ask",
    )(block_count, block_col[None, :])
    asked = exchange(asked)
    table = jnp.concatenate([me.reshape(1).astype(jnp.int32), block_count, block_row, block_col])

    params = pltpu.CompilerParams(vmem_limit_bytes=48 * MIB)
    scratch = [
        pltpu.VMEM(kernel_blocks.shape, kernel_blocks.dtype),
        pltpu.SemaphoreType.DMA((slots // CHUNK,)),
    ]
    tiles_shape = jax.ShapeDtypeStruct((row_blocks, columns, size), jnp.bfloat16)
    image_shape = jax.ShapeDtypeStruct((row_blocks, columns, size), jnp.float32)
    out_shape = jax.ShapeDtypeStruct((devices, columns, size), jnp.bfloat16)

    def image_of(tiles, wanted, arrived, with_projection):
        parts = 2 if with_projection else 1
        half = jax.ShapeDtypeStruct((1, (parts * ROWS + 1) * LANES), jnp.float32)
        return pl.pallas_call(
            functools.partial(image_kernel, with_projection),
            out_shape=(image_shape, half, half),
            in_specs=[SMEM] * 2 + [VMEM] * 2 + [ANY],
            out_specs=(VMEM, VMEM, VMEM),
            scratch_shapes=scratch,
            compiler_params=params,
            name="image",
        )(table, wanted, tiles, arrived, kernel_blocks)

    outgoing, tiles = pl.pallas_call(
        first_kernel,
        out_shape=(out_shape, tiles_shape),
        in_specs=[SMEM] + [VMEM, ANY],
        out_specs=(VMEM, VMEM),
        scratch_shapes=scratch,
        compiler_params=params,
        name="first",
    )(table, start_basis.T, kernel_blocks)
    outgoing, wanted = pl.pallas_call(
        place_kernel,
        out_shape=(out_shape, jax.ShapeDtypeStruct((devices,), jnp.int32)),
        in_specs=[SMEM] * 2 + [VMEM, ANY],
        out_specs=(VMEM, SMEM),
        scratch_shapes=[pltpu.SemaphoreType.DMA((8,))],
        compiler_params=params,
        name="place",
    )(table, asked, tiles, outgoing)
    image, own, given = image_of(tiles, wanted, exchange(outgoing), False)
    own, other = sum_over_devices(own, given)
    outgoing, tiles = pl.pallas_call(
        functools.partial(normal_kernel, total_rows),
        out_shape=(out_shape, tiles_shape),
        in_specs=[SMEM] * 2 + [VMEM] * 3 + [ANY],
        out_specs=(VMEM, VMEM),
        scratch_shapes=scratch,
        compiler_params=params,
        name="normal",
    )(table, wanted, own, other, image, kernel_blocks)
    image, own, given = image_of(tiles, wanted, exchange(outgoing), True)
    own, other = sum_over_devices(own, given)
    result, projected = pl.pallas_call(
        functools.partial(last_kernel, total_rows),
        out_shape=(
            jax.ShapeDtypeStruct((columns, own_rows), jnp.float32),
            jax.ShapeDtypeStruct((columns, columns), jnp.float32),
        ),
        in_specs=[SMEM] + [VMEM] * 3,
        out_specs=(VMEM, VMEM),
        compiler_params=params,
        name="last",
    )(table, own, other, image)
    return result.T, projected


def solution(mesh):
    in_specs = (
        P(AXES, None),
        P(AXES, None, None),
        P(AXES),
        P(AXES),
        P(AXES),
    )
    out_specs = (P(AXES, None), P())
    return jax.shard_map(
        on_device, mesh=mesh, in_specs=in_specs, out_specs=out_specs, check_vma=False
    )
```

```python
import functools

import jax
import jax.numpy as jnp
from jax import lax
from jax.experimental import pallas as pl
from jax.experimental.pallas import tpu as pltpu
from jax.sharding import PartitionSpec as P

AXES = ("rows", "grp")
HIGHEST = lax.Precision.HIGHEST
CHUNK = 4
PANEL = 8
ROWS, LANES = 8, 128
ME, LIVE, FIRST = 0, 1, 2
NT = (((1,), (1,)), ((), ()))
VMEM = pl.BlockSpec(memory_space=pltpu.VMEM)
SMEM = pl.BlockSpec(memory_space=pltpu.SMEM)
ANY = pl.BlockSpec(memory_space=pl.ANY)
MIB = 1024 * 1024
SMALL = pltpu.CompilerParams(vmem_limit_bytes=8 * MIB)


def block_copy(blocks_ref, held, sems, i):
    at = pl.ds(i * CHUNK, CHUNK)
    return pltpu.make_async_copy(blocks_ref.at[at], held.at[at], sems.at[i])


def start_blocks(live, blocks_ref, held, sems):
    chunks = (live + CHUNK - 1) // CHUNK

    def start(i, carry):
        block_copy(blocks_ref, held, sems, i).start()
        return carry

    lax.fori_loop(0, chunks, start, 0)
    return chunks


def multiply_mirrors(me, table_ref, live, chunks, tiles_ref, blocks_ref, held, sems, out_ref):
    row_blocks = tiles_ref.shape[0]

    def visit(i, carry):
        block_copy(blocks_ref, held, sems, i).wait()
        for j in range(CHUNK):
            s = i * CHUNK + j
            local = table_ref[FIRST + s] - me * row_blocks
            place = jnp.where(s < live, table_ref[FIRST + held.shape[0] + s] // row_blocks, 0)
            product = jnp.dot(tiles_ref[local], held[s], preferred_element_type=jnp.float32)
            out_ref[place] = product.astype(out_ref.dtype)
        return carry

    lax.fori_loop(0, chunks, visit, 0)


def place_tiles(start, end, wanted_ref, tiles_ref, out_ref):
    def visit(i, carry):
        for j in range(CHUNK):
            d = jnp.minimum(start + i * CHUNK + j, end - 1)
            out_ref[d] = tiles_ref[jnp.maximum(wanted_ref[d], 0)]
        return carry

    lax.fori_loop(0, (end - start + CHUNK - 1) // CHUNK, visit, 0)


def ask_kernel(row_blocks, count_ref, col_ref, out_ref):
    devices, slots = out_ref.shape[0], col_ref.shape[1]
    column = jnp.broadcast_to(col_ref[...], (devices, slots))
    owner = column // row_blocks
    device = lax.broadcasted_iota(jnp.int32, (devices, slots), 0)
    alive = lax.broadcasted_iota(jnp.int32, (devices, slots), 1) < count_ref[0]
    block = jnp.where((owner == device) & alive, column - owner * row_blocks, -1)
    asked = jnp.max(block, axis=1, keepdims=True)
    out_ref[...] = jnp.broadcast_to(asked, (devices, out_ref.shape[2]))[:, None, :]


def first_kernel(table_ref, basis_ref, blocks_ref, out_ref, tiles_ref, held, sems):
    live = table_ref[LIVE]
    chunks = start_blocks(live, blocks_ref, held, sems)
    row_blocks, _, size = tiles_ref.shape
    for j in range(row_blocks):
        tiles_ref[j] = basis_ref[:, j * size : (j + 1) * size]
    multiply_mirrors(table_ref[ME], table_ref, live, chunks, tiles_ref, blocks_ref, held, sems, out_ref)


def place_kernel(table_ref, asked_ref, tiles_ref, given_ref, out_ref, wanted_ref, sems):
    me = table_ref[ME]
    groups = sems.shape[0]
    size = out_ref.shape[0] // groups
    first = me // size

    def copy_of(g):
        at = pl.ds(g * size, size)
        return pltpu.make_async_copy(given_ref.at[at], out_ref.at[at], sems.at[g])

    def start(g, carry):
        copy_of(g).start()
        return carry

    def wait(g, carry):
        copy_of(g).wait()
        return carry

    def compact(i, carry):
        for j in range(CHUNK):
            wanted_ref[i * CHUNK + j] = asked_ref[i * CHUNK + j, 0, 0]
        return carry

    lax.fori_loop(first, groups, start, 0)
    lax.fori_loop(0, wanted_ref.shape[0] // CHUNK, compact, 0)
    place_tiles(0, first * size, wanted_ref, tiles_ref, out_ref)
    lax.fori_loop(first, groups, wait, 0)
    place_tiles(first * size, me, wanted_ref, tiles_ref, out_ref)


def row_of(k):
    return slice(k * LANES, (k + 1) * LANES)


def fold(square):
    half = square.shape[0] // 2
    row_at = lax.broadcasted_iota(jnp.int32, (half, half), 0)
    col_at = lax.broadcasted_iota(jnp.int32, (half, half), 1)
    corner = square[half:, half:]
    mixed = jnp.where(row_at >= col_at, square[:half, :half], corner)
    sides = jnp.concatenate([mixed, square[half:, :half]], axis=1)
    folded = jnp.concatenate([sides[: half // 2], sides[half // 2 :]], axis=1)
    diagonal = jnp.sum(jnp.where(row_at == col_at, corner, 0.0), axis=0, keepdims=True)
    return folded, diagonal


def unfold(folded, diagonal):
    width = folded.shape[1] // 2
    half = width // 2
    row_at = lax.broadcasted_iota(jnp.int32, (half, half), 0)
    col_at = lax.broadcasted_iota(jnp.int32, (half, half), 1)
    sides = jnp.concatenate([folded[:, :width], folded[:, width:]], axis=0)
    mixed, side = sides[:, :half], sides[:, half:]
    turned = mixed.T
    upper = jnp.where(row_at >= col_at, mixed, turned)
    corner = jnp.where(row_at < col_at, mixed, turned)
    corner = jnp.where(row_at == col_at, jnp.broadcast_to(diagonal, (half, half)), corner)
    return jnp.concatenate(
        [jnp.concatenate([upper, side.T], axis=1), jnp.concatenate([side, corner], axis=1)], axis=0
    )


def image_kernel(
    with_projection, table_ref, wanted_ref, tiles_ref, arrived_ref, blocks_ref,
    image_ref, own_ref, given_ref, held, sems,
):
    me, live = table_ref[ME], table_ref[LIVE]
    chunks = start_blocks(live, blocks_ref, held, sems)
    row_blocks = tiles_ref.shape[0]
    image_ref[...] = jnp.zeros_like(image_ref)

    def add_mirror(d, carry):
        @pl.when(wanted_ref[d] >= 0)
        def _():
            image_ref[wanted_ref[d]] += arrived_ref[d].astype(jnp.float32)

        return carry

    lax.fori_loop(0, me + 1, add_mirror, 0)

    def visit(i, carry):
        block_copy(blocks_ref, held, sems, i).wait()
        for j in range(CHUNK):
            s = i * CHUNK + j
            local = table_ref[FIRST + s] - me * row_blocks
            column = table_ref[FIRST + held.shape[0] + s]
            owner = column // row_blocks
            tile = jnp.where(owner == me, tiles_ref[column - owner * row_blocks], arrived_ref[owner])
            tile = jnp.where(s < live, tile, jnp.zeros_like(tile))
            image_ref[local] += lax.dot_general(tile, held[s], NT, preferred_element_type=jnp.float32)
        return carry

    lax.fori_loop(0, chunks, visit, 0)

    def summed(left_ref):
        total = None
        for j in range(image_ref.shape[0]):
            term = lax.dot_general(
                left_ref[j].astype(jnp.float32), image_ref[j], NT, precision=HIGHEST,
                preferred_element_type=jnp.float32,
            )
            total = term if total is None else total + term
        return total

    squares = [summed(image_ref)]
    if with_projection:
        product = summed(tiles_ref)
        squares.append((product + product.T) * 0.5)
    diagonals = []
    for k, square in enumerate(squares):
        folded, diagonal = fold(square)
        diagonals.append(diagonal)
        low, high = folded[:ROWS], folded[ROWS:]
        own, given = jnp.where(me % 2 == 0, low, high), jnp.where(me % 2 == 0, high, low)
        for r in range(ROWS):
            at = row_of(k * ROWS + r)
            own_ref[:, at] = own[r : r + 1]
            given_ref[:, at] = given[r : r + 1]
    rest = own_ref.shape[1] // LANES - 1
    missing = LANES - len(diagonals) * diagonals[0].shape[1]
    last = jnp.concatenate(diagonals + [jnp.zeros((1, missing), jnp.float32)], axis=1)
    own_ref[:, row_of(rest)] = last
    given_ref[:, row_of(rest)] = last


def inverse_factor(gram):
    n = gram.shape[0]
    row_at = lax.broadcasted_iota(jnp.int32, (n, n), 0)
    col_at = lax.broadcasted_iota(jnp.int32, (n, n), 1)
    work = jnp.concatenate([gram, (row_at == col_at).astype(jnp.float32)], axis=1)
    at = lax.broadcasted_iota(jnp.int32, work.shape, 0)
    pivots = jnp.zeros(work.shape, jnp.float32)
    for k in range(0, n, PANEL):
        spread = [jnp.broadcast_to(work[:, k + j : k + j + 1], work.shape) for j in range(PANEL)]
        rows = [work[k + j : k + j + 1, :] for j in range(PANEL)]
        for j in range(PANEL):
            pivot = spread[j][k + j : k + j + 1, :]
            pivots = jnp.where(at == k + j, pivot, pivots)
            share = 1.0 / pivot
            scaled = rows[j] * share
            for m in range(j + 1, PANEL):
                spread[m] = spread[m] - spread[j] * (spread[m][k + j : k + j + 1, :] * share)
                rows[m] = rows[m] - spread[j][k + m : k + m + 1, :] * scaled
            rows[j] = scaled
        for j in range(PANEL):
            work = work - jnp.where(at > k + j, spread[j], 0.0) * rows[j]
    return work[:, n:] * (1.0 / jnp.sqrt(pivots[:, n:]))


def whole_sum(core, own_ref, other_ref, k):
    at = [row_of(k * ROWS + r) for r in range(ROWS)]
    own = jnp.concatenate([own_ref[:, a] for a in at], axis=0)
    other = jnp.concatenate([other_ref[:, a] for a in at], axis=0)
    rest = row_of(own_ref.shape[1] // LANES - 1)
    diagonals = jnp.where(core == 0, own_ref[:, rest], other_ref[:, rest])
    first = jnp.where(core == 0, own, other)
    second = jnp.where(core == 0, other, own)
    width = LANES // 4
    return unfold(jnp.concatenate([first, second], axis=0), diagonals[:, k * width : (k + 1) * width])


def normal_kernel(
    total_rows, table_ref, wanted_ref, own_ref, other_ref, image_ref, blocks_ref,
    out_ref, tiles_ref, held, sems,
):
    me, live = table_ref[ME], table_ref[LIVE]
    chunks = start_blocks(live, blocks_ref, held, sems)
    inverse = inverse_factor(whole_sum(me % 2, own_ref, other_ref, 0) / total_rows)
    for j in range(tiles_ref.shape[0]):
        tiles_ref[j] = jnp.dot(
            inverse, image_ref[j], precision=HIGHEST, preferred_element_type=jnp.float32
        ).astype(tiles_ref.dtype)
    multiply_mirrors(me, table_ref, live, chunks, tiles_ref, blocks_ref, held, sems, out_ref)
    place_tiles(0, me, wanted_ref, tiles_ref, out_ref)


def last_kernel(total_rows, table_ref, own_ref, other_ref, image_ref, result_ref, projected_ref):
    core = table_ref[ME] % 2
    inverse = inverse_factor(whole_sum(core, own_ref, other_ref, 0) / total_rows)
    size = image_ref.shape[2]
    for j in range(image_ref.shape[0]):
        result_ref[:, j * size : (j + 1) * size] = jnp.dot(
            inverse, image_ref[j], precision=HIGHEST, preferred_element_type=jnp.float32
        )
    projected_ref[...] = whole_sum(core, own_ref, other_ref, 1) / total_rows


def spread_kernel(own_ref, given_ref, out_ref):
    chip = own_ref[...] + given_ref[...]
    for i in range(out_ref.shape[0]):
        out_ref[i] = chip


def total_kernel(parts_ref, out_ref):
    terms = [parts_ref[i] for i in range(parts_ref.shape[0])]
    while len(terms) > 1:
        terms = [a + b for a, b in zip(terms[::2], terms[1::2])] + terms[len(terms) // 2 * 2 :]
    out_ref[...] = terms[0]


def sum_over_devices(mine, given):
    swap = [(0, 1), (1, 0)]
    chips = lax.axis_size("rows")
    spread = pl.pallas_call(
        spread_kernel,
        out_shape=jax.ShapeDtypeStruct((chips,) + mine.shape, mine.dtype),
        in_specs=[VMEM] * 2,
        out_specs=VMEM,
        compiler_params=SMALL,
        name="spread",
    )(mine, lax.ppermute(given, "grp", swap))
    own = pl.pallas_call(
        total_kernel,
        out_shape=jax.ShapeDtypeStruct(mine.shape, mine.dtype),
        in_specs=[VMEM],
        out_specs=VMEM,
        compiler_params=SMALL,
        name="total",
    )(lax.all_to_all(spread, "rows", 0, 0, tiled=True))
    return own, lax.ppermute(own, "grp", swap)


def exchange(outgoing):
    return lax.all_to_all(outgoing, AXES, split_axis=0, concat_axis=0, tiled=True)


def on_device(start_basis, kernel_blocks, block_row, block_col, block_count):
    devices = lax.axis_size(AXES)
    me = lax.axis_index(AXES)
    slots, size, _ = kernel_blocks.shape
    own_rows, columns = start_basis.shape
    row_blocks = own_rows // size
    total_rows = own_rows * devices

    asked = pl.pallas_call(
        functools.partial(ask_kernel, row_blocks),
        out_shape=jax.ShapeDtypeStruct((devices, 1, 128), jnp.int32),
        in_specs=[SMEM, VMEM],
        out_specs=VMEM,
        compiler_params=SMALL,
        name="ask",
    )(block_count, block_col[None, :])
    asked = exchange(asked)
    table = jnp.concatenate([me.reshape(1).astype(jnp.int32), block_count, block_row, block_col])

    params = pltpu.CompilerParams(vmem_limit_bytes=48 * MIB)
    scratch = [
        pltpu.VMEM(kernel_blocks.shape, kernel_blocks.dtype),
        pltpu.SemaphoreType.DMA((slots // CHUNK,)),
    ]
    tiles_shape = jax.ShapeDtypeStruct((row_blocks, columns, size), jnp.bfloat16)
    image_shape = jax.ShapeDtypeStruct((row_blocks, columns, size), jnp.float32)
    out_shape = jax.ShapeDtypeStruct((devices, columns, size), jnp.bfloat16)

    def image_of(tiles, wanted, arrived, with_projection):
        parts = 2 if with_projection else 1
        half = jax.ShapeDtypeStruct((1, (parts * ROWS + 1) * LANES), jnp.float32)
        return pl.pallas_call(
            functools.partial(image_kernel, with_projection),
            out_shape=(image_shape, half, half),
            in_specs=[SMEM] * 2 + [VMEM] * 2 + [ANY],
            out_specs=(VMEM, VMEM, VMEM),
            scratch_shapes=scratch,
            compiler_params=params,
            name="image",
        )(table, wanted, tiles, arrived, kernel_blocks)

    outgoing, tiles = pl.pallas_call(
        first_kernel,
        out_shape=(out_shape, tiles_shape),
        in_specs=[SMEM] + [VMEM, ANY],
        out_specs=(VMEM, VMEM),
        scratch_shapes=scratch,
        compiler_params=params,
        name="first",
    )(table, start_basis.T, kernel_blocks)
    outgoing, wanted = pl.pallas_call(
        place_kernel,
        out_shape=(out_shape, jax.ShapeDtypeStruct((devices,), jnp.int32)),
        in_specs=[SMEM] * 2 + [VMEM, ANY],
        out_specs=(VMEM, SMEM),
        scratch_shapes=[pltpu.SemaphoreType.DMA((8,))],
        compiler_params=params,
        name="place",
    )(table, asked, tiles, outgoing)
    image, own, given = image_of(tiles, wanted, exchange(outgoing), False)
    own, other = sum_over_devices(own, given)
    outgoing, tiles = pl.pallas_call(
        functools.partial(normal_kernel, total_rows),
        out_shape=(out_shape, tiles_shape),
        in_specs=[SMEM] * 2 + [VMEM] * 3 + [ANY],
        out_specs=(VMEM, VMEM),
        scratch_shapes=scratch,
        compiler_params=params,
        name="normal",
    )(table, wanted, own, other, image, kernel_blocks)
    image, own, given = image_of(tiles, wanted, exchange(outgoing), True)
    own, other = sum_over_devices(own, given)
    result, projected = pl.pallas_call(
        functools.partial(last_kernel, total_rows),
        out_shape=(
            jax.ShapeDtypeStruct((columns, own_rows), jnp.float32),
            jax.ShapeDtypeStruct((columns, columns), jnp.float32),
        ),
        in_specs=[SMEM] + [VMEM] * 3,
        out_specs=(VMEM, VMEM),
        compiler_params=params,
        name="last",
    )(table, own, other, image)
    return result.T, projected


def solution(mesh):
    in_specs = (
        P(AXES, None),
        P(AXES, None, None),
        P(AXES),
        P(AXES),
        P(AXES),
    )
    out_specs = (P(AXES, None), P())
    return jax.shard_map(
        on_device, mesh=mesh, in_specs=in_specs, out_specs=out_specs, check_vma=False
    )
```

```python
import functools

import jax
import jax.numpy as jnp
from jax import lax
from jax.experimental import pallas as pl
from jax.experimental.pallas import tpu as pltpu
from jax.sharding import PartitionSpec as P

AXES = ("rows", "grp")
HIGHEST = lax.Precision.HIGHEST
CHUNK = 23
PANEL = 8
ROWS, LANES = 8, 128
ME, LIVE, FIRST = 0, 1, 2
NT = (((1,), (1,)), ((), ()))
VMEM = pl.BlockSpec(memory_space=pltpu.VMEM)
SMEM = pl.BlockSpec(memory_space=pltpu.SMEM)
ANY = pl.BlockSpec(memory_space=pl.ANY)
MIB = 1024 * 1024
SMALL = pltpu.CompilerParams(vmem_limit_bytes=8 * MIB)


def block_copy(blocks_ref, held, sems, i):
    at = pl.ds(i * CHUNK, CHUNK)
    return pltpu.make_async_copy(blocks_ref.at[at], held.at[at], sems.at[i])


def start_blocks(live, blocks_ref, held, sems):
    chunks = (live + CHUNK - 1) // CHUNK

    def start(i, carry):
        block_copy(blocks_ref, held, sems, i).start()
        return carry

    lax.fori_loop(0, chunks, start, 0)
    return chunks


def multiply_mirrors(me, table_ref, live, chunks, tiles_ref, blocks_ref, held, sems, out_ref):
    row_blocks = tiles_ref.shape[0]

    def visit(i, carry):
        block_copy(blocks_ref, held, sems, i).wait()
        for j in range(CHUNK):
            s = i * CHUNK + j
            local = table_ref[FIRST + s] - me * row_blocks
            place = jnp.where(s < live, table_ref[FIRST + held.shape[0] + s] // row_blocks, 0)
            product = jnp.dot(tiles_ref[local], held[s], preferred_element_type=jnp.float32)
            out_ref[place] = product.astype(out_ref.dtype)
        return carry

    lax.fori_loop(0, chunks, visit, 0)


def place_tiles(start, end, wanted_ref, tiles_ref, out_ref):
    tiles = [tiles_ref[j].astype(jnp.float32) for j in range(tiles_ref.shape[0])]
    group = 4

    def visit(i, carry):
        for j in range(group):
            d = jnp.minimum(start + i * group + j, end - 1)
            wanted = spread_lanes(wanted_ref[d], tiles[0].shape[1])
            tile = tiles[0]
            for k in range(1, len(tiles)):
                tile = jnp.where(wanted == k, tiles[k], tile)
            out_ref[d] = tile.astype(out_ref.dtype)
        return carry

    lax.fori_loop(0, (end - start + group - 1) // group, visit, 0)


def spread_lanes(row, width):
    return jnp.concatenate([row] * (width // row.shape[1]), axis=1)


def ask_kernel(row_blocks, count_ref, col_ref, out_ref):
    devices, slots = out_ref.shape[0], col_ref.shape[1]
    column = jnp.broadcast_to(col_ref[...], (devices, slots))
    owner = column // row_blocks
    device = lax.broadcasted_iota(jnp.int32, (devices, slots), 0)
    alive = lax.broadcasted_iota(jnp.int32, (devices, slots), 1) < count_ref[0]
    block = jnp.where((owner == device) & alive, column - owner * row_blocks, -1)
    asked = jnp.max(block, axis=1, keepdims=True)
    out_ref[...] = jnp.broadcast_to(asked, (devices, out_ref.shape[2]))[:, None, :]


def first_kernel(table_ref, basis_ref, blocks_ref, out_ref, tiles_ref, held, sems):
    live = table_ref[LIVE]
    chunks = start_blocks(live, blocks_ref, held, sems)
    row_blocks, _, size = tiles_ref.shape
    for j in range(row_blocks):
        tiles_ref[j] = basis_ref[:, j * size : (j + 1) * size]
    multiply_mirrors(table_ref[ME], table_ref, live, chunks, tiles_ref, blocks_ref, held, sems, out_ref)


def place_kernel(table_ref, wanted_ref, tiles_ref, given_ref, out_ref, sems):
    me = table_ref[ME]
    groups = sems.shape[0]
    size = out_ref.shape[0] // groups
    first = me // size

    def copy_of(g):
        at = pl.ds(g * size, size)
        return pltpu.make_async_copy(given_ref.at[at], out_ref.at[at], sems.at[g])

    def start(g, carry):
        copy_of(g).start()
        return carry

    def wait(g, carry):
        copy_of(g).wait()
        return carry

    lax.fori_loop(first, groups, start, 0)
    place_tiles(0, first * size, wanted_ref, tiles_ref, out_ref)
    lax.fori_loop(first, groups, wait, 0)
    place_tiles(first * size, me, wanted_ref, tiles_ref, out_ref)


def row_of(k):
    return slice(k * LANES, (k + 1) * LANES)


def fold(square):
    half = square.shape[0] // 2
    row_at = lax.broadcasted_iota(jnp.int32, (half, half), 0)
    col_at = lax.broadcasted_iota(jnp.int32, (half, half), 1)
    corner = square[half:, half:]
    mixed = jnp.where(row_at >= col_at, square[:half, :half], corner)
    sides = jnp.concatenate([mixed, square[half:, :half]], axis=1)
    folded = jnp.concatenate([sides[: half // 2], sides[half // 2 :]], axis=1)
    diagonal = jnp.sum(jnp.where(row_at == col_at, corner, 0.0), axis=0, keepdims=True)
    return folded, diagonal


def unfold(folded, diagonal):
    width = folded.shape[1] // 2
    half = width // 2
    row_at = lax.broadcasted_iota(jnp.int32, (half, half), 0)
    col_at = lax.broadcasted_iota(jnp.int32, (half, half), 1)
    sides = jnp.concatenate([folded[:, :width], folded[:, width:]], axis=0)
    mixed, side = sides[:, :half], sides[:, half:]
    turned = mixed.T
    upper = jnp.where(row_at >= col_at, mixed, turned)
    corner = jnp.where(row_at < col_at, mixed, turned)
    corner = jnp.where(row_at == col_at, jnp.broadcast_to(diagonal, (half, half)), corner)
    return jnp.concatenate(
        [jnp.concatenate([upper, side.T], axis=1), jnp.concatenate([side, corner], axis=1)], axis=0
    )


def image_kernel(
    with_projection, table_ref, wanted_ref, tiles_ref, arrived_ref, blocks_ref,
    image_ref, own_ref, given_ref, held, sems,
):
    me, live = table_ref[ME], table_ref[LIVE]
    chunks = start_blocks(live, blocks_ref, held, sems)
    row_blocks = tiles_ref.shape[0]

    def add_mirror(d, sums):
        wanted = spread_lanes(wanted_ref[d], image_ref.shape[2])
        mirror = arrived_ref[d].astype(jnp.float32)
        return tuple(total + jnp.where(wanted == k, mirror, 0.0) for k, total in enumerate(sums))

    zero = jnp.zeros(image_ref.shape[1:], image_ref.dtype)
    sums = lax.fori_loop(0, me + 1, add_mirror, (zero,) * row_blocks)
    for k, total in enumerate(sums):
        image_ref[k] = total

    def visit(i, carry):
        block_copy(blocks_ref, held, sems, i).wait()
        for j in range(CHUNK):
            s = i * CHUNK + j
            local = table_ref[FIRST + s] - me * row_blocks
            column = table_ref[FIRST + held.shape[0] + s]
            owner = column // row_blocks
            tile = jnp.where(owner == me, tiles_ref[column - owner * row_blocks], arrived_ref[owner])
            tile = jnp.where(s < live, tile, jnp.zeros_like(tile))
            image_ref[local] += lax.dot_general(tile, held[s], NT, preferred_element_type=jnp.float32)
        return carry

    lax.fori_loop(0, chunks, visit, 0)

    def summed(left_ref):
        total = None
        for j in range(image_ref.shape[0]):
            term = lax.dot_general(
                left_ref[j].astype(jnp.float32), image_ref[j], NT, precision=HIGHEST,
                preferred_element_type=jnp.float32,
            )
            total = term if total is None else total + term
        return total

    squares = [summed(image_ref)]
    if with_projection:
        product = summed(tiles_ref)
        squares.append((product + product.T) * 0.5)
    diagonals = []
    for k, square in enumerate(squares):
        folded, diagonal = fold(square)
        diagonals.append(diagonal)
        low, high = folded[:ROWS], folded[ROWS:]
        own, given = jnp.where(me % 2 == 0, low, high), jnp.where(me % 2 == 0, high, low)
        for r in range(ROWS):
            at = row_of(k * ROWS + r)
            own_ref[:, at] = own[r : r + 1]
            given_ref[:, at] = given[r : r + 1]
    rest = own_ref.shape[1] // LANES - 1
    missing = LANES - len(diagonals) * diagonals[0].shape[1]
    last = jnp.concatenate(diagonals + [jnp.zeros((1, missing), jnp.float32)], axis=1)
    own_ref[:, row_of(rest)] = last
    given_ref[:, row_of(rest)] = last


def inverse_factor(gram):
    n = gram.shape[0]
    row_at = lax.broadcasted_iota(jnp.int32, (n, n), 0)
    col_at = lax.broadcasted_iota(jnp.int32, (n, n), 1)
    work = jnp.concatenate([gram, (row_at == col_at).astype(jnp.float32)], axis=1)
    at = lax.broadcasted_iota(jnp.int32, work.shape, 0)
    pivots = jnp.zeros(work.shape, jnp.float32)
    for k in range(0, n, PANEL):
        spread = [jnp.broadcast_to(work[:, k + j : k + j + 1], work.shape) for j in range(PANEL)]
        rows = [work[k + j : k + j + 1, :] for j in range(PANEL)]
        for j in range(PANEL):
            pivot = spread[j][k + j : k + j + 1, :]
            pivots = jnp.where(at == k + j, pivot, pivots)
            share = 1.0 / pivot
            scaled = rows[j] * share
            for m in range(j + 1, PANEL):
                spread[m] = spread[m] - spread[j] * (spread[m][k + j : k + j + 1, :] * share)
                rows[m] = rows[m] - spread[j][k + m : k + m + 1, :] * scaled
            rows[j] = scaled
        for j in range(PANEL):
            work = work - jnp.where(at > k + j, spread[j], 0.0) * rows[j]
    return work[:, n:] * (1.0 / jnp.sqrt(pivots[:, n:]))


def whole_sum(core, own_ref, other_ref, k):
    at = [row_of(k * ROWS + r) for r in range(ROWS)]
    own = jnp.concatenate([own_ref[:, a] for a in at], axis=0)
    other = jnp.concatenate([other_ref[:, a] for a in at], axis=0)
    rest = row_of(own_ref.shape[1] // LANES - 1)
    diagonals = jnp.where(core == 0, own_ref[:, rest], other_ref[:, rest])
    first = jnp.where(core == 0, own, other)
    second = jnp.where(core == 0, other, own)
    width = LANES // 4
    return unfold(jnp.concatenate([first, second], axis=0), diagonals[:, k * width : (k + 1) * width])


def normal_kernel(
    total_rows, table_ref, wanted_ref, own_ref, other_ref, image_ref, blocks_ref,
    out_ref, tiles_ref, held, sems,
):
    me, live = table_ref[ME], table_ref[LIVE]
    chunks = start_blocks(live, blocks_ref, held, sems)
    inverse = inverse_factor(whole_sum(me % 2, own_ref, other_ref, 0) / total_rows)
    for j in range(tiles_ref.shape[0]):
        tiles_ref[j] = jnp.dot(
            inverse, image_ref[j], precision=HIGHEST, preferred_element_type=jnp.float32
        ).astype(tiles_ref.dtype)
    multiply_mirrors(me, table_ref, live, chunks, tiles_ref, blocks_ref, held, sems, out_ref)
    place_tiles(0, me, wanted_ref, tiles_ref, out_ref)


def last_kernel(total_rows, table_ref, own_ref, other_ref, image_ref, result_ref, projected_ref):
    core = table_ref[ME] % 2
    inverse = inverse_factor(whole_sum(core, own_ref, other_ref, 0) / total_rows)
    size = image_ref.shape[2]
    for j in range(image_ref.shape[0]):
        result_ref[:, j * size : (j + 1) * size] = jnp.dot(
            inverse, image_ref[j], precision=HIGHEST, preferred_element_type=jnp.float32
        )
    projected_ref[...] = whole_sum(core, own_ref, other_ref, 1) / total_rows


def spread_kernel(own_ref, given_ref, out_ref):
    chip = own_ref[...] + given_ref[...]
    for i in range(out_ref.shape[0]):
        out_ref[i] = chip


def total_kernel(parts_ref, out_ref):
    terms = [parts_ref[i] for i in range(parts_ref.shape[0])]
    while len(terms) > 1:
        terms = [a + b for a, b in zip(terms[::2], terms[1::2])] + terms[len(terms) // 2 * 2 :]
    out_ref[...] = terms[0]


def sum_over_devices(mine, given):
    swap = [(0, 1), (1, 0)]
    chips = lax.axis_size("rows")
    spread = pl.pallas_call(
        spread_kernel,
        out_shape=jax.ShapeDtypeStruct((chips,) + mine.shape, mine.dtype),
        in_specs=[VMEM] * 2,
        out_specs=VMEM,
        compiler_params=SMALL,
        name="spread",
    )(mine, lax.ppermute(given, "grp", swap))
    own = pl.pallas_call(
        total_kernel,
        out_shape=jax.ShapeDtypeStruct(mine.shape, mine.dtype),
        in_specs=[VMEM],
        out_specs=VMEM,
        compiler_params=SMALL,
        name="total",
    )(lax.all_to_all(spread, "rows", 0, 0, tiled=True))
    return own, lax.ppermute(own, "grp", swap)


def exchange(outgoing):
    return lax.all_to_all(outgoing, AXES, split_axis=0, concat_axis=0, tiled=True)


def on_device(start_basis, kernel_blocks, block_row, block_col, block_count):
    devices = lax.axis_size(AXES)
    me = lax.axis_index(AXES)
    slots, size, _ = kernel_blocks.shape
    own_rows, columns = start_basis.shape
    row_blocks = own_rows // size
    total_rows = own_rows * devices

    asked = pl.pallas_call(
        functools.partial(ask_kernel, row_blocks),
        out_shape=jax.ShapeDtypeStruct((devices, 1, 128), jnp.int32),
        in_specs=[SMEM, VMEM],
        out_specs=VMEM,
        compiler_params=SMALL,
        name="ask",
    )(block_count, block_col[None, :])
    wanted = exchange(asked)
    table = jnp.concatenate([me.reshape(1).astype(jnp.int32), block_count, block_row, block_col])

    params = pltpu.CompilerParams(vmem_limit_bytes=48 * MIB)
    scratch = [
        pltpu.VMEM(kernel_blocks.shape, kernel_blocks.dtype),
        pltpu.SemaphoreType.DMA((slots // CHUNK,)),
    ]
    tiles_shape = jax.ShapeDtypeStruct((row_blocks, columns, size), jnp.bfloat16)
    image_shape = jax.ShapeDtypeStruct((row_blocks, columns, size), jnp.float32)
    out_shape = jax.ShapeDtypeStruct((devices, columns, size), jnp.bfloat16)

    def image_of(tiles, arrived, with_projection):
        parts = 2 if with_projection else 1
        half = jax.ShapeDtypeStruct((1, (parts * ROWS + 1) * LANES), jnp.float32)
        return pl.pallas_call(
            functools.partial(image_kernel, with_projection),
            out_shape=(image_shape, half, half),
            in_specs=[SMEM] + [VMEM] * 3 + [ANY],
            out_specs=(VMEM, VMEM, VMEM),
            scratch_shapes=scratch,
            compiler_params=params,
            name="image",
        )(table, wanted, tiles, arrived, kernel_blocks)

    outgoing, tiles = pl.pallas_call(
        first_kernel,
        out_shape=(out_shape, tiles_shape),
        in_specs=[SMEM] + [VMEM, ANY],
        out_specs=(VMEM, VMEM),
        scratch_shapes=scratch,
        compiler_params=params,
        name="first",
    )(table, start_basis.T, kernel_blocks)
    outgoing = pl.pallas_call(
        place_kernel,
        out_shape=out_shape,
        in_specs=[SMEM] + [VMEM] * 2 + [ANY],
        out_specs=VMEM,
        scratch_shapes=[pltpu.SemaphoreType.DMA((8,))],
        compiler_params=params,
        name="place",
    )(table, wanted, tiles, outgoing)
    image, own, given = image_of(tiles, exchange(outgoing), False)
    own, other = sum_over_devices(own, given)
    outgoing, tiles = pl.pallas_call(
        functools.partial(normal_kernel, total_rows),
        out_shape=(out_shape, tiles_shape),
        in_specs=[SMEM] + [VMEM] * 4 + [ANY],
        out_specs=(VMEM, VMEM),
        scratch_shapes=scratch,
        compiler_params=params,
        name="normal",
    )(table, wanted, own, other, image, kernel_blocks)
    image, own, given = image_of(tiles, exchange(outgoing), True)
    own, other = sum_over_devices(own, given)
    result, projected = pl.pallas_call(
        functools.partial(last_kernel, total_rows),
        out_shape=(
            jax.ShapeDtypeStruct((columns, own_rows), jnp.float32),
            jax.ShapeDtypeStruct((columns, columns), jnp.float32),
        ),
        in_specs=[SMEM] + [VMEM] * 3,
        out_specs=(VMEM, VMEM),
        compiler_params=params,
        name="last",
    )(table, own, other, image)
    return result.T, projected


def solution(mesh):
    in_specs = (
        P(AXES, None),
        P(AXES, None, None),
        P(AXES),
        P(AXES),
        P(AXES),
    )
    out_specs = (P(AXES, None), P())
    return jax.shard_map(
        on_device, mesh=mesh, in_specs=in_specs, out_specs=out_specs, check_vma=False
    )
```

```python
import functools

import jax
import jax.numpy as jnp
from jax import lax
from jax.experimental import pallas as pl
from jax.experimental.pallas import tpu as pltpu
from jax.sharding import PartitionSpec as P

AXES = ("rows", "grp")
HIGHEST = lax.Precision.HIGHEST
CHUNK = 23
PANEL = 8
ROWS, LANES = 8, 128
ME, LIVE, FIRST = 0, 1, 2
NT = (((1,), (1,)), ((), ()))
VMEM = pl.BlockSpec(memory_space=pltpu.VMEM)
SMEM = pl.BlockSpec(memory_space=pltpu.SMEM)
ANY = pl.BlockSpec(memory_space=pl.ANY)
MIB = 1024 * 1024
SMALL = pltpu.CompilerParams(vmem_limit_bytes=8 * MIB)
LARGE = pltpu.CompilerParams(vmem_limit_bytes=48 * MIB)


def block_copy(blocks_ref, held, sems, i):
    at = pl.ds(i * CHUNK, CHUNK)
    return pltpu.make_async_copy(blocks_ref.at[at], held.at[at], sems.at[i])


def start_blocks(live, blocks_ref, held, sems):
    def start(i, carry):
        block_copy(blocks_ref, held, sems, i).start()
        return carry

    lax.fori_loop(0, (live + CHUNK - 1) // CHUNK, start, 0)


def multiply_mirrors(me, table_ref, live, tiles_ref, held, out_ref, wait):
    row_blocks = tiles_ref.shape[0]

    def visit(i, carry):
        wait(i)
        for j in range(CHUNK):
            s = i * CHUNK + j
            local = table_ref[FIRST + s] - me * row_blocks
            place = jnp.where(s < live, table_ref[FIRST + held.shape[0] + s] // row_blocks, 0)
            product = jnp.dot(tiles_ref[local], held[s], preferred_element_type=jnp.float32)
            out_ref[place] = product.astype(out_ref.dtype)
        return carry

    lax.fori_loop(0, (live + CHUNK - 1) // CHUNK, visit, 0)


def place_tiles(start, end, wanted_ref, tiles_ref, out_ref):
    tiles = [tiles_ref[j].astype(jnp.float32) for j in range(tiles_ref.shape[0])]
    group = 4

    def visit(i, carry):
        for j in range(group):
            d = jnp.minimum(start + i * group + j, end - 1)
            wanted = spread_lanes(wanted_ref[d], tiles[0].shape[1])
            tile = tiles[0]
            for k in range(1, len(tiles)):
                tile = jnp.where(wanted == k, tiles[k], tile)
            out_ref[d] = tile.astype(out_ref.dtype)
        return carry

    lax.fori_loop(0, (end - start + group - 1) // group, visit, 0)


def spread_lanes(row, width):
    return jnp.concatenate([row] * (width // row.shape[1]), axis=1)


def ask_kernel(row_blocks, count_ref, col_ref, out_ref):
    devices, slots = out_ref.shape[0], col_ref.shape[1]
    column = jnp.broadcast_to(col_ref[...], (devices, slots))
    owner = column // row_blocks
    device = lax.broadcasted_iota(jnp.int32, (devices, slots), 0)
    alive = lax.broadcasted_iota(jnp.int32, (devices, slots), 1) < count_ref[0]
    block = jnp.where((owner == device) & alive, column - owner * row_blocks, -1)
    asked = jnp.max(block, axis=1, keepdims=True)
    out_ref[...] = jnp.broadcast_to(asked, (devices, out_ref.shape[2]))[:, None, :]


def first_kernel(table_ref, basis_ref, blocks_ref, out_ref, tiles_ref, held, sems):
    live = table_ref[LIVE]
    start_blocks(live, blocks_ref, held, sems)
    row_blocks, _, size = tiles_ref.shape
    for j in range(row_blocks):
        tiles_ref[j] = basis_ref[:, j * size : (j + 1) * size]
    multiply_mirrors(
        table_ref[ME], table_ref, live, tiles_ref, held, out_ref,
        lambda i: block_copy(blocks_ref, held, sems, i).wait(),
    )


def place_kernel(table_ref, wanted_ref, tiles_ref, given_ref, out_ref, sems):
    me = table_ref[ME]
    groups = sems.shape[0]
    size = out_ref.shape[0] // groups
    first = me // size

    def copy_of(g):
        at = pl.ds(g * size, size)
        return pltpu.make_async_copy(given_ref.at[at], out_ref.at[at], sems.at[g])

    def start(g, carry):
        copy_of(g).start()
        return carry

    def wait(g, carry):
        copy_of(g).wait()
        return carry

    lax.fori_loop(first, groups, start, 0)
    place_tiles(0, first * size, wanted_ref, tiles_ref, out_ref)
    lax.fori_loop(first, groups, wait, 0)
    place_tiles(first * size, me, wanted_ref, tiles_ref, out_ref)


def row_of(k):
    return slice(k * LANES, (k + 1) * LANES)


def fold(square):
    half = square.shape[0] // 2
    row_at = lax.broadcasted_iota(jnp.int32, (half, half), 0)
    col_at = lax.broadcasted_iota(jnp.int32, (half, half), 1)
    corner = square[half:, half:]
    mixed = jnp.where(row_at >= col_at, square[:half, :half], corner)
    sides = jnp.concatenate([mixed, square[half:, :half]], axis=1)
    folded = jnp.concatenate([sides[: half // 2], sides[half // 2 :]], axis=1)
    diagonal = jnp.sum(jnp.where(row_at == col_at, corner, 0.0), axis=0, keepdims=True)
    return folded, diagonal


def unfold(folded, diagonal):
    width = folded.shape[1] // 2
    half = width // 2
    row_at = lax.broadcasted_iota(jnp.int32, (half, half), 0)
    col_at = lax.broadcasted_iota(jnp.int32, (half, half), 1)
    sides = jnp.concatenate([folded[:, :width], folded[:, width:]], axis=0)
    mixed, side = sides[:, :half], sides[:, half:]
    turned = mixed.T
    upper = jnp.where(row_at >= col_at, mixed, turned)
    corner = jnp.where(row_at < col_at, mixed, turned)
    corner = jnp.where(row_at == col_at, jnp.broadcast_to(diagonal, (half, half)), corner)
    return jnp.concatenate(
        [jnp.concatenate([upper, side.T], axis=1), jnp.concatenate([side, corner], axis=1)], axis=0
    )


def image_kernel(
    with_projection, table_ref, wanted_ref, tiles_ref, arrived_ref, held,
    image_ref, own_ref, given_ref,
):
    me, live = table_ref[ME], table_ref[LIVE]
    row_blocks = tiles_ref.shape[0]

    def add_mirror(d, sums):
        wanted = spread_lanes(wanted_ref[d], image_ref.shape[2])
        mirror = arrived_ref[d].astype(jnp.float32)
        return tuple(total + jnp.where(wanted == k, mirror, 0.0) for k, total in enumerate(sums))

    zero = jnp.zeros(image_ref.shape[1:], image_ref.dtype)
    sums = lax.fori_loop(0, me + 1, add_mirror, (zero,) * row_blocks)
    for k, total in enumerate(sums):
        image_ref[k] = total

    def visit(i, carry):
        for j in range(CHUNK):
            s = i * CHUNK + j
            local = table_ref[FIRST + s] - me * row_blocks
            column = table_ref[FIRST + held.shape[0] + s]
            owner = column // row_blocks
            tile = jnp.where(owner == me, tiles_ref[column - owner * row_blocks], arrived_ref[owner])
            tile = jnp.where(s < live, tile, jnp.zeros_like(tile))
            image_ref[local] += lax.dot_general(tile, held[s], NT, preferred_element_type=jnp.float32)
        return carry

    lax.fori_loop(0, (live + CHUNK - 1) // CHUNK, visit, 0)

    def summed(left_ref):
        total = None
        for j in range(image_ref.shape[0]):
            term = lax.dot_general(
                left_ref[j].astype(jnp.float32), image_ref[j], NT, precision=HIGHEST,
                preferred_element_type=jnp.float32,
            )
            total = term if total is None else total + term
        return total

    squares = [summed(image_ref)]
    if with_projection:
        product = summed(tiles_ref)
        squares.append((product + product.T) * 0.5)
    diagonals = []
    for k, square in enumerate(squares):
        folded, diagonal = fold(square)
        diagonals.append(diagonal)
        low, high = folded[:ROWS], folded[ROWS:]
        own, given = jnp.where(me % 2 == 0, low, high), jnp.where(me % 2 == 0, high, low)
        for r in range(ROWS):
            at = row_of(k * ROWS + r)
            own_ref[:, at] = own[r : r + 1]
            given_ref[:, at] = given[r : r + 1]
    rest = own_ref.shape[1] // LANES - 1
    missing = LANES - len(diagonals) * diagonals[0].shape[1]
    last = jnp.concatenate(diagonals + [jnp.zeros((1, missing), jnp.float32)], axis=1)
    own_ref[:, row_of(rest)] = last
    given_ref[:, row_of(rest)] = last


def inverse_factor(gram):
    n = gram.shape[0]
    row_at = lax.broadcasted_iota(jnp.int32, (n, n), 0)
    col_at = lax.broadcasted_iota(jnp.int32, (n, n), 1)
    work = jnp.concatenate([gram, (row_at == col_at).astype(jnp.float32)], axis=1)
    at = lax.broadcasted_iota(jnp.int32, work.shape, 0)
    pivots = jnp.zeros(work.shape, jnp.float32)
    for k in range(0, n, PANEL):
        spread = [jnp.broadcast_to(work[:, k + j : k + j + 1], work.shape) for j in range(PANEL)]
        rows = [work[k + j : k + j + 1, :] for j in range(PANEL)]
        for j in range(PANEL):
            pivot = spread[j][k + j : k + j + 1, :]
            pivots = jnp.where(at == k + j, pivot, pivots)
            share = 1.0 / pivot
            scaled = rows[j] * share
            for m in range(j + 1, PANEL):
                spread[m] = spread[m] - spread[j] * (spread[m][k + j : k + j + 1, :] * share)
                rows[m] = rows[m] - spread[j][k + m : k + m + 1, :] * scaled
            rows[j] = scaled
        for j in range(PANEL):
            work = work - jnp.where(at > k + j, spread[j], 0.0) * rows[j]
    return work[:, n:] * (1.0 / jnp.sqrt(pivots[:, n:]))


def whole_sum(core, own_ref, other_ref, k):
    at = [row_of(k * ROWS + r) for r in range(ROWS)]
    own = jnp.concatenate([own_ref[:, a] for a in at], axis=0)
    other = jnp.concatenate([other_ref[:, a] for a in at], axis=0)
    rest = row_of(own_ref.shape[1] // LANES - 1)
    diagonals = jnp.where(core == 0, own_ref[:, rest], other_ref[:, rest])
    first = jnp.where(core == 0, own, other)
    second = jnp.where(core == 0, other, own)
    width = LANES // 4
    return unfold(jnp.concatenate([first, second], axis=0), diagonals[:, k * width : (k + 1) * width])


def normal_kernel(
    total_rows, table_ref, wanted_ref, own_ref, other_ref, image_ref, held, out_ref, tiles_ref,
):
    me, live = table_ref[ME], table_ref[LIVE]
    inverse = inverse_factor(whole_sum(me % 2, own_ref, other_ref, 0) / total_rows)
    for j in range(tiles_ref.shape[0]):
        tiles_ref[j] = jnp.dot(
            inverse, image_ref[j], precision=HIGHEST, preferred_element_type=jnp.float32
        ).astype(tiles_ref.dtype)
    multiply_mirrors(me, table_ref, live, tiles_ref, held, out_ref, lambda i: None)
    place_tiles(0, me, wanted_ref, tiles_ref, out_ref)


def last_kernel(total_rows, table_ref, own_ref, other_ref, image_ref, result_ref, projected_ref):
    core = table_ref[ME] % 2
    inverse = inverse_factor(whole_sum(core, own_ref, other_ref, 0) / total_rows)
    size = image_ref.shape[2]
    for j in range(image_ref.shape[0]):
        result_ref[:, j * size : (j + 1) * size] = jnp.dot(
            inverse, image_ref[j], precision=HIGHEST, preferred_element_type=jnp.float32
        )
    projected_ref[...] = whole_sum(core, own_ref, other_ref, 1) / total_rows


def spread_kernel(own_ref, given_ref, out_ref):
    chip = own_ref[...] + given_ref[...]
    for i in range(out_ref.shape[0]):
        out_ref[i] = chip


def total_kernel(parts_ref, out_ref):
    terms = [parts_ref[i] for i in range(parts_ref.shape[0])]
    while len(terms) > 1:
        terms = [a + b for a, b in zip(terms[::2], terms[1::2])] + terms[len(terms) // 2 * 2 :]
    out_ref[...] = terms[0]


def sum_over_devices(mine, given):
    swap = [(0, 1), (1, 0)]
    chips = lax.axis_size("rows")
    spread = pl.pallas_call(
        spread_kernel,
        out_shape=jax.ShapeDtypeStruct((chips,) + mine.shape, mine.dtype),
        in_specs=[VMEM] * 2,
        out_specs=VMEM,
        compiler_params=SMALL,
        name="spread",
    )(mine, lax.ppermute(given, "grp", swap))
    own = pl.pallas_call(
        total_kernel,
        out_shape=jax.ShapeDtypeStruct(mine.shape, mine.dtype),
        in_specs=[VMEM],
        out_specs=VMEM,
        compiler_params=SMALL,
        name="total",
    )(lax.all_to_all(spread, "rows", 0, 0, tiled=True))
    return own, lax.ppermute(own, "grp", swap)


def exchange(outgoing):
    return lax.all_to_all(outgoing, AXES, split_axis=0, concat_axis=0, tiled=True)


def on_device(start_basis, kernel_blocks, block_row, block_col, block_count):
    devices = lax.axis_size(AXES)
    me = lax.axis_index(AXES)
    slots, size, _ = kernel_blocks.shape
    own_rows, columns = start_basis.shape
    row_blocks = own_rows // size
    total_rows = own_rows * devices

    asked = pl.pallas_call(
        functools.partial(ask_kernel, row_blocks),
        out_shape=jax.ShapeDtypeStruct((devices, 1, 128), jnp.int32),
        in_specs=[SMEM, VMEM],
        out_specs=VMEM,
        compiler_params=SMALL,
        name="ask",
    )(block_count, block_col[None, :])
    wanted = exchange(asked)
    table = jnp.concatenate([me.reshape(1).astype(jnp.int32), block_count, block_row, block_col])

    params = pltpu.CompilerParams(vmem_limit_bytes=12 * MIB)
    tiles_shape = jax.ShapeDtypeStruct((row_blocks, columns, size), jnp.bfloat16)
    image_shape = jax.ShapeDtypeStruct((row_blocks, columns, size), jnp.float32)
    out_shape = jax.ShapeDtypeStruct((devices, columns, size), jnp.bfloat16)

    def image_of(tiles, arrived, with_projection):
        parts = 2 if with_projection else 1
        half = jax.ShapeDtypeStruct((1, (parts * ROWS + 1) * LANES), jnp.float32)
        return pl.pallas_call(
            functools.partial(image_kernel, with_projection),
            out_shape=(image_shape, half, half),
            in_specs=[SMEM] + [VMEM] * 4,
            out_specs=(VMEM, VMEM, VMEM),
            compiler_params=params,
            name="image",
        )(table, wanted, tiles, arrived, kernel_blocks)

    outgoing, tiles = pl.pallas_call(
        first_kernel,
        out_shape=(out_shape, tiles_shape),
        in_specs=[SMEM] + [VMEM, ANY],
        out_specs=(VMEM, VMEM),
        scratch_shapes=[
            pltpu.VMEM(kernel_blocks.shape, kernel_blocks.dtype),
            pltpu.SemaphoreType.DMA((slots // CHUNK,)),
        ],
        compiler_params=LARGE,
        name="first",
    )(table, start_basis.T, kernel_blocks)
    outgoing = pl.pallas_call(
        place_kernel,
        out_shape=out_shape,
        in_specs=[SMEM] + [VMEM] * 2 + [ANY],
        out_specs=VMEM,
        scratch_shapes=[pltpu.SemaphoreType.DMA((8,))],
        compiler_params=pltpu.CompilerParams(vmem_limit_bytes=56 * MIB),
        name="place",
    )(table, wanted, tiles, outgoing)
    image, own, given = image_of(tiles, exchange(outgoing), False)
    own, other = sum_over_devices(own, given)
    outgoing, tiles = pl.pallas_call(
        functools.partial(normal_kernel, total_rows),
        out_shape=(out_shape, tiles_shape),
        in_specs=[SMEM] + [VMEM] * 5,
        out_specs=(VMEM, VMEM),
        compiler_params=params,
        name="normal",
    )(table, wanted, own, other, image, kernel_blocks)
    image, own, given = image_of(tiles, exchange(outgoing), True)
    own, other = sum_over_devices(own, given)
    result, projected = pl.pallas_call(
        functools.partial(last_kernel, total_rows),
        out_shape=(
            jax.ShapeDtypeStruct((columns, own_rows), jnp.float32),
            jax.ShapeDtypeStruct((columns, columns), jnp.float32),
        ),
        in_specs=[SMEM] + [VMEM] * 3,
        out_specs=(VMEM, VMEM),
        compiler_params=params,
        name="last",
    )(table, own, other, image)
    return result.T, projected


def solution(mesh):
    in_specs = (
        P(AXES, None),
        P(AXES, None, None),
        P(AXES),
        P(AXES),
        P(AXES),
    )
    out_specs = (P(AXES, None), P())
    return jax.shard_map(
        on_device, mesh=mesh, in_specs=in_specs, out_specs=out_specs, check_vma=False
    )
```

```python
import functools

import jax
import jax.numpy as jnp
from jax import lax
from jax.experimental import pallas as pl
from jax.experimental.pallas import tpu as pltpu
from jax.sharding import PartitionSpec as P

AXES = ("rows", "grp")
HIGHEST = lax.Precision.HIGHEST
CHUNK = 23
PANEL = 8
ROWS, LANES = 8, 128
ME, LIVE, FIRST = 0, 1, 2
NT = (((1,), (1,)), ((), ()))
VMEM = pl.BlockSpec(memory_space=pltpu.VMEM)
SMEM = pl.BlockSpec(memory_space=pltpu.SMEM)
ANY = pl.BlockSpec(memory_space=pl.ANY)
MIB = 1024 * 1024
SMALL = pltpu.CompilerParams(vmem_limit_bytes=8 * MIB)
LARGE = pltpu.CompilerParams(vmem_limit_bytes=48 * MIB)


def block_copy(blocks_ref, held, sems, i):
    at = pl.ds(i * CHUNK, CHUNK)
    return pltpu.make_async_copy(blocks_ref.at[at], held.at[at], sems.at[i])


def start_blocks(live, blocks_ref, held, sems):
    def start(i, carry):
        block_copy(blocks_ref, held, sems, i).start()
        return carry

    lax.fori_loop(0, (live + CHUNK - 1) // CHUNK, start, 0)


def multiply_mirrors(me, table_ref, live, tiles_ref, held, out_ref, wait):
    row_blocks = tiles_ref.shape[0]

    def visit(i, carry):
        wait(i)
        for j in range(CHUNK):
            s = i * CHUNK + j
            local = table_ref[FIRST + s] - me * row_blocks
            place = jnp.where(s < live, table_ref[FIRST + held.shape[0] + s] // row_blocks, 0)
            product = jnp.dot(tiles_ref[local], held[s], preferred_element_type=jnp.float32)
            out_ref[place] = product.astype(out_ref.dtype)
        return carry

    lax.fori_loop(0, (live + CHUNK - 1) // CHUNK, visit, 0)


def place_tiles(start, end, wanted_ref, tiles_ref, out_ref):
    tiles = [tiles_ref[j].astype(jnp.float32) for j in range(tiles_ref.shape[0])]
    group = 4

    def visit(i, carry):
        for j in range(group):
            d = jnp.minimum(start + i * group + j, end - 1)
            wanted = spread_lanes(wanted_ref[d], tiles[0].shape[1])
            tile = tiles[0]
            for k in range(1, len(tiles)):
                tile = jnp.where(wanted == k, tiles[k], tile)
            out_ref[d] = tile.astype(out_ref.dtype)
        return carry

    lax.fori_loop(0, (end - start + group - 1) // group, visit, 0)


def spread_lanes(row, width):
    return jnp.concatenate([row] * (width // row.shape[1]), axis=1)


def ask_kernel(row_blocks, count_ref, col_ref, out_ref):
    devices, slots = out_ref.shape[0], col_ref.shape[1]
    column = jnp.broadcast_to(col_ref[...], (devices, slots))
    owner = column // row_blocks
    device = lax.broadcasted_iota(jnp.int32, (devices, slots), 0)
    alive = lax.broadcasted_iota(jnp.int32, (devices, slots), 1) < count_ref[0]
    block = jnp.where((owner == device) & alive, column - owner * row_blocks, -1)
    asked = jnp.max(block, axis=1, keepdims=True)
    out_ref[...] = jnp.broadcast_to(asked, (devices, out_ref.shape[2]))[:, None, :]


def first_kernel(table_ref, basis_ref, blocks_ref, out_ref, tiles_ref, held, sems):
    live = table_ref[LIVE]
    start_blocks(live, blocks_ref, held, sems)
    row_blocks, _, size = tiles_ref.shape
    for j in range(row_blocks):
        tiles_ref[j] = basis_ref[:, j * size : (j + 1) * size]
    multiply_mirrors(
        table_ref[ME], table_ref, live, tiles_ref, held, out_ref,
        lambda i: block_copy(blocks_ref, held, sems, i).wait(),
    )


def place_kernel(table_ref, wanted_ref, tiles_ref, given_ref, out_ref):
    me, devices = table_ref[ME], out_ref.shape[0]
    place_tiles(0, me, wanted_ref, tiles_ref, out_ref)
    group = 4

    def keep(i, carry):
        for j in range(group):
            d = jnp.minimum(me + i * group + j, devices - 1)
            out_ref[d] = given_ref[d]
        return carry

    lax.fori_loop(0, (devices - me + group - 1) // group, keep, 0)


def row_of(k):
    return slice(k * LANES, (k + 1) * LANES)


def fold(square):
    half = square.shape[0] // 2
    row_at = lax.broadcasted_iota(jnp.int32, (half, half), 0)
    col_at = lax.broadcasted_iota(jnp.int32, (half, half), 1)
    corner = square[half:, half:]
    mixed = jnp.where(row_at >= col_at, square[:half, :half], corner)
    sides = jnp.concatenate([mixed, square[half:, :half]], axis=1)
    folded = jnp.concatenate([sides[: half // 2], sides[half // 2 :]], axis=1)
    diagonal = jnp.sum(jnp.where(row_at == col_at, corner, 0.0), axis=0, keepdims=True)
    return folded, diagonal


def unfold(folded, diagonal):
    width = folded.shape[1] // 2
    half = width // 2
    row_at = lax.broadcasted_iota(jnp.int32, (half, half), 0)
    col_at = lax.broadcasted_iota(jnp.int32, (half, half), 1)
    sides = jnp.concatenate([folded[:, :width], folded[:, width:]], axis=0)
    mixed, side = sides[:, :half], sides[:, half:]
    turned = mixed.T
    upper = jnp.where(row_at >= col_at, mixed, turned)
    corner = jnp.where(row_at < col_at, mixed, turned)
    corner = jnp.where(row_at == col_at, jnp.broadcast_to(diagonal, (half, half)), corner)
    return jnp.concatenate(
        [jnp.concatenate([upper, side.T], axis=1), jnp.concatenate([side, corner], axis=1)], axis=0
    )


def image_kernel(
    with_projection, table_ref, wanted_ref, tiles_ref, arrived_ref, held,
    image_ref, own_ref, given_ref,
):
    me, live = table_ref[ME], table_ref[LIVE]
    row_blocks = tiles_ref.shape[0]

    def add_mirror(d, sums):
        wanted = spread_lanes(wanted_ref[d], image_ref.shape[2])
        mirror = arrived_ref[d].astype(jnp.float32)
        return tuple(total + jnp.where(wanted == k, mirror, 0.0) for k, total in enumerate(sums))

    zero = jnp.zeros(image_ref.shape[1:], image_ref.dtype)
    sums = lax.fori_loop(0, me + 1, add_mirror, (zero,) * row_blocks)
    for k, total in enumerate(sums):
        image_ref[k] = total

    def visit(i, carry):
        for j in range(CHUNK):
            s = i * CHUNK + j
            local = table_ref[FIRST + s] - me * row_blocks
            column = table_ref[FIRST + held.shape[0] + s]
            owner = column // row_blocks
            tile = jnp.where(owner == me, tiles_ref[column - owner * row_blocks], arrived_ref[owner])
            tile = jnp.where(s < live, tile, jnp.zeros_like(tile))
            image_ref[local] += lax.dot_general(tile, held[s], NT, preferred_element_type=jnp.float32)
        return carry

    lax.fori_loop(0, (live + CHUNK - 1) // CHUNK, visit, 0)

    def summed(left_ref):
        total = None
        for j in range(image_ref.shape[0]):
            term = lax.dot_general(
                left_ref[j].astype(jnp.float32), image_ref[j], NT, precision=HIGHEST,
                preferred_element_type=jnp.float32,
            )
            total = term if total is None else total + term
        return total

    squares = [summed(image_ref)]
    if with_projection:
        product = summed(tiles_ref)
        squares.append((product + product.T) * 0.5)
    diagonals = []
    for k, square in enumerate(squares):
        folded, diagonal = fold(square)
        diagonals.append(diagonal)
        low, high = folded[:ROWS], folded[ROWS:]
        own, given = jnp.where(me % 2 == 0, low, high), jnp.where(me % 2 == 0, high, low)
        for r in range(ROWS):
            at = row_of(k * ROWS + r)
            own_ref[:, at] = own[r : r + 1]
            given_ref[:, at] = given[r : r + 1]
    rest = own_ref.shape[1] // LANES - 1
    missing = LANES - len(diagonals) * diagonals[0].shape[1]
    last = jnp.concatenate(diagonals + [jnp.zeros((1, missing), jnp.float32)], axis=1)
    own_ref[:, row_of(rest)] = last
    given_ref[:, row_of(rest)] = last


def inverse_factor(gram):
    n = gram.shape[0]
    row_at = lax.broadcasted_iota(jnp.int32, (n, n), 0)
    col_at = lax.broadcasted_iota(jnp.int32, (n, n), 1)
    work = jnp.concatenate([gram, (row_at == col_at).astype(jnp.float32)], axis=1)
    at = lax.broadcasted_iota(jnp.int32, work.shape, 0)
    pivots = jnp.zeros(work.shape, jnp.float32)
    for k in range(0, n, PANEL):
        spread = [jnp.broadcast_to(work[:, k + j : k + j + 1], work.shape) for j in range(PANEL)]
        rows = [work[k + j : k + j + 1, :] for j in range(PANEL)]
        for j in range(PANEL):
            pivot = spread[j][k + j : k + j + 1, :]
            pivots = jnp.where(at == k + j, pivot, pivots)
            share = 1.0 / pivot
            scaled = rows[j] * share
            for m in range(j + 1, PANEL):
                spread[m] = spread[m] - spread[j] * (spread[m][k + j : k + j + 1, :] * share)
                rows[m] = rows[m] - spread[j][k + m : k + m + 1, :] * scaled
            rows[j] = scaled
        for j in range(PANEL):
            work = work - jnp.where(at > k + j, spread[j], 0.0) * rows[j]
    return work[:, n:] * (1.0 / jnp.sqrt(pivots[:, n:]))


def whole_sum(core, own_ref, other_ref, k):
    at = [row_of(k * ROWS + r) for r in range(ROWS)]
    own = jnp.concatenate([own_ref[:, a] for a in at], axis=0)
    other = jnp.concatenate([other_ref[:, a] for a in at], axis=0)
    rest = row_of(own_ref.shape[1] // LANES - 1)
    diagonals = jnp.where(core == 0, own_ref[:, rest], other_ref[:, rest])
    first = jnp.where(core == 0, own, other)
    second = jnp.where(core == 0, other, own)
    width = LANES // 4
    return unfold(jnp.concatenate([first, second], axis=0), diagonals[:, k * width : (k + 1) * width])


def normal_kernel(
    total_rows, table_ref, wanted_ref, own_ref, other_ref, image_ref, held, out_ref, tiles_ref,
):
    me, live = table_ref[ME], table_ref[LIVE]
    inverse = inverse_factor(whole_sum(me % 2, own_ref, other_ref, 0) / total_rows)
    for j in range(tiles_ref.shape[0]):
        tiles_ref[j] = jnp.dot(
            inverse, image_ref[j], precision=HIGHEST, preferred_element_type=jnp.float32
        ).astype(tiles_ref.dtype)
    multiply_mirrors(me, table_ref, live, tiles_ref, held, out_ref, lambda i: None)
    place_tiles(0, me, wanted_ref, tiles_ref, out_ref)


def last_kernel(total_rows, table_ref, own_ref, other_ref, image_ref, result_ref, projected_ref):
    core = table_ref[ME] % 2
    inverse = inverse_factor(whole_sum(core, own_ref, other_ref, 0) / total_rows)
    size = image_ref.shape[2]
    for j in range(image_ref.shape[0]):
        result_ref[:, j * size : (j + 1) * size] = jnp.dot(
            inverse, image_ref[j], precision=HIGHEST, preferred_element_type=jnp.float32
        )
    projected_ref[...] = whole_sum(core, own_ref, other_ref, 1) / total_rows


def spread_kernel(own_ref, given_ref, out_ref):
    chip = own_ref[...] + given_ref[...]
    for i in range(out_ref.shape[0]):
        out_ref[i] = chip


def total_kernel(parts_ref, out_ref):
    terms = [parts_ref[i] for i in range(parts_ref.shape[0])]
    while len(terms) > 1:
        terms = [a + b for a, b in zip(terms[::2], terms[1::2])] + terms[len(terms) // 2 * 2 :]
    out_ref[...] = terms[0]


def sum_over_devices(mine, given):
    swap = [(0, 1), (1, 0)]
    chips = lax.axis_size("rows")
    spread = pl.pallas_call(
        spread_kernel,
        out_shape=jax.ShapeDtypeStruct((chips,) + mine.shape, mine.dtype),
        in_specs=[VMEM] * 2,
        out_specs=VMEM,
        compiler_params=SMALL,
        name="spread",
    )(mine, lax.ppermute(given, "grp", swap))
    own = pl.pallas_call(
        total_kernel,
        out_shape=jax.ShapeDtypeStruct(mine.shape, mine.dtype),
        in_specs=[VMEM],
        out_specs=VMEM,
        compiler_params=SMALL,
        name="total",
    )(lax.all_to_all(spread, "rows", 0, 0, tiled=True))
    return own, lax.ppermute(own, "grp", swap)


def exchange(outgoing):
    return lax.all_to_all(outgoing, AXES, split_axis=0, concat_axis=0, tiled=True)


def on_device(start_basis, kernel_blocks, block_row, block_col, block_count):
    devices = lax.axis_size(AXES)
    me = lax.axis_index(AXES)
    slots, size, _ = kernel_blocks.shape
    own_rows, columns = start_basis.shape
    row_blocks = own_rows // size
    total_rows = own_rows * devices

    asked = pl.pallas_call(
        functools.partial(ask_kernel, row_blocks),
        out_shape=jax.ShapeDtypeStruct((devices, 1, 128), jnp.int32),
        in_specs=[SMEM, VMEM],
        out_specs=VMEM,
        compiler_params=SMALL,
        name="ask",
    )(block_count, block_col[None, :])
    wanted = exchange(asked)
    table = jnp.concatenate([me.reshape(1).astype(jnp.int32), block_count, block_row, block_col])

    params = pltpu.CompilerParams(vmem_limit_bytes=12 * MIB)
    tiles_shape = jax.ShapeDtypeStruct((row_blocks, columns, size), jnp.bfloat16)
    image_shape = jax.ShapeDtypeStruct((row_blocks, columns, size), jnp.float32)
    out_shape = jax.ShapeDtypeStruct((devices, columns, size), jnp.bfloat16)

    def image_of(tiles, arrived, with_projection):
        parts = 2 if with_projection else 1
        half = jax.ShapeDtypeStruct((1, (parts * ROWS + 1) * LANES), jnp.float32)
        return pl.pallas_call(
            functools.partial(image_kernel, with_projection),
            out_shape=(image_shape, half, half),
            in_specs=[SMEM] + [VMEM] * 4,
            out_specs=(VMEM, VMEM, VMEM),
            compiler_params=params,
            name="image",
        )(table, wanted, tiles, arrived, kernel_blocks)

    outgoing, tiles = pl.pallas_call(
        first_kernel,
        out_shape=(out_shape, tiles_shape),
        in_specs=[SMEM] + [VMEM, ANY],
        out_specs=(VMEM, VMEM),
        scratch_shapes=[
            pltpu.VMEM(kernel_blocks.shape, kernel_blocks.dtype),
            pltpu.SemaphoreType.DMA((slots // CHUNK,)),
        ],
        compiler_params=LARGE,
        name="first",
    )(table, start_basis.T, kernel_blocks)
    outgoing = pl.pallas_call(
        place_kernel,
        out_shape=out_shape,
        in_specs=[SMEM] + [VMEM] * 3,
        out_specs=VMEM,
        compiler_params=params,
        name="place",
    )(table, wanted, tiles, outgoing)
    image, own, given = image_of(tiles, exchange(outgoing), False)
    own, other = sum_over_devices(own, given)
    outgoing, tiles = pl.pallas_call(
        functools.partial(normal_kernel, total_rows),
        out_shape=(out_shape, tiles_shape),
        in_specs=[SMEM] + [VMEM] * 5,
        out_specs=(VMEM, VMEM),
        compiler_params=params,
        name="normal",
    )(table, wanted, own, other, image, kernel_blocks)
    image, own, given = image_of(tiles, exchange(outgoing), True)
    own, other = sum_over_devices(own, given)
    result, projected = pl.pallas_call(
        functools.partial(last_kernel, total_rows),
        out_shape=(
            jax.ShapeDtypeStruct((columns, own_rows), jnp.float32),
            jax.ShapeDtypeStruct((columns, columns), jnp.float32),
        ),
        in_specs=[SMEM] + [VMEM] * 3,
        out_specs=(VMEM, VMEM),
        compiler_params=params,
        name="last",
    )(table, own, other, image)
    return result.T, projected


def solution(mesh):
    in_specs = (
        P(AXES, None),
        P(AXES, None, None),
        P(AXES),
        P(AXES),
        P(AXES),
    )
    out_specs = (P(AXES, None), P())
    return jax.shard_map(
        on_device, mesh=mesh, in_specs=in_specs, out_specs=out_specs, check_vma=False
    )
```

```python
import functools

import jax
import jax.numpy as jnp
from jax import lax
from jax.experimental import pallas as pl
from jax.experimental.pallas import tpu as pltpu
from jax.sharding import PartitionSpec as P

AXES = ("rows", "grp")
HIGHEST = lax.Precision.HIGHEST
CHUNK = 23
PANEL = 8
ROWS, LANES = 8, 128
ME, LIVE, FIRST = 0, 1, 2
NT = (((1,), (1,)), ((), ()))
VMEM = pl.BlockSpec(memory_space=pltpu.VMEM)
SMEM = pl.BlockSpec(memory_space=pltpu.SMEM)
ANY = pl.BlockSpec(memory_space=pl.ANY)
MIB = 1024 * 1024
SMALL = pltpu.CompilerParams(vmem_limit_bytes=8 * MIB)
LARGE = pltpu.CompilerParams(vmem_limit_bytes=48 * MIB)


def block_copy(blocks_ref, held, sems, i):
    at = pl.ds(i * CHUNK, CHUNK)
    return pltpu.make_async_copy(blocks_ref.at[at], held.at[at], sems.at[i])


def start_blocks(live, blocks_ref, held, sems):
    def start(i, carry):
        block_copy(blocks_ref, held, sems, i).start()
        return carry

    lax.fori_loop(0, (live + CHUNK - 1) // CHUNK, start, 0)


def place_of(s, table_ref, live, row_blocks, slots):
    return jnp.where(s < live, table_ref[FIRST + slots + s] // row_blocks, 0)


def multiply_mirrors(me, table_ref, live, tiles_ref, held, out_ref, wait, placed):
    row_blocks = tiles_ref.shape[0]

    def visit(i, carry):
        wait(i)
        for j in range(CHUNK):
            s = i * CHUNK + j
            local = table_ref[FIRST + s] - me * row_blocks
            place = place_of(s, table_ref, live, row_blocks, held.shape[0]) if placed else s
            product = jnp.dot(tiles_ref[local], held[s], preferred_element_type=jnp.float32)
            out_ref[place] = product.astype(out_ref.dtype)
        return carry

    lax.fori_loop(0, (live + CHUNK - 1) // CHUNK, visit, 0)


def place_tiles(start, end, wanted_ref, tiles_ref, out_ref):
    tiles = [tiles_ref[j].astype(jnp.float32) for j in range(tiles_ref.shape[0])]
    group = 4

    def visit(i, carry):
        for j in range(group):
            d = jnp.minimum(start + i * group + j, end - 1)
            wanted = spread_lanes(wanted_ref[d], tiles[0].shape[1])
            tile = tiles[0]
            for k in range(1, len(tiles)):
                tile = jnp.where(wanted == k, tiles[k], tile)
            out_ref[d] = tile.astype(out_ref.dtype)
        return carry

    lax.fori_loop(0, (end - start + group - 1) // group, visit, 0)


def spread_lanes(row, width):
    return jnp.concatenate([row] * (width // row.shape[1]), axis=1)


def ask_kernel(row_blocks, count_ref, col_ref, out_ref):
    devices, slots = out_ref.shape[0], col_ref.shape[1]
    column = jnp.broadcast_to(col_ref[...], (devices, slots))
    owner = column // row_blocks
    device = lax.broadcasted_iota(jnp.int32, (devices, slots), 0)
    alive = lax.broadcasted_iota(jnp.int32, (devices, slots), 1) < count_ref[0]
    block = jnp.where((owner == device) & alive, column - owner * row_blocks, -1)
    asked = jnp.max(block, axis=1, keepdims=True)
    out_ref[...] = jnp.broadcast_to(asked, (devices, out_ref.shape[2]))[:, None, :]


def first_kernel(table_ref, basis_ref, blocks_ref, out_ref, tiles_ref, held, sems):
    live = table_ref[LIVE]
    start_blocks(live, blocks_ref, held, sems)
    row_blocks, _, size = tiles_ref.shape
    for j in range(row_blocks):
        tiles_ref[j] = basis_ref[:, j * size : (j + 1) * size]
    multiply_mirrors(
        table_ref[ME], table_ref, live, tiles_ref, held, out_ref,
        lambda i: block_copy(blocks_ref, held, sems, i).wait(), False,
    )


def place_kernel(table_ref, wanted_ref, tiles_ref, products_ref, out_ref):
    me, live = table_ref[ME], table_ref[LIVE]
    slots = products_ref.shape[0]
    group = 4

    def place(i, carry):
        for j in range(group):
            s = i * group + j
            out_ref[place_of(s, table_ref, live, tiles_ref.shape[0], slots)] = products_ref[s]
        return carry

    lax.fori_loop(0, (live + group - 1) // group, place, 0)
    place_tiles(0, me, wanted_ref, tiles_ref, out_ref)


def row_of(k):
    return slice(k * LANES, (k + 1) * LANES)


def fold(square):
    half = square.shape[0] // 2
    row_at = lax.broadcasted_iota(jnp.int32, (half, half), 0)
    col_at = lax.broadcasted_iota(jnp.int32, (half, half), 1)
    corner = square[half:, half:]
    mixed = jnp.where(row_at >= col_at, square[:half, :half], corner)
    sides = jnp.concatenate([mixed, square[half:, :half]], axis=1)
    folded = jnp.concatenate([sides[: half // 2], sides[half // 2 :]], axis=1)
    diagonal = jnp.sum(jnp.where(row_at == col_at, corner, 0.0), axis=0, keepdims=True)
    return folded, diagonal


def unfold(folded, diagonal):
    width = folded.shape[1] // 2
    half = width // 2
    row_at = lax.broadcasted_iota(jnp.int32, (half, half), 0)
    col_at = lax.broadcasted_iota(jnp.int32, (half, half), 1)
    sides = jnp.concatenate([folded[:, :width], folded[:, width:]], axis=0)
    mixed, side = sides[:, :half], sides[:, half:]
    turned = mixed.T
    upper = jnp.where(row_at >= col_at, mixed, turned)
    corner = jnp.where(row_at < col_at, mixed, turned)
    corner = jnp.where(row_at == col_at, jnp.broadcast_to(diagonal, (half, half)), corner)
    return jnp.concatenate(
        [jnp.concatenate([upper, side.T], axis=1), jnp.concatenate([side, corner], axis=1)], axis=0
    )


def image_kernel(
    with_projection, table_ref, wanted_ref, tiles_ref, arrived_ref, held,
    image_ref, own_ref, given_ref, *turned_ref,
):
    me, live = table_ref[ME], table_ref[LIVE]
    row_blocks = tiles_ref.shape[0]

    group = 4

    def add_mirrors(i, sums):
        for j in range(group):
            d = i * group + j
            at = jnp.minimum(d, me)
            wanted = spread_lanes(wanted_ref[at], image_ref.shape[2])
            wanted = jnp.where(d <= me, wanted, -1)
            mirror = arrived_ref[at].astype(jnp.float32)
            sums = tuple(total + jnp.where(wanted == k, mirror, 0.0) for k, total in enumerate(sums))
        return sums

    zero = jnp.zeros(image_ref.shape[1:], image_ref.dtype)
    sums = lax.fori_loop(0, (me + group) // group, add_mirrors, (zero,) * row_blocks)
    for k, total in enumerate(sums):
        image_ref[k] = total

    def visit(i, carry):
        for j in range(CHUNK):
            s = i * CHUNK + j
            local = table_ref[FIRST + s] - me * row_blocks
            column = table_ref[FIRST + held.shape[0] + s]
            owner = column // row_blocks
            tile = jnp.where(owner == me, tiles_ref[column - owner * row_blocks], arrived_ref[owner])
            tile = jnp.where(s < live, tile, jnp.zeros_like(tile))
            block = held[s]
            if turned_ref:
                block = block.T
                turned_ref[0][s] = block
            image_ref[local] += jnp.dot(tile, block, preferred_element_type=jnp.float32)
        return carry

    lax.fori_loop(0, (live + CHUNK - 1) // CHUNK, visit, 0)

    def summed(left_ref):
        total = None
        for j in range(image_ref.shape[0]):
            term = lax.dot_general(
                left_ref[j].astype(jnp.float32), image_ref[j], NT, precision=HIGHEST,
                preferred_element_type=jnp.float32,
            )
            total = term if total is None else total + term
        return total

    squares = [summed(image_ref)]
    if with_projection:
        product = summed(tiles_ref)
        squares.append((product + product.T) * 0.5)
    diagonals = []
    for k, square in enumerate(squares):
        folded, diagonal = fold(square)
        diagonals.append(diagonal)
        low, high = folded[:ROWS], folded[ROWS:]
        own, given = jnp.where(me % 2 == 0, low, high), jnp.where(me % 2 == 0, high, low)
        for r in range(ROWS):
            at = row_of(k * ROWS + r)
            own_ref[:, at] = own[r : r + 1]
            given_ref[:, at] = given[r : r + 1]
    rest = own_ref.shape[1] // LANES - 1
    missing = LANES - len(diagonals) * diagonals[0].shape[1]
    last = jnp.concatenate(diagonals + [jnp.zeros((1, missing), jnp.float32)], axis=1)
    own_ref[:, row_of(rest)] = last
    given_ref[:, row_of(rest)] = last


def inverse_factor(gram):
    n = gram.shape[0]
    row_at = lax.broadcasted_iota(jnp.int32, (n, n), 0)
    col_at = lax.broadcasted_iota(jnp.int32, (n, n), 1)
    work = jnp.concatenate([gram, (row_at == col_at).astype(jnp.float32)], axis=1)
    at = lax.broadcasted_iota(jnp.int32, work.shape, 0)
    pivots = jnp.zeros(work.shape, jnp.float32)
    for k in range(0, n, PANEL):
        spread = [jnp.broadcast_to(work[:, k + j : k + j + 1], work.shape) for j in range(PANEL)]
        rows = [work[k + j : k + j + 1, :] for j in range(PANEL)]
        for j in range(PANEL):
            pivot = spread[j][k + j : k + j + 1, :]
            pivots = jnp.where(at == k + j, pivot, pivots)
            share = 1.0 / pivot
            scaled = rows[j] * share
            for m in range(j + 1, PANEL):
                spread[m] = spread[m] - spread[j] * (spread[m][k + j : k + j + 1, :] * share)
                rows[m] = rows[m] - spread[j][k + m : k + m + 1, :] * scaled
            rows[j] = scaled
        for j in range(PANEL):
            work = work - jnp.where(at > k + j, spread[j], 0.0) * rows[j]
    return work[:, n:] * (1.0 / jnp.sqrt(pivots[:, n:]))


def whole_sum(core, own_ref, other_ref, k):
    at = [row_of(k * ROWS + r) for r in range(ROWS)]
    own = jnp.concatenate([own_ref[:, a] for a in at], axis=0)
    other = jnp.concatenate([other_ref[:, a] for a in at], axis=0)
    rest = row_of(own_ref.shape[1] // LANES - 1)
    diagonals = jnp.where(core == 0, own_ref[:, rest], other_ref[:, rest])
    first = jnp.where(core == 0, own, other)
    second = jnp.where(core == 0, other, own)
    width = LANES // 4
    return unfold(jnp.concatenate([first, second], axis=0), diagonals[:, k * width : (k + 1) * width])


def normal_kernel(
    total_rows, table_ref, wanted_ref, own_ref, other_ref, image_ref, held, out_ref, tiles_ref,
):
    me, live = table_ref[ME], table_ref[LIVE]
    inverse = inverse_factor(whole_sum(me % 2, own_ref, other_ref, 0) / total_rows)
    for j in range(tiles_ref.shape[0]):
        tiles_ref[j] = jnp.dot(
            inverse, image_ref[j], precision=HIGHEST, preferred_element_type=jnp.float32
        ).astype(tiles_ref.dtype)
    multiply_mirrors(me, table_ref, live, tiles_ref, held, out_ref, lambda i: None, True)
    place_tiles(0, me, wanted_ref, tiles_ref, out_ref)


def last_kernel(total_rows, table_ref, own_ref, other_ref, image_ref, result_ref, projected_ref):
    core = table_ref[ME] % 2
    inverse = inverse_factor(whole_sum(core, own_ref, other_ref, 0) / total_rows)
    size = image_ref.shape[2]
    for j in range(image_ref.shape[0]):
        result_ref[:, j * size : (j + 1) * size] = jnp.dot(
            inverse, image_ref[j], precision=HIGHEST, preferred_element_type=jnp.float32
        )
    projected_ref[...] = whole_sum(core, own_ref, other_ref, 1) / total_rows


def spread_kernel(own_ref, given_ref, out_ref):
    chip = own_ref[...] + given_ref[...]
    for i in range(out_ref.shape[0]):
        out_ref[i] = chip


def total_kernel(parts_ref, out_ref):
    terms = [parts_ref[i] for i in range(parts_ref.shape[0])]
    while len(terms) > 1:
        terms = [a + b for a, b in zip(terms[::2], terms[1::2])] + terms[len(terms) // 2 * 2 :]
    out_ref[...] = terms[0]


def sum_over_devices(mine, given):
    swap = [(0, 1), (1, 0)]
    chips = lax.axis_size("rows")
    spread = pl.pallas_call(
        spread_kernel,
        out_shape=jax.ShapeDtypeStruct((chips,) + mine.shape, mine.dtype),
        in_specs=[VMEM] * 2,
        out_specs=VMEM,
        compiler_params=SMALL,
        name="spread",
    )(mine, lax.ppermute(given, "grp", swap))
    own = pl.pallas_call(
        total_kernel,
        out_shape=jax.ShapeDtypeStruct(mine.shape, mine.dtype),
        in_specs=[VMEM],
        out_specs=VMEM,
        compiler_params=SMALL,
        name="total",
    )(lax.all_to_all(spread, "rows", 0, 0, tiled=True))
    return own, lax.ppermute(own, "grp", swap)


def exchange(outgoing):
    return lax.all_to_all(outgoing, AXES, split_axis=0, concat_axis=0, tiled=True)


def on_device(start_basis, kernel_blocks, block_row, block_col, block_count):
    devices = lax.axis_size(AXES)
    me = lax.axis_index(AXES)
    slots, size, _ = kernel_blocks.shape
    own_rows, columns = start_basis.shape
    row_blocks = own_rows // size
    total_rows = own_rows * devices

    asked = pl.pallas_call(
        functools.partial(ask_kernel, row_blocks),
        out_shape=jax.ShapeDtypeStruct((devices, 1, 128), jnp.int32),
        in_specs=[SMEM, VMEM],
        out_specs=VMEM,
        compiler_params=SMALL,
        name="ask",
    )(block_count, block_col[None, :])
    wanted = exchange(asked)
    table = jnp.concatenate([me.reshape(1).astype(jnp.int32), block_count, block_row, block_col])

    params = pltpu.CompilerParams(vmem_limit_bytes=12 * MIB)
    tiles_shape = jax.ShapeDtypeStruct((row_blocks, columns, size), jnp.bfloat16)
    image_shape = jax.ShapeDtypeStruct((row_blocks, columns, size), jnp.float32)
    out_shape = jax.ShapeDtypeStruct((devices, columns, size), jnp.bfloat16)

    def image_of(tiles, arrived, blocks, with_projection):
        parts = 2 if with_projection else 1
        half = jax.ShapeDtypeStruct((1, (parts * ROWS + 1) * LANES), jnp.float32)
        turned = () if with_projection else (jax.ShapeDtypeStruct(blocks.shape, blocks.dtype),)
        return pl.pallas_call(
            functools.partial(image_kernel, with_projection),
            out_shape=(image_shape, half, half) + turned,
            in_specs=[SMEM] + [VMEM] * 4,
            out_specs=(VMEM,) * (3 + len(turned)),
            compiler_params=params,
            name="image",
        )(table, wanted, tiles, arrived, blocks)

    products, tiles = pl.pallas_call(
        first_kernel,
        out_shape=(jax.ShapeDtypeStruct((slots, columns, size), jnp.bfloat16), tiles_shape),
        in_specs=[SMEM] + [VMEM, ANY],
        out_specs=(VMEM, VMEM),
        scratch_shapes=[
            pltpu.VMEM(kernel_blocks.shape, kernel_blocks.dtype),
            pltpu.SemaphoreType.DMA((slots // CHUNK,)),
        ],
        compiler_params=LARGE,
        name="first",
    )(table, start_basis.T, kernel_blocks)
    outgoing = pl.pallas_call(
        place_kernel,
        out_shape=out_shape,
        in_specs=[SMEM] + [VMEM] * 3,
        out_specs=VMEM,
        compiler_params=params,
        name="place",
    )(table, wanted, tiles, products)
    image, own, given, turned = image_of(tiles, exchange(outgoing), kernel_blocks, False)
    own, other = sum_over_devices(own, given)
    outgoing, tiles = pl.pallas_call(
        functools.partial(normal_kernel, total_rows),
        out_shape=(out_shape, tiles_shape),
        in_specs=[SMEM] + [VMEM] * 5,
        out_specs=(VMEM, VMEM),
        compiler_params=params,
        name="normal",
    )(table, wanted, own, other, image, kernel_blocks)
    image, own, given = image_of(tiles, exchange(outgoing), turned, True)
    own, other = sum_over_devices(own, given)
    result, projected = pl.pallas_call(
        functools.partial(last_kernel, total_rows),
        out_shape=(
            jax.ShapeDtypeStruct((columns, own_rows), jnp.float32),
            jax.ShapeDtypeStruct((columns, columns), jnp.float32),
        ),
        in_specs=[SMEM] + [VMEM] * 3,
        out_specs=(VMEM, VMEM),
        compiler_params=params,
        name="last",
    )(table, own, other, image)
    return result.T, projected


def solution(mesh):
    in_specs = (
        P(AXES, None),
        P(AXES, None, None),
        P(AXES),
        P(AXES),
        P(AXES),
    )
    out_specs = (P(AXES, None), P())
    return jax.shard_map(
        on_device, mesh=mesh, in_specs=in_specs, out_specs=out_specs, check_vma=False
    )
```

```python
import functools

import jax
import jax.numpy as jnp
from jax import lax
from jax.experimental import pallas as pl
from jax.experimental.pallas import tpu as pltpu
from jax.sharding import PartitionSpec as P

AXES = ("rows", "grp")
HIGHEST = lax.Precision.HIGHEST
CHUNK = 23
PANEL = 8
ROWS, LANES = 8, 128
ME, LIVE, FIRST = 0, 1, 2
NT = (((1,), (1,)), ((), ()))
VMEM = pl.BlockSpec(memory_space=pltpu.VMEM)
SMEM = pl.BlockSpec(memory_space=pltpu.SMEM)
ANY = pl.BlockSpec(memory_space=pl.ANY)
MIB = 1024 * 1024
SMALL = pltpu.CompilerParams(vmem_limit_bytes=8 * MIB)
LARGE = pltpu.CompilerParams(vmem_limit_bytes=48 * MIB)


def block_copy(blocks_ref, held, sems, i):
    at = pl.ds(i * CHUNK, CHUNK)
    return pltpu.make_async_copy(blocks_ref.at[at], held.at[at], sems.at[i])


def start_blocks(live, blocks_ref, held, sems):
    def start(i, carry):
        block_copy(blocks_ref, held, sems, i).start()
        return carry

    lax.fori_loop(0, (live + CHUNK - 1) // CHUNK, start, 0)


def place_of(s, table_ref, live, row_blocks, slots):
    return jnp.where(s < live, table_ref[FIRST + slots + s] // row_blocks, 0)


def multiply_mirrors(me, table_ref, live, tiles_ref, held, out_ref, wait, placed):
    row_blocks = tiles_ref.shape[0]

    def visit(i, carry):
        wait(i)
        for j in range(CHUNK):
            s = i * CHUNK + j
            local = table_ref[FIRST + s] - me * row_blocks
            place = place_of(s, table_ref, live, row_blocks, held.shape[0]) if placed else s
            product = jnp.dot(tiles_ref[local], held[s], preferred_element_type=jnp.float32)
            out_ref[place] = product.astype(out_ref.dtype)
        return carry

    lax.fori_loop(0, (live + CHUNK - 1) // CHUNK, visit, 0)


def place_tiles(start, end, wanted_ref, tiles_ref, out_ref):
    tiles = [tiles_ref[j].astype(jnp.float32) for j in range(tiles_ref.shape[0])]
    group = 4

    def visit(i, carry):
        for j in range(group):
            d = jnp.minimum(start + i * group + j, end - 1)
            wanted = spread_lanes(wanted_ref[d], tiles[0].shape[1])
            tile = tiles[0]
            for k in range(1, len(tiles)):
                tile = jnp.where(wanted == k, tiles[k], tile)
            out_ref[d] = tile.astype(out_ref.dtype)
        return carry

    lax.fori_loop(0, (end - start + group - 1) // group, visit, 0)


def spread_lanes(row, width):
    return jnp.concatenate([row] * (width // row.shape[1]), axis=1)


def ask_kernel(row_blocks, count_ref, col_ref, out_ref):
    devices, slots = out_ref.shape[0], col_ref.shape[1]
    column = jnp.broadcast_to(col_ref[...], (devices, slots))
    owner = column // row_blocks
    device = lax.broadcasted_iota(jnp.int32, (devices, slots), 0)
    alive = lax.broadcasted_iota(jnp.int32, (devices, slots), 1) < count_ref[0]
    block = jnp.where((owner == device) & alive, column - owner * row_blocks, -1)
    asked = jnp.max(block, axis=1, keepdims=True)
    out_ref[...] = jnp.broadcast_to(asked, (devices, out_ref.shape[2]))[:, None, :]


def first_kernel(table_ref, basis_ref, blocks_ref, out_ref, tiles_ref, held, sems):
    live = table_ref[LIVE]
    start_blocks(live, blocks_ref, held, sems)
    row_blocks, _, size = tiles_ref.shape
    for j in range(row_blocks):
        tiles_ref[j] = basis_ref[:, j * size : (j + 1) * size]
    multiply_mirrors(
        table_ref[ME], table_ref, live, tiles_ref, held, out_ref,
        lambda i: block_copy(blocks_ref, held, sems, i).wait(), False,
    )


def place_kernel(table_ref, wanted_ref, tiles_ref, products_ref, out_ref):
    me, live = table_ref[ME], table_ref[LIVE]
    slots = products_ref.shape[0]
    group = 4

    def place(i, carry):
        for j in range(group):
            s = i * group + j
            out_ref[place_of(s, table_ref, live, tiles_ref.shape[0], slots)] = products_ref[s]
        return carry

    lax.fori_loop(0, (live + group - 1) // group, place, 0)
    place_tiles(0, me, wanted_ref, tiles_ref, out_ref)


def row_of(k):
    return slice(k * LANES, (k + 1) * LANES)


def fold(square):
    half = square.shape[0] // 2
    row_at = lax.broadcasted_iota(jnp.int32, (half, half), 0)
    col_at = lax.broadcasted_iota(jnp.int32, (half, half), 1)
    corner = square[half:, half:]
    mixed = jnp.where(row_at >= col_at, square[:half, :half], corner)
    sides = jnp.concatenate([mixed, square[half:, :half]], axis=1)
    folded = jnp.concatenate([sides[: half // 2], sides[half // 2 :]], axis=1)
    diagonal = jnp.sum(jnp.where(row_at == col_at, corner, 0.0), axis=0, keepdims=True)
    return folded, diagonal


def unfold(folded, diagonal):
    width = folded.shape[1] // 2
    half = width // 2
    row_at = lax.broadcasted_iota(jnp.int32, (half, half), 0)
    col_at = lax.broadcasted_iota(jnp.int32, (half, half), 1)
    sides = jnp.concatenate([folded[:, :width], folded[:, width:]], axis=0)
    mixed, side = sides[:, :half], sides[:, half:]
    turned = mixed.T
    upper = jnp.where(row_at >= col_at, mixed, turned)
    corner = jnp.where(row_at < col_at, mixed, turned)
    corner = jnp.where(row_at == col_at, jnp.broadcast_to(diagonal, (half, half)), corner)
    return jnp.concatenate(
        [jnp.concatenate([upper, side.T], axis=1), jnp.concatenate([side, corner], axis=1)], axis=0
    )


def image_kernel(
    with_projection, table_ref, wanted_ref, tiles_ref, arrived_ref, held,
    image_ref, own_ref, given_ref, *turned_ref,
):
    me, live = table_ref[ME], table_ref[LIVE]
    row_blocks = tiles_ref.shape[0]

    group = 4

    for part in range(image_ref.shape[2] // LANES):

        def add_mirrors(i, sums, at=row_of(part)):
            for j in range(group):
                d = i * group + j
                inside = jnp.minimum(d, me)
                wanted = jnp.where(d <= me, wanted_ref[inside], -1)
                mirror = arrived_ref[inside, :, at].astype(jnp.float32)
                sums = tuple(total + jnp.where(wanted == k, mirror, 0.0) for k, total in enumerate(sums))
            return sums

        zero = jnp.zeros((image_ref.shape[1], LANES), image_ref.dtype)
        sums = lax.fori_loop(0, (me + group) // group, add_mirrors, (zero,) * row_blocks)
        for k, total in enumerate(sums):
            image_ref[k, :, row_of(part)] = total

    def visit(i, carry):
        for j in range(CHUNK):
            s = i * CHUNK + j
            local = table_ref[FIRST + s] - me * row_blocks
            column = table_ref[FIRST + held.shape[0] + s]
            owner = column // row_blocks
            tile = jnp.where(owner == me, tiles_ref[column - owner * row_blocks], arrived_ref[owner])
            tile = jnp.where(s < live, tile, jnp.zeros_like(tile))
            block = held[s]
            if turned_ref:
                block = block.T
                turned_ref[0][s] = block
            image_ref[local] += jnp.dot(tile, block, preferred_element_type=jnp.float32)
        return carry

    lax.fori_loop(0, (live + CHUNK - 1) // CHUNK, visit, 0)

    def summed(left_ref):
        total = None
        for j in range(image_ref.shape[0]):
            term = lax.dot_general(
                left_ref[j].astype(jnp.float32), image_ref[j], NT, precision=HIGHEST,
                preferred_element_type=jnp.float32,
            )
            total = term if total is None else total + term
        return total

    squares = [summed(image_ref)]
    if with_projection:
        product = summed(tiles_ref)
        squares.append((product + product.T) * 0.5)
    diagonals = []
    for k, square in enumerate(squares):
        folded, diagonal = fold(square)
        diagonals.append(diagonal)
        low, high = folded[:ROWS], folded[ROWS:]
        own, given = jnp.where(me % 2 == 0, low, high), jnp.where(me % 2 == 0, high, low)
        for r in range(ROWS):
            at = row_of(k * ROWS + r)
            own_ref[:, at] = own[r : r + 1]
            given_ref[:, at] = given[r : r + 1]
    rest = own_ref.shape[1] // LANES - 1
    missing = LANES - len(diagonals) * diagonals[0].shape[1]
    last = jnp.concatenate(diagonals + [jnp.zeros((1, missing), jnp.float32)], axis=1)
    own_ref[:, row_of(rest)] = last
    given_ref[:, row_of(rest)] = last


def inverse_factor(gram):
    n = gram.shape[0]
    row_at = lax.broadcasted_iota(jnp.int32, (n, n), 0)
    col_at = lax.broadcasted_iota(jnp.int32, (n, n), 1)
    work = jnp.concatenate([gram, (row_at == col_at).astype(jnp.float32)], axis=1)
    at = lax.broadcasted_iota(jnp.int32, work.shape, 0)
    pivots = jnp.zeros(work.shape, jnp.float32)
    for k in range(0, n, PANEL):
        spread = [jnp.broadcast_to(work[:, k + j : k + j + 1], work.shape) for j in range(PANEL)]
        rows = [work[k + j : k + j + 1, :] for j in range(PANEL)]
        for j in range(PANEL):
            pivot = spread[j][k + j : k + j + 1, :]
            pivots = jnp.where(at == k + j, pivot, pivots)
            share = 1.0 / pivot
            scaled = rows[j] * share
            for m in range(j + 1, PANEL):
                spread[m] = spread[m] - spread[j] * (spread[m][k + j : k + j + 1, :] * share)
                rows[m] = rows[m] - spread[j][k + m : k + m + 1, :] * scaled
            rows[j] = scaled
        for j in range(PANEL):
            work = work - jnp.where(at > k + j, spread[j], 0.0) * rows[j]
    return work[:, n:] * (1.0 / jnp.sqrt(pivots[:, n:]))


def whole_sum(core, own_ref, other_ref, k):
    at = [row_of(k * ROWS + r) for r in range(ROWS)]
    own = jnp.concatenate([own_ref[:, a] for a in at], axis=0)
    other = jnp.concatenate([other_ref[:, a] for a in at], axis=0)
    rest = row_of(own_ref.shape[1] // LANES - 1)
    diagonals = jnp.where(core == 0, own_ref[:, rest], other_ref[:, rest])
    first = jnp.where(core == 0, own, other)
    second = jnp.where(core == 0, other, own)
    width = LANES // 4
    return unfold(jnp.concatenate([first, second], axis=0), diagonals[:, k * width : (k + 1) * width])


def normal_kernel(
    total_rows, table_ref, wanted_ref, own_ref, other_ref, image_ref, held, out_ref, tiles_ref,
):
    me, live = table_ref[ME], table_ref[LIVE]
    inverse = inverse_factor(whole_sum(me % 2, own_ref, other_ref, 0) / total_rows)
    for j in range(tiles_ref.shape[0]):
        tiles_ref[j] = jnp.dot(
            inverse, image_ref[j], precision=HIGHEST, preferred_element_type=jnp.float32
        ).astype(tiles_ref.dtype)
    multiply_mirrors(me, table_ref, live, tiles_ref, held, out_ref, lambda i: None, True)
    place_tiles(0, me, wanted_ref, tiles_ref, out_ref)


def last_kernel(total_rows, table_ref, own_ref, other_ref, image_ref, result_ref, projected_ref):
    core = table_ref[ME] % 2
    inverse = inverse_factor(whole_sum(core, own_ref, other_ref, 0) / total_rows)
    size = image_ref.shape[2]
    for j in range(image_ref.shape[0]):
        result_ref[:, j * size : (j + 1) * size] = jnp.dot(
            inverse, image_ref[j], precision=HIGHEST, preferred_element_type=jnp.float32
        )
    projected_ref[...] = whole_sum(core, own_ref, other_ref, 1) / total_rows


def spread_kernel(own_ref, given_ref, out_ref):
    chip = own_ref[...] + given_ref[...]
    for i in range(out_ref.shape[0]):
        out_ref[i] = chip


def total_kernel(parts_ref, out_ref):
    terms = [parts_ref[i] for i in range(parts_ref.shape[0])]
    while len(terms) > 1:
        terms = [a + b for a, b in zip(terms[::2], terms[1::2])] + terms[len(terms) // 2 * 2 :]
    out_ref[...] = terms[0]


def sum_over_devices(mine, given):
    swap = [(0, 1), (1, 0)]
    chips = lax.axis_size("rows")
    spread = pl.pallas_call(
        spread_kernel,
        out_shape=jax.ShapeDtypeStruct((chips,) + mine.shape, mine.dtype),
        in_specs=[VMEM] * 2,
        out_specs=VMEM,
        compiler_params=SMALL,
        name="spread",
    )(mine, lax.ppermute(given, "grp", swap))
    own = pl.pallas_call(
        total_kernel,
        out_shape=jax.ShapeDtypeStruct(mine.shape, mine.dtype),
        in_specs=[VMEM],
        out_specs=VMEM,
        compiler_params=SMALL,
        name="total",
    )(lax.all_to_all(spread, "rows", 0, 0, tiled=True))
    return own, lax.ppermute(own, "grp", swap)


def exchange(outgoing):
    return lax.all_to_all(outgoing, AXES, split_axis=0, concat_axis=0, tiled=True)


def on_device(start_basis, kernel_blocks, block_row, block_col, block_count):
    devices = lax.axis_size(AXES)
    me = lax.axis_index(AXES)
    slots, size, _ = kernel_blocks.shape
    own_rows, columns = start_basis.shape
    row_blocks = own_rows // size
    total_rows = own_rows * devices

    asked = pl.pallas_call(
        functools.partial(ask_kernel, row_blocks),
        out_shape=jax.ShapeDtypeStruct((devices, 1, 128), jnp.int32),
        in_specs=[SMEM, VMEM],
        out_specs=VMEM,
        compiler_params=SMALL,
        name="ask",
    )(block_count, block_col[None, :])
    wanted = exchange(asked)
    table = jnp.concatenate([me.reshape(1).astype(jnp.int32), block_count, block_row, block_col])

    params = pltpu.CompilerParams(vmem_limit_bytes=12 * MIB)
    tiles_shape = jax.ShapeDtypeStruct((row_blocks, columns, size), jnp.bfloat16)
    image_shape = jax.ShapeDtypeStruct((row_blocks, columns, size), jnp.float32)
    out_shape = jax.ShapeDtypeStruct((devices, columns, size), jnp.bfloat16)

    def image_of(tiles, arrived, blocks, with_projection):
        parts = 2 if with_projection else 1
        half = jax.ShapeDtypeStruct((1, (parts * ROWS + 1) * LANES), jnp.float32)
        turned = () if with_projection else (jax.ShapeDtypeStruct(blocks.shape, blocks.dtype),)
        return pl.pallas_call(
            functools.partial(image_kernel, with_projection),
            out_shape=(image_shape, half, half) + turned,
            in_specs=[SMEM] + [VMEM] * 4,
            out_specs=(VMEM,) * (3 + len(turned)),
            compiler_params=params,
            name="image",
        )(table, wanted, tiles, arrived, blocks)

    products, tiles = pl.pallas_call(
        first_kernel,
        out_shape=(jax.ShapeDtypeStruct((slots, columns, size), jnp.bfloat16), tiles_shape),
        in_specs=[SMEM] + [VMEM, ANY],
        out_specs=(VMEM, VMEM),
        scratch_shapes=[
            pltpu.VMEM(kernel_blocks.shape, kernel_blocks.dtype),
            pltpu.SemaphoreType.DMA((slots // CHUNK,)),
        ],
        compiler_params=LARGE,
        name="first",
    )(table, start_basis.T, kernel_blocks)
    outgoing = pl.pallas_call(
        place_kernel,
        out_shape=out_shape,
        in_specs=[SMEM] + [VMEM] * 3,
        out_specs=VMEM,
        compiler_params=params,
        name="place",
    )(table, wanted, tiles, products)
    image, own, given, turned = image_of(tiles, exchange(outgoing), kernel_blocks, False)
    own, other = sum_over_devices(own, given)
    outgoing, tiles = pl.pallas_call(
        functools.partial(normal_kernel, total_rows),
        out_shape=(out_shape, tiles_shape),
        in_specs=[SMEM] + [VMEM] * 5,
        out_specs=(VMEM, VMEM),
        compiler_params=params,
        name="normal",
    )(table, wanted, own, other, image, kernel_blocks)
    image, own, given = image_of(tiles, exchange(outgoing), turned, True)
    own, other = sum_over_devices(own, given)
    result, projected = pl.pallas_call(
        functools.partial(last_kernel, total_rows),
        out_shape=(
            jax.ShapeDtypeStruct((columns, own_rows), jnp.float32),
            jax.ShapeDtypeStruct((columns, columns), jnp.float32),
        ),
        in_specs=[SMEM] + [VMEM] * 3,
        out_specs=(VMEM, VMEM),
        compiler_params=params,
        name="last",
    )(table, own, other, image)
    return result.T, projected


def solution(mesh):
    in_specs = (
        P(AXES, None),
        P(AXES, None, None),
        P(AXES),
        P(AXES),
        P(AXES),
    )
    out_specs = (P(AXES, None), P())
    return jax.shard_map(
        on_device, mesh=mesh, in_specs=in_specs, out_specs=out_specs, check_vma=False
    )
```

```python
import functools

import jax
import jax.numpy as jnp
from jax import lax
from jax.experimental import pallas as pl
from jax.experimental.pallas import tpu as pltpu
from jax.sharding import PartitionSpec as P

AXES = ("rows", "grp")
HIGHEST = lax.Precision.HIGHEST
CHUNK = 23
PANEL = 8
ROWS, LANES = 8, 128
ME, LIVE, FIRST = 0, 1, 2
NT = (((1,), (1,)), ((), ()))
VMEM = pl.BlockSpec(memory_space=pltpu.VMEM)
SMEM = pl.BlockSpec(memory_space=pltpu.SMEM)
ANY = pl.BlockSpec(memory_space=pl.ANY)
MIB = 1024 * 1024
SMALL = pltpu.CompilerParams(vmem_limit_bytes=8 * MIB)
LARGE = pltpu.CompilerParams(vmem_limit_bytes=48 * MIB)


def block_copy(blocks_ref, held, sems, i):
    at = pl.ds(i * CHUNK, CHUNK)
    return pltpu.make_async_copy(blocks_ref.at[at], held.at[at], sems.at[i])


def start_blocks(live, blocks_ref, held, sems):
    def start(i, carry):
        block_copy(blocks_ref, held, sems, i).start()
        return carry

    lax.fori_loop(0, (live + CHUNK - 1) // CHUNK, start, 0)


def place_of(s, table_ref, live, row_blocks, slots):
    return jnp.where(s < live, table_ref[FIRST + slots + s] // row_blocks, 0)


def multiply_mirrors(me, table_ref, live, tiles_ref, held, out_ref, wait, placed):
    row_blocks = tiles_ref.shape[0]

    def visit(i, carry):
        wait(i)
        for j in range(CHUNK):
            s = i * CHUNK + j
            local = table_ref[FIRST + s] - me * row_blocks
            place = place_of(s, table_ref, live, row_blocks, held.shape[0]) if placed else s
            product = jnp.dot(tiles_ref[local], held[s], preferred_element_type=jnp.float32)
            out_ref[place] = product.astype(out_ref.dtype)
        return carry

    lax.fori_loop(0, (live + CHUNK - 1) // CHUNK, visit, 0)


def place_tiles(start, end, wanted_ref, tiles_ref, out_ref):
    tiles = [tiles_ref[j].astype(jnp.float32) for j in range(tiles_ref.shape[0])]
    group = 4

    def visit(i, carry):
        for j in range(group):
            d = jnp.minimum(start + i * group + j, end - 1)
            wanted = spread_lanes(wanted_ref[d], tiles[0].shape[1])
            tile = tiles[0]
            for k in range(1, len(tiles)):
                tile = jnp.where(wanted == k, tiles[k], tile)
            out_ref[d] = tile.astype(out_ref.dtype)
        return carry

    lax.fori_loop(0, (end - start + group - 1) // group, visit, 0)


def spread_lanes(row, width):
    return jnp.concatenate([row] * (width // row.shape[1]), axis=1)


def ask_kernel(row_blocks, count_ref, col_ref, out_ref):
    devices, slots = out_ref.shape[0], col_ref.shape[1]
    column = jnp.broadcast_to(col_ref[...], (devices, slots))
    owner = column // row_blocks
    device = lax.broadcasted_iota(jnp.int32, (devices, slots), 0)
    alive = lax.broadcasted_iota(jnp.int32, (devices, slots), 1) < count_ref[0]
    block = jnp.where((owner == device) & alive, column - owner * row_blocks, -1)
    asked = jnp.max(block, axis=1, keepdims=True)
    out_ref[...] = jnp.broadcast_to(asked, (devices, out_ref.shape[2]))[:, None, :]


def first_kernel(table_ref, basis_ref, blocks_ref, out_ref, tiles_ref, held, sems):
    live = table_ref[LIVE]
    start_blocks(live, blocks_ref, held, sems)
    row_blocks, _, size = tiles_ref.shape
    for j in range(row_blocks):
        tiles_ref[j] = basis_ref[:, j * size : (j + 1) * size]
    multiply_mirrors(
        table_ref[ME], table_ref, live, tiles_ref, held, out_ref,
        lambda i: block_copy(blocks_ref, held, sems, i).wait(), False,
    )


def place_kernel(table_ref, wanted_ref, tiles_ref, products_ref, out_ref):
    me, live = table_ref[ME], table_ref[LIVE]
    slots = products_ref.shape[0]
    group = 4

    def place(i, carry):
        for j in range(group):
            s = i * group + j
            out_ref[place_of(s, table_ref, live, tiles_ref.shape[0], slots)] = products_ref[s]
        return carry

    lax.fori_loop(0, (live + group - 1) // group, place, 0)
    place_tiles(0, me, wanted_ref, tiles_ref, out_ref)


def row_of(k):
    return slice(k * LANES, (k + 1) * LANES)


def fold(square):
    half = square.shape[0] // 2
    row_at = lax.broadcasted_iota(jnp.int32, (half, half), 0)
    col_at = lax.broadcasted_iota(jnp.int32, (half, half), 1)
    corner = square[half:, half:]
    mixed = jnp.where(row_at >= col_at, square[:half, :half], corner)
    sides = jnp.concatenate([mixed, square[half:, :half]], axis=1)
    folded = jnp.concatenate([sides[: half // 2], sides[half // 2 :]], axis=1)
    diagonal = jnp.sum(jnp.where(row_at == col_at, corner, 0.0), axis=0, keepdims=True)
    return folded, diagonal


def unfold(folded, diagonal):
    width = folded.shape[1] // 2
    half = width // 2
    row_at = lax.broadcasted_iota(jnp.int32, (half, half), 0)
    col_at = lax.broadcasted_iota(jnp.int32, (half, half), 1)
    sides = jnp.concatenate([folded[:, :width], folded[:, width:]], axis=0)
    mixed, side = sides[:, :half], sides[:, half:]
    turned = mixed.T
    upper = jnp.where(row_at >= col_at, mixed, turned)
    corner = jnp.where(row_at < col_at, mixed, turned)
    corner = jnp.where(row_at == col_at, jnp.broadcast_to(diagonal, (half, half)), corner)
    return jnp.concatenate(
        [jnp.concatenate([upper, side.T], axis=1), jnp.concatenate([side, corner], axis=1)], axis=0
    )


def image_kernel(
    with_projection, table_ref, wanted_ref, tiles_ref, arrived_ref, held,
    image_ref, own_ref, given_ref, *rest,
):
    me, live = table_ref[ME], table_ref[LIVE]
    row_blocks = tiles_ref.shape[0]
    turned_ref, sum_ref = rest[:-1], rest[-1]
    group = 4

    for part in range(image_ref.shape[2] // LANES):

        def add_mirrors(i, sums, at=row_of(part)):
            for j in range(group):
                d = i * group + j
                inside = jnp.minimum(d, me)
                wanted = jnp.where(d <= me, wanted_ref[inside], -1)
                mirror = arrived_ref[inside, :, at].astype(jnp.float32)
                sums = tuple(total + jnp.where(wanted == k, mirror, 0.0) for k, total in enumerate(sums))
            return sums

        zero = jnp.zeros((image_ref.shape[1], LANES), image_ref.dtype)
        sums = lax.fori_loop(0, (me + group) // group, add_mirrors, (zero,) * row_blocks)
        for k, total in enumerate(sums):
            sum_ref[k, :, row_of(part)] = total

    def visit(i, own_slot):
        for j in range(CHUNK):
            s = i * CHUNK + j
            owner = table_ref[FIRST + held.shape[0] + s] // row_blocks
            local = table_ref[FIRST + s] - me * row_blocks
            own_slot = jnp.where((owner == me) & (s < live), s, own_slot)
            place = jnp.where((owner == me) | (s >= live), row_blocks, local)
            block = held[s]
            if turned_ref:
                block = block.T
                turned_ref[0][s] = block
            sum_ref[place] += jnp.dot(arrived_ref[owner], block, preferred_element_type=jnp.float32)
        return own_slot

    own_slot = lax.fori_loop(0, (live + CHUNK - 1) // CHUNK, visit, jnp.int32(-1))

    @pl.when(own_slot >= 0)
    def _():
        local = table_ref[FIRST + own_slot] - me * row_blocks
        tile = tiles_ref[table_ref[FIRST + held.shape[0] + own_slot] - me * row_blocks]
        block = turned_ref[0][own_slot] if turned_ref else held[own_slot]
        sum_ref[local] += jnp.dot(tile, block, preferred_element_type=jnp.float32)

    for k in range(row_blocks):
        image_ref[k] = sum_ref[k]

    def summed(left_ref):
        total = None
        for j in range(image_ref.shape[0]):
            term = lax.dot_general(
                left_ref[j].astype(jnp.float32), image_ref[j], NT, precision=HIGHEST,
                preferred_element_type=jnp.float32,
            )
            total = term if total is None else total + term
        return total

    squares = [summed(image_ref)]
    if with_projection:
        product = summed(tiles_ref)
        squares.append((product + product.T) * 0.5)
    diagonals = []
    for k, square in enumerate(squares):
        folded, diagonal = fold(square)
        diagonals.append(diagonal)
        low, high = folded[:ROWS], folded[ROWS:]
        own, given = jnp.where(me % 2 == 0, low, high), jnp.where(me % 2 == 0, high, low)
        for r in range(ROWS):
            at = row_of(k * ROWS + r)
            own_ref[:, at] = own[r : r + 1]
            given_ref[:, at] = given[r : r + 1]
    rest = own_ref.shape[1] // LANES - 1
    missing = LANES - len(diagonals) * diagonals[0].shape[1]
    last = jnp.concatenate(diagonals + [jnp.zeros((1, missing), jnp.float32)], axis=1)
    own_ref[:, row_of(rest)] = last
    given_ref[:, row_of(rest)] = last


def inverse_factor(gram):
    n = gram.shape[0]
    row_at = lax.broadcasted_iota(jnp.int32, (n, n), 0)
    col_at = lax.broadcasted_iota(jnp.int32, (n, n), 1)
    work = jnp.concatenate([gram, (row_at == col_at).astype(jnp.float32)], axis=1)
    at = lax.broadcasted_iota(jnp.int32, work.shape, 0)
    pivots = jnp.zeros(work.shape, jnp.float32)
    for k in range(0, n, PANEL):
        spread = [jnp.broadcast_to(work[:, k + j : k + j + 1], work.shape) for j in range(PANEL)]
        rows = [work[k + j : k + j + 1, :] for j in range(PANEL)]
        for j in range(PANEL):
            pivot = spread[j][k + j : k + j + 1, :]
            pivots = jnp.where(at == k + j, pivot, pivots)
            share = 1.0 / pivot
            scaled = rows[j] * share
            for m in range(j + 1, PANEL):
                spread[m] = spread[m] - spread[j] * (spread[m][k + j : k + j + 1, :] * share)
                rows[m] = rows[m] - spread[j][k + m : k + m + 1, :] * scaled
            rows[j] = scaled
        for j in range(PANEL):
            work = work - jnp.where(at > k + j, spread[j], 0.0) * rows[j]
    return work[:, n:] * (1.0 / jnp.sqrt(pivots[:, n:]))


def whole_sum(core, own_ref, other_ref, k):
    at = [row_of(k * ROWS + r) for r in range(ROWS)]
    own = jnp.concatenate([own_ref[:, a] for a in at], axis=0)
    other = jnp.concatenate([other_ref[:, a] for a in at], axis=0)
    rest = row_of(own_ref.shape[1] // LANES - 1)
    diagonals = jnp.where(core == 0, own_ref[:, rest], other_ref[:, rest])
    first = jnp.where(core == 0, own, other)
    second = jnp.where(core == 0, other, own)
    width = LANES // 4
    return unfold(jnp.concatenate([first, second], axis=0), diagonals[:, k * width : (k + 1) * width])


def normal_kernel(
    total_rows, table_ref, wanted_ref, own_ref, other_ref, image_ref, held, out_ref, tiles_ref,
):
    me, live = table_ref[ME], table_ref[LIVE]
    inverse = inverse_factor(whole_sum(me % 2, own_ref, other_ref, 0) / total_rows)
    for j in range(tiles_ref.shape[0]):
        tiles_ref[j] = jnp.dot(
            inverse, image_ref[j], precision=HIGHEST, preferred_element_type=jnp.float32
        ).astype(tiles_ref.dtype)
    multiply_mirrors(me, table_ref, live, tiles_ref, held, out_ref, lambda i: None, True)
    place_tiles(0, me, wanted_ref, tiles_ref, out_ref)


def last_kernel(total_rows, table_ref, own_ref, other_ref, image_ref, result_ref, projected_ref):
    core = table_ref[ME] % 2
    inverse = inverse_factor(whole_sum(core, own_ref, other_ref, 0) / total_rows)
    size = image_ref.shape[2]
    for j in range(image_ref.shape[0]):
        result_ref[:, j * size : (j + 1) * size] = jnp.dot(
            inverse, image_ref[j], precision=HIGHEST, preferred_element_type=jnp.float32
        )
    projected_ref[...] = whole_sum(core, own_ref, other_ref, 1) / total_rows


def spread_kernel(own_ref, given_ref, out_ref):
    chip = own_ref[...] + given_ref[...]
    for i in range(out_ref.shape[0]):
        out_ref[i] = chip


def total_kernel(parts_ref, out_ref):
    terms = [parts_ref[i] for i in range(parts_ref.shape[0])]
    while len(terms) > 1:
        terms = [a + b for a, b in zip(terms[::2], terms[1::2])] + terms[len(terms) // 2 * 2 :]
    out_ref[...] = terms[0]


def sum_over_devices(mine, given):
    swap = [(0, 1), (1, 0)]
    chips = lax.axis_size("rows")
    spread = pl.pallas_call(
        spread_kernel,
        out_shape=jax.ShapeDtypeStruct((chips,) + mine.shape, mine.dtype),
        in_specs=[VMEM] * 2,
        out_specs=VMEM,
        compiler_params=SMALL,
        name="spread",
    )(mine, lax.ppermute(given, "grp", swap))
    own = pl.pallas_call(
        total_kernel,
        out_shape=jax.ShapeDtypeStruct(mine.shape, mine.dtype),
        in_specs=[VMEM],
        out_specs=VMEM,
        compiler_params=SMALL,
        name="total",
    )(lax.all_to_all(spread, "rows", 0, 0, tiled=True))
    return own, lax.ppermute(own, "grp", swap)


def exchange(outgoing):
    return lax.all_to_all(outgoing, AXES, split_axis=0, concat_axis=0, tiled=True)


def on_device(start_basis, kernel_blocks, block_row, block_col, block_count):
    devices = lax.axis_size(AXES)
    me = lax.axis_index(AXES)
    slots, size, _ = kernel_blocks.shape
    own_rows, columns = start_basis.shape
    row_blocks = own_rows // size
    total_rows = own_rows * devices

    asked = pl.pallas_call(
        functools.partial(ask_kernel, row_blocks),
        out_shape=jax.ShapeDtypeStruct((devices, 1, 128), jnp.int32),
        in_specs=[SMEM, VMEM],
        out_specs=VMEM,
        compiler_params=SMALL,
        name="ask",
    )(block_count, block_col[None, :])
    wanted = exchange(asked)
    table = jnp.concatenate([me.reshape(1).astype(jnp.int32), block_count, block_row, block_col])

    params = pltpu.CompilerParams(vmem_limit_bytes=12 * MIB)
    tiles_shape = jax.ShapeDtypeStruct((row_blocks, columns, size), jnp.bfloat16)
    image_shape = jax.ShapeDtypeStruct((row_blocks, columns, size), jnp.float32)
    out_shape = jax.ShapeDtypeStruct((devices, columns, size), jnp.bfloat16)

    def image_of(tiles, arrived, blocks, with_projection):
        parts = 2 if with_projection else 1
        half = jax.ShapeDtypeStruct((1, (parts * ROWS + 1) * LANES), jnp.float32)
        turned = () if with_projection else (jax.ShapeDtypeStruct(blocks.shape, blocks.dtype),)
        return pl.pallas_call(
            functools.partial(image_kernel, with_projection),
            out_shape=(image_shape, half, half) + turned,
            in_specs=[SMEM] + [VMEM] * 4,
            out_specs=(VMEM,) * (3 + len(turned)),
            scratch_shapes=[pltpu.VMEM((row_blocks + 1, columns, size), jnp.float32)],
            compiler_params=params,
            name="image",
        )(table, wanted, tiles, arrived, blocks)

    products, tiles = pl.pallas_call(
        first_kernel,
        out_shape=(jax.ShapeDtypeStruct((slots, columns, size), jnp.bfloat16), tiles_shape),
        in_specs=[SMEM] + [VMEM, ANY],
        out_specs=(VMEM, VMEM),
        scratch_shapes=[
            pltpu.VMEM(kernel_blocks.shape, kernel_blocks.dtype),
            pltpu.SemaphoreType.DMA((slots // CHUNK,)),
        ],
        compiler_params=LARGE,
        name="first",
    )(table, start_basis.T, kernel_blocks)
    outgoing = pl.pallas_call(
        place_kernel,
        out_shape=out_shape,
        in_specs=[SMEM] + [VMEM] * 3,
        out_specs=VMEM,
        compiler_params=params,
        name="place",
    )(table, wanted, tiles, products)
    image, own, given, turned = image_of(tiles, exchange(outgoing), kernel_blocks, False)
    own, other = sum_over_devices(own, given)
    outgoing, tiles = pl.pallas_call(
        functools.partial(normal_kernel, total_rows),
        out_shape=(out_shape, tiles_shape),
        in_specs=[SMEM] + [VMEM] * 5,
        out_specs=(VMEM, VMEM),
        compiler_params=params,
        name="normal",
    )(table, wanted, own, other, image, kernel_blocks)
    image, own, given = image_of(tiles, exchange(outgoing), turned, True)
    own, other = sum_over_devices(own, given)
    result, projected = pl.pallas_call(
        functools.partial(last_kernel, total_rows),
        out_shape=(
            jax.ShapeDtypeStruct((columns, own_rows), jnp.float32),
            jax.ShapeDtypeStruct((columns, columns), jnp.float32),
        ),
        in_specs=[SMEM] + [VMEM] * 3,
        out_specs=(VMEM, VMEM),
        compiler_params=params,
        name="last",
    )(table, own, other, image)
    return result.T, projected


def solution(mesh):
    in_specs = (
        P(AXES, None),
        P(AXES, None, None),
        P(AXES),
        P(AXES),
        P(AXES),
    )
    out_specs = (P(AXES, None), P())
    return jax.shard_map(
        on_device, mesh=mesh, in_specs=in_specs, out_specs=out_specs, check_vma=False
    )
```

```python
import functools

import jax
import jax.numpy as jnp
from jax import lax
from jax.experimental import pallas as pl
from jax.experimental.pallas import tpu as pltpu
from jax.sharding import PartitionSpec as P

AXES = ("rows", "grp")
HIGHEST = lax.Precision.HIGHEST
CHUNK, FEW = 23, 6
PANEL = 8
ROWS, LANES = 8, 128
ME, LIVE, FIRST = 0, 1, 2
NT = (((1,), (1,)), ((), ()))
VMEM = pl.BlockSpec(memory_space=pltpu.VMEM)
SMEM = pl.BlockSpec(memory_space=pltpu.SMEM)
ANY = pl.BlockSpec(memory_space=pl.ANY)
MIB = 1024 * 1024
SMALL = pltpu.CompilerParams(vmem_limit_bytes=8 * MIB)
LARGE = pltpu.CompilerParams(vmem_limit_bytes=48 * MIB)


def block_copy(blocks_ref, held, sems, i):
    at = pl.ds(i * CHUNK, CHUNK)
    return pltpu.make_async_copy(blocks_ref.at[at], held.at[at], sems.at[i])


def start_blocks(live, blocks_ref, held, sems):
    def start(i, carry):
        block_copy(blocks_ref, held, sems, i).start()
        return carry

    lax.fori_loop(0, (live + CHUNK - 1) // CHUNK, start, 0)


def place_of(s, table_ref, live, row_blocks, slots):
    return jnp.where(s < live, table_ref[FIRST + slots + s] // row_blocks, 0)


def over_slots(live, turn):
    full = (live + CHUNK - 2 * FEW - 1) // CHUNK

    def whole(i, carry):
        turn(i * CHUNK, CHUNK)
        return carry

    def part(i, carry):
        turn(full * CHUNK + i * FEW, FEW)
        return carry

    lax.fori_loop(0, full, whole, 0)
    lax.fori_loop(0, (jnp.maximum(live - full * CHUNK, 0) + FEW - 1) // FEW, part, 0)


def multiply_mirrors(me, table_ref, live, tiles_ref, held, out_ref, placed, first, count):
    row_blocks = tiles_ref.shape[0]
    for j in range(count):
        s = first + j
        local = table_ref[FIRST + s] - me * row_blocks
        place = place_of(s, table_ref, live, row_blocks, held.shape[0]) if placed else s
        product = jnp.dot(tiles_ref[local], held[s], preferred_element_type=jnp.float32)
        out_ref[place] = product.astype(out_ref.dtype)


def place_tiles(start, end, wanted_ref, tiles_ref, out_ref):
    tiles = [tiles_ref[j].astype(jnp.float32) for j in range(tiles_ref.shape[0])]
    group = 4

    def visit(i, carry):
        for j in range(group):
            d = jnp.minimum(start + i * group + j, end - 1)
            wanted = spread_lanes(wanted_ref[d], tiles[0].shape[1])
            tile = tiles[0]
            for k in range(1, len(tiles)):
                tile = jnp.where(wanted == k, tiles[k], tile)
            out_ref[d] = tile.astype(out_ref.dtype)
        return carry

    lax.fori_loop(0, (end - start + group - 1) // group, visit, 0)


def spread_lanes(row, width):
    return jnp.concatenate([row] * (width // row.shape[1]), axis=1)


def ask_kernel(row_blocks, count_ref, col_ref, out_ref):
    devices, slots = out_ref.shape[0], col_ref.shape[1]
    column = jnp.broadcast_to(col_ref[...], (devices, slots))
    owner = column // row_blocks
    device = lax.broadcasted_iota(jnp.int32, (devices, slots), 0)
    alive = lax.broadcasted_iota(jnp.int32, (devices, slots), 1) < count_ref[0]
    block = jnp.where((owner == device) & alive, column - owner * row_blocks, -1)
    asked = jnp.max(block, axis=1, keepdims=True)
    out_ref[...] = jnp.broadcast_to(asked, (devices, out_ref.shape[2]))[:, None, :]


def first_kernel(table_ref, basis_ref, blocks_ref, out_ref, tiles_ref, held, sems):
    live = table_ref[LIVE]
    start_blocks(live, blocks_ref, held, sems)
    row_blocks, _, size = tiles_ref.shape
    for j in range(row_blocks):
        tiles_ref[j] = basis_ref[:, j * size : (j + 1) * size]

    def visit(i, carry):
        block_copy(blocks_ref, held, sems, i).wait()
        multiply_mirrors(table_ref[ME], table_ref, live, tiles_ref, held, out_ref, False, i * CHUNK, CHUNK)
        return carry

    lax.fori_loop(0, (live + CHUNK - 1) // CHUNK, visit, 0)


def place_kernel(table_ref, wanted_ref, tiles_ref, products_ref, out_ref):
    me, live = table_ref[ME], table_ref[LIVE]
    slots = products_ref.shape[0]
    group = 4

    def place(i, carry):
        for j in range(group):
            s = i * group + j
            out_ref[place_of(s, table_ref, live, tiles_ref.shape[0], slots)] = products_ref[s]
        return carry

    lax.fori_loop(0, (live + group - 1) // group, place, 0)
    place_tiles(0, me, wanted_ref, tiles_ref, out_ref)


def row_of(k):
    return slice(k * LANES, (k + 1) * LANES)


def fold(square):
    half = square.shape[0] // 2
    row_at = lax.broadcasted_iota(jnp.int32, (half, half), 0)
    col_at = lax.broadcasted_iota(jnp.int32, (half, half), 1)
    corner = square[half:, half:]
    mixed = jnp.where(row_at >= col_at, square[:half, :half], corner)
    sides = jnp.concatenate([mixed, square[half:, :half]], axis=1)
    folded = jnp.concatenate([sides[: half // 2], sides[half // 2 :]], axis=1)
    diagonal = jnp.sum(jnp.where(row_at == col_at, corner, 0.0), axis=0, keepdims=True)
    return folded, diagonal


def unfold(folded, diagonal):
    width = folded.shape[1] // 2
    half = width // 2
    row_at = lax.broadcasted_iota(jnp.int32, (half, half), 0)
    col_at = lax.broadcasted_iota(jnp.int32, (half, half), 1)
    sides = jnp.concatenate([folded[:, :width], folded[:, width:]], axis=0)
    mixed, side = sides[:, :half], sides[:, half:]
    turned = mixed.T
    upper = jnp.where(row_at >= col_at, mixed, turned)
    corner = jnp.where(row_at < col_at, mixed, turned)
    corner = jnp.where(row_at == col_at, jnp.broadcast_to(diagonal, (half, half)), corner)
    return jnp.concatenate(
        [jnp.concatenate([upper, side.T], axis=1), jnp.concatenate([side, corner], axis=1)], axis=0
    )


def image_kernel(
    with_projection, table_ref, wanted_ref, tiles_ref, arrived_ref, held,
    image_ref, own_ref, given_ref, *turned_ref,
):
    me, live = table_ref[ME], table_ref[LIVE]
    row_blocks = tiles_ref.shape[0]

    group = 4

    for part in range(image_ref.shape[2] // LANES):

        def add_mirrors(i, sums, at=row_of(part)):
            for j in range(group):
                d = i * group + j
                inside = jnp.minimum(d, me)
                wanted = jnp.where(d <= me, wanted_ref[inside], -1)
                mirror = arrived_ref[inside, :, at].astype(jnp.float32)
                sums = tuple(total + jnp.where(wanted == k, mirror, 0.0) for k, total in enumerate(sums))
            return sums

        zero = jnp.zeros((image_ref.shape[1], LANES), image_ref.dtype)
        sums = lax.fori_loop(0, (me + group) // group, add_mirrors, (zero,) * row_blocks)
        for k, total in enumerate(sums):
            image_ref[k, :, row_of(part)] = total

    def visit(first, count):
        for j in range(count):
            s = first + j
            local = table_ref[FIRST + s] - me * row_blocks
            column = table_ref[FIRST + held.shape[0] + s]
            owner = column // row_blocks
            tile = jnp.where(owner == me, tiles_ref[column - owner * row_blocks], arrived_ref[owner])
            tile = jnp.where(s < live, tile, jnp.zeros_like(tile))
            block = held[s]
            if turned_ref:
                block = block.T
                turned_ref[0][s] = block
            image_ref[local] += jnp.dot(tile, block, preferred_element_type=jnp.float32)

    over_slots(live, visit)

    def summed(left_ref):
        total = None
        for j in range(image_ref.shape[0]):
            term = lax.dot_general(
                left_ref[j].astype(jnp.float32), image_ref[j], NT, precision=HIGHEST,
                preferred_element_type=jnp.float32,
            )
            total = term if total is None else total + term
        return total

    squares = [summed(image_ref)]
    if with_projection:
        product = summed(tiles_ref)
        squares.append((product + product.T) * 0.5)
    diagonals = []
    for k, square in enumerate(squares):
        folded, diagonal = fold(square)
        diagonals.append(diagonal)
        low, high = folded[:ROWS], folded[ROWS:]
        own, given = jnp.where(me % 2 == 0, low, high), jnp.where(me % 2 == 0, high, low)
        for r in range(ROWS):
            at = row_of(k * ROWS + r)
            own_ref[:, at] = own[r : r + 1]
            given_ref[:, at] = given[r : r + 1]
    rest = own_ref.shape[1] // LANES - 1
    missing = LANES - len(diagonals) * diagonals[0].shape[1]
    last = jnp.concatenate(diagonals + [jnp.zeros((1, missing), jnp.float32)], axis=1)
    own_ref[:, row_of(rest)] = last
    given_ref[:, row_of(rest)] = last


def inverse_factor(gram):
    n = gram.shape[0]
    row_at = lax.broadcasted_iota(jnp.int32, (n, n), 0)
    col_at = lax.broadcasted_iota(jnp.int32, (n, n), 1)
    work = jnp.concatenate([gram, (row_at == col_at).astype(jnp.float32)], axis=1)
    at = lax.broadcasted_iota(jnp.int32, work.shape, 0)
    pivots = jnp.zeros(work.shape, jnp.float32)
    for k in range(0, n, PANEL):
        spread = [jnp.broadcast_to(work[:, k + j : k + j + 1], work.shape) for j in range(PANEL)]
        rows = [work[k + j : k + j + 1, :] for j in range(PANEL)]
        for j in range(PANEL):
            pivot = spread[j][k + j : k + j + 1, :]
            pivots = jnp.where(at == k + j, pivot, pivots)
            share = 1.0 / pivot
            scaled = rows[j] * share
            for m in range(j + 1, PANEL):
                spread[m] = spread[m] - spread[j] * (spread[m][k + j : k + j + 1, :] * share)
                rows[m] = rows[m] - spread[j][k + m : k + m + 1, :] * scaled
            rows[j] = scaled
        for j in range(PANEL):
            work = work - jnp.where(at > k + j, spread[j], 0.0) * rows[j]
    return work[:, n:] * (1.0 / jnp.sqrt(pivots[:, n:]))


def whole_sum(core, own_ref, other_ref, k):
    at = [row_of(k * ROWS + r) for r in range(ROWS)]
    own = jnp.concatenate([own_ref[:, a] for a in at], axis=0)
    other = jnp.concatenate([other_ref[:, a] for a in at], axis=0)
    rest = row_of(own_ref.shape[1] // LANES - 1)
    diagonals = jnp.where(core == 0, own_ref[:, rest], other_ref[:, rest])
    first = jnp.where(core == 0, own, other)
    second = jnp.where(core == 0, other, own)
    width = LANES // 4
    return unfold(jnp.concatenate([first, second], axis=0), diagonals[:, k * width : (k + 1) * width])


def normal_kernel(
    total_rows, table_ref, wanted_ref, own_ref, other_ref, image_ref, held, out_ref, tiles_ref,
):
    me, live = table_ref[ME], table_ref[LIVE]
    inverse = inverse_factor(whole_sum(me % 2, own_ref, other_ref, 0) / total_rows)
    for j in range(tiles_ref.shape[0]):
        tiles_ref[j] = jnp.dot(
            inverse, image_ref[j], precision=HIGHEST, preferred_element_type=jnp.float32
        ).astype(tiles_ref.dtype)
    over_slots(live, functools.partial(multiply_mirrors, me, table_ref, live, tiles_ref, held, out_ref, True))
    place_tiles(0, me, wanted_ref, tiles_ref, out_ref)


def last_kernel(total_rows, table_ref, own_ref, other_ref, image_ref, result_ref, projected_ref):
    core = table_ref[ME] % 2
    inverse = inverse_factor(whole_sum(core, own_ref, other_ref, 0) / total_rows)
    size = image_ref.shape[2]
    for j in range(image_ref.shape[0]):
        result_ref[:, j * size : (j + 1) * size] = jnp.dot(
            inverse, image_ref[j], precision=HIGHEST, preferred_element_type=jnp.float32
        )
    projected_ref[...] = whole_sum(core, own_ref, other_ref, 1) / total_rows


def spread_kernel(own_ref, given_ref, out_ref):
    chip = own_ref[...] + given_ref[...]
    for i in range(out_ref.shape[0]):
        out_ref[i] = chip


def total_kernel(parts_ref, out_ref):
    terms = [parts_ref[i] for i in range(parts_ref.shape[0])]
    while len(terms) > 1:
        terms = [a + b for a, b in zip(terms[::2], terms[1::2])] + terms[len(terms) // 2 * 2 :]
    out_ref[...] = terms[0]


def sum_over_devices(mine, given):
    swap = [(0, 1), (1, 0)]
    chips = lax.axis_size("rows")
    spread = pl.pallas_call(
        spread_kernel,
        out_shape=jax.ShapeDtypeStruct((chips,) + mine.shape, mine.dtype),
        in_specs=[VMEM] * 2,
        out_specs=VMEM,
        compiler_params=SMALL,
        name="spread",
    )(mine, lax.ppermute(given, "grp", swap))
    own = pl.pallas_call(
        total_kernel,
        out_shape=jax.ShapeDtypeStruct(mine.shape, mine.dtype),
        in_specs=[VMEM],
        out_specs=VMEM,
        compiler_params=SMALL,
        name="total",
    )(lax.all_to_all(spread, "rows", 0, 0, tiled=True))
    return own, lax.ppermute(own, "grp", swap)


def exchange(outgoing):
    return lax.all_to_all(outgoing, AXES, split_axis=0, concat_axis=0, tiled=True)


def on_device(start_basis, kernel_blocks, block_row, block_col, block_count):
    devices = lax.axis_size(AXES)
    me = lax.axis_index(AXES)
    slots, size, _ = kernel_blocks.shape
    own_rows, columns = start_basis.shape
    row_blocks = own_rows // size
    total_rows = own_rows * devices

    asked = pl.pallas_call(
        functools.partial(ask_kernel, row_blocks),
        out_shape=jax.ShapeDtypeStruct((devices, 1, 128), jnp.int32),
        in_specs=[SMEM, VMEM],
        out_specs=VMEM,
        compiler_params=SMALL,
        name="ask",
    )(block_count, block_col[None, :])
    wanted = exchange(asked)
    table = jnp.concatenate([me.reshape(1).astype(jnp.int32), block_count, block_row, block_col])

    params = pltpu.CompilerParams(vmem_limit_bytes=12 * MIB)
    tiles_shape = jax.ShapeDtypeStruct((row_blocks, columns, size), jnp.bfloat16)
    image_shape = jax.ShapeDtypeStruct((row_blocks, columns, size), jnp.float32)
    out_shape = jax.ShapeDtypeStruct((devices, columns, size), jnp.bfloat16)

    def image_of(tiles, arrived, blocks, with_projection):
        parts = 2 if with_projection else 1
        half = jax.ShapeDtypeStruct((1, (parts * ROWS + 1) * LANES), jnp.float32)
        turned = () if with_projection else (jax.ShapeDtypeStruct(blocks.shape, blocks.dtype),)
        return pl.pallas_call(
            functools.partial(image_kernel, with_projection),
            out_shape=(image_shape, half, half) + turned,
            in_specs=[SMEM] + [VMEM] * 4,
            out_specs=(VMEM,) * (3 + len(turned)),
            compiler_params=params,
            name="image",
        )(table, wanted, tiles, arrived, blocks)

    products, tiles = pl.pallas_call(
        first_kernel,
        out_shape=(jax.ShapeDtypeStruct((slots, columns, size), jnp.bfloat16), tiles_shape),
        in_specs=[SMEM] + [VMEM, ANY],
        out_specs=(VMEM, VMEM),
        scratch_shapes=[
            pltpu.VMEM(kernel_blocks.shape, kernel_blocks.dtype),
            pltpu.SemaphoreType.DMA((slots // CHUNK,)),
        ],
        compiler_params=LARGE,
        name="first",
    )(table, start_basis.T, kernel_blocks)
    outgoing = pl.pallas_call(
        place_kernel,
        out_shape=out_shape,
        in_specs=[SMEM] + [VMEM] * 3,
        out_specs=VMEM,
        compiler_params=params,
        name="place",
    )(table, wanted, tiles, products)
    image, own, given, turned = image_of(tiles, exchange(outgoing), kernel_blocks, False)
    own, other = sum_over_devices(own, given)
    outgoing, tiles = pl.pallas_call(
        functools.partial(normal_kernel, total_rows),
        out_shape=(out_shape, tiles_shape),
        in_specs=[SMEM] + [VMEM] * 5,
        out_specs=(VMEM, VMEM),
        compiler_params=params,
        name="normal",
    )(table, wanted, own, other, image, kernel_blocks)
    image, own, given = image_of(tiles, exchange(outgoing), turned, True)
    own, other = sum_over_devices(own, given)
    result, projected = pl.pallas_call(
        functools.partial(last_kernel, total_rows),
        out_shape=(
            jax.ShapeDtypeStruct((columns, own_rows), jnp.float32),
            jax.ShapeDtypeStruct((columns, columns), jnp.float32),
        ),
        in_specs=[SMEM] + [VMEM] * 3,
        out_specs=(VMEM, VMEM),
        compiler_params=params,
        name="last",
    )(table, own, other, image)
    return result.T, projected


def solution(mesh):
    in_specs = (
        P(AXES, None),
        P(AXES, None, None),
        P(AXES),
        P(AXES),
        P(AXES),
    )
    out_specs = (P(AXES, None), P())
    return jax.shard_map(
        on_device, mesh=mesh, in_specs=in_specs, out_specs=out_specs, check_vma=False
    )
```

```python
import functools

import jax
import jax.numpy as jnp
from jax import lax
from jax.experimental import pallas as pl
from jax.experimental.pallas import tpu as pltpu
from jax.sharding import PartitionSpec as P

AXES = ("rows", "grp")
HIGHEST = lax.Precision.HIGHEST
CHUNK, FEW = 23, 6
PANEL = 8
ROWS, LANES = 8, 128
ME, LIVE, FIRST = 0, 1, 2
NT = (((1,), (1,)), ((), ()))
VMEM = pl.BlockSpec(memory_space=pltpu.VMEM)
SMEM = pl.BlockSpec(memory_space=pltpu.SMEM)
ANY = pl.BlockSpec(memory_space=pl.ANY)
MIB = 1024 * 1024
SMALL = pltpu.CompilerParams(vmem_limit_bytes=8 * MIB)
LARGE = pltpu.CompilerParams(vmem_limit_bytes=48 * MIB)


def block_copy(blocks_ref, held, sems, i):
    at = pl.ds(i * CHUNK, CHUNK)
    return pltpu.make_async_copy(blocks_ref.at[at], held.at[at], sems.at[i])


def start_blocks(live, blocks_ref, held, sems):
    def start(i, carry):
        block_copy(blocks_ref, held, sems, i).start()
        return carry

    lax.fori_loop(0, (live + CHUNK - 1) // CHUNK, start, 0)


def place_of(s, table_ref, live, row_blocks, slots):
    return jnp.where(s < live, table_ref[FIRST + slots + s] // row_blocks, 0)


def over_slots(live, turn):
    full = (live + CHUNK - 2 * FEW - 1) // CHUNK

    def double(i, carry):
        turn(i * 2 * CHUNK, 2 * CHUNK)
        return carry

    def whole(i, carry):
        turn(i * CHUNK, CHUNK)
        return carry

    def part(i, carry):
        turn(full * CHUNK + i * FEW, FEW)
        return carry

    lax.fori_loop(0, full // 2, double, 0)
    lax.fori_loop(full // 2 * 2, full, whole, 0)
    lax.fori_loop(0, (jnp.maximum(live - full * CHUNK, 0) + FEW - 1) // FEW, part, 0)


def multiply_mirrors(me, table_ref, live, tiles_ref, held, out_ref, placed, first, count):
    row_blocks = tiles_ref.shape[0]
    for j in range(count):
        s = first + j
        local = table_ref[FIRST + s] - me * row_blocks
        place = place_of(s, table_ref, live, row_blocks, held.shape[0]) if placed else s
        product = jnp.dot(tiles_ref[local], held[s], preferred_element_type=jnp.float32)
        out_ref[place] = product.astype(out_ref.dtype)


def place_tiles(start, end, wanted_ref, tiles_ref, out_ref):
    tiles = [tiles_ref[j].astype(jnp.float32) for j in range(tiles_ref.shape[0])]
    group = 4

    def visit(i, carry):
        for j in range(group):
            d = jnp.minimum(start + i * group + j, end - 1)
            wanted = spread_lanes(wanted_ref[d], tiles[0].shape[1])
            tile = tiles[0]
            for k in range(1, len(tiles)):
                tile = jnp.where(wanted == k, tiles[k], tile)
            out_ref[d] = tile.astype(out_ref.dtype)
        return carry

    lax.fori_loop(0, (end - start + group - 1) // group, visit, 0)


def spread_lanes(row, width):
    return jnp.concatenate([row] * (width // row.shape[1]), axis=1)


def ask_kernel(row_blocks, count_ref, col_ref, out_ref):
    devices, slots = out_ref.shape[0], col_ref.shape[1]
    column = jnp.broadcast_to(col_ref[...], (devices, slots))
    owner = column // row_blocks
    device = lax.broadcasted_iota(jnp.int32, (devices, slots), 0)
    alive = lax.broadcasted_iota(jnp.int32, (devices, slots), 1) < count_ref[0]
    block = jnp.where((owner == device) & alive, column - owner * row_blocks, -1)
    asked = jnp.max(block, axis=1, keepdims=True)
    out_ref[...] = jnp.broadcast_to(asked, (devices, out_ref.shape[2]))[:, None, :]


def first_kernel(table_ref, basis_ref, blocks_ref, out_ref, tiles_ref, held, sems):
    live = table_ref[LIVE]
    start_blocks(live, blocks_ref, held, sems)
    row_blocks, _, size = tiles_ref.shape
    for j in range(row_blocks):
        tiles_ref[j] = basis_ref[:, j * size : (j + 1) * size]

    def visit(i, carry):
        block_copy(blocks_ref, held, sems, i).wait()
        multiply_mirrors(table_ref[ME], table_ref, live, tiles_ref, held, out_ref, False, i * CHUNK, CHUNK)
        return carry

    lax.fori_loop(0, (live + CHUNK - 1) // CHUNK, visit, 0)


def place_kernel(table_ref, wanted_ref, tiles_ref, products_ref, out_ref):
    me, live = table_ref[ME], table_ref[LIVE]
    slots = products_ref.shape[0]
    group = 4

    def place(i, carry):
        for j in range(group):
            s = i * group + j
            out_ref[place_of(s, table_ref, live, tiles_ref.shape[0], slots)] = products_ref[s]
        return carry

    lax.fori_loop(0, (live + group - 1) // group, place, 0)
    place_tiles(0, me, wanted_ref, tiles_ref, out_ref)


def row_of(k):
    return slice(k * LANES, (k + 1) * LANES)


def fold(square):
    half = square.shape[0] // 2
    row_at = lax.broadcasted_iota(jnp.int32, (half, half), 0)
    col_at = lax.broadcasted_iota(jnp.int32, (half, half), 1)
    corner = square[half:, half:]
    mixed = jnp.where(row_at >= col_at, square[:half, :half], corner)
    sides = jnp.concatenate([mixed, square[half:, :half]], axis=1)
    folded = jnp.concatenate([sides[: half // 2], sides[half // 2 :]], axis=1)
    diagonal = jnp.sum(jnp.where(row_at == col_at, corner, 0.0), axis=0, keepdims=True)
    return folded, diagonal


def unfold(folded, diagonal):
    width = folded.shape[1] // 2
    half = width // 2
    row_at = lax.broadcasted_iota(jnp.int32, (half, half), 0)
    col_at = lax.broadcasted_iota(jnp.int32, (half, half), 1)
    sides = jnp.concatenate([folded[:, :width], folded[:, width:]], axis=0)
    mixed, side = sides[:, :half], sides[:, half:]
    turned = mixed.T
    upper = jnp.where(row_at >= col_at, mixed, turned)
    corner = jnp.where(row_at < col_at, mixed, turned)
    corner = jnp.where(row_at == col_at, jnp.broadcast_to(diagonal, (half, half)), corner)
    return jnp.concatenate(
        [jnp.concatenate([upper, side.T], axis=1), jnp.concatenate([side, corner], axis=1)], axis=0
    )


def image_kernel(
    with_projection, table_ref, wanted_ref, tiles_ref, arrived_ref, held,
    image_ref, own_ref, given_ref, *turned_ref,
):
    me, live = table_ref[ME], table_ref[LIVE]
    row_blocks = tiles_ref.shape[0]

    group = 4

    for part in range(image_ref.shape[2] // LANES):

        def add_mirrors(i, sums, at=row_of(part)):
            for j in range(group):
                d = i * group + j
                inside = jnp.minimum(d, me)
                wanted = jnp.where(d <= me, wanted_ref[inside], -1)
                mirror = arrived_ref[inside, :, at].astype(jnp.float32)
                sums = tuple(total + jnp.where(wanted == k, mirror, 0.0) for k, total in enumerate(sums))
            return sums

        zero = jnp.zeros((image_ref.shape[1], LANES), image_ref.dtype)
        sums = lax.fori_loop(0, (me + group) // group, add_mirrors, (zero,) * row_blocks)
        for k, total in enumerate(sums):
            image_ref[k, :, row_of(part)] = total

    def visit(first, count):
        for j in range(count):
            s = first + j
            local = table_ref[FIRST + s] - me * row_blocks
            column = table_ref[FIRST + held.shape[0] + s]
            owner = column // row_blocks
            tile = jnp.where(owner == me, tiles_ref[column - owner * row_blocks], arrived_ref[owner])
            tile = jnp.where(s < live, tile, jnp.zeros_like(tile))
            block = held[s]
            if turned_ref:
                block = block.T
                turned_ref[0][s] = block
            image_ref[local] += jnp.dot(tile, block, preferred_element_type=jnp.float32)

    over_slots(live, visit)

    def summed(left_ref):
        total = None
        for j in range(image_ref.shape[0]):
            term = lax.dot_general(
                left_ref[j].astype(jnp.float32), image_ref[j], NT, precision=HIGHEST,
                preferred_element_type=jnp.float32,
            )
            total = term if total is None else total + term
        return total

    squares = [summed(image_ref)]
    if with_projection:
        product = summed(tiles_ref)
        squares.append((product + product.T) * 0.5)
    diagonals = []
    for k, square in enumerate(squares):
        folded, diagonal = fold(square)
        diagonals.append(diagonal)
        low, high = folded[:ROWS], folded[ROWS:]
        own, given = jnp.where(me % 2 == 0, low, high), jnp.where(me % 2 == 0, high, low)
        for r in range(ROWS):
            at = row_of(k * ROWS + r)
            own_ref[:, at] = own[r : r + 1]
            given_ref[:, at] = given[r : r + 1]
    rest = own_ref.shape[1] // LANES - 1
    missing = LANES - len(diagonals) * diagonals[0].shape[1]
    last = jnp.concatenate(diagonals + [jnp.zeros((1, missing), jnp.float32)], axis=1)
    own_ref[:, row_of(rest)] = last
    given_ref[:, row_of(rest)] = last


def inverse_factor(gram):
    n = gram.shape[0]
    row_at = lax.broadcasted_iota(jnp.int32, (n, n), 0)
    col_at = lax.broadcasted_iota(jnp.int32, (n, n), 1)
    work = jnp.concatenate([gram, (row_at == col_at).astype(jnp.float32)], axis=1)
    at = lax.broadcasted_iota(jnp.int32, work.shape, 0)
    pivots = jnp.zeros(work.shape, jnp.float32)
    for k in range(0, n, PANEL):
        spread = [jnp.broadcast_to(work[:, k + j : k + j + 1], work.shape) for j in range(PANEL)]
        rows = [work[k + j : k + j + 1, :] for j in range(PANEL)]
        for j in range(PANEL):
            pivot = spread[j][k + j : k + j + 1, :]
            pivots = jnp.where(at == k + j, pivot, pivots)
            share = 1.0 / pivot
            scaled = rows[j] * share
            for m in range(j + 1, PANEL):
                spread[m] = spread[m] - spread[j] * (spread[m][k + j : k + j + 1, :] * share)
                rows[m] = rows[m] - spread[j][k + m : k + m + 1, :] * scaled
            rows[j] = scaled
        for j in range(PANEL):
            work = work - jnp.where(at > k + j, spread[j], 0.0) * rows[j]
    return work[:, n:] * (1.0 / jnp.sqrt(pivots[:, n:]))


def whole_sum(core, own_ref, other_ref, k):
    at = [row_of(k * ROWS + r) for r in range(ROWS)]
    own = jnp.concatenate([own_ref[:, a] for a in at], axis=0)
    other = jnp.concatenate([other_ref[:, a] for a in at], axis=0)
    rest = row_of(own_ref.shape[1] // LANES - 1)
    diagonals = jnp.where(core == 0, own_ref[:, rest], other_ref[:, rest])
    first = jnp.where(core == 0, own, other)
    second = jnp.where(core == 0, other, own)
    width = LANES // 4
    return unfold(jnp.concatenate([first, second], axis=0), diagonals[:, k * width : (k + 1) * width])


def normal_kernel(
    total_rows, table_ref, wanted_ref, own_ref, other_ref, image_ref, held, out_ref, tiles_ref,
):
    me, live = table_ref[ME], table_ref[LIVE]
    inverse = inverse_factor(whole_sum(me % 2, own_ref, other_ref, 0) / total_rows)
    for j in range(tiles_ref.shape[0]):
        tiles_ref[j] = jnp.dot(
            inverse, image_ref[j], precision=HIGHEST, preferred_element_type=jnp.float32
        ).astype(tiles_ref.dtype)
    over_slots(live, functools.partial(multiply_mirrors, me, table_ref, live, tiles_ref, held, out_ref, True))
    place_tiles(0, me, wanted_ref, tiles_ref, out_ref)


def last_kernel(total_rows, table_ref, own_ref, other_ref, image_ref, result_ref, projected_ref):
    core = table_ref[ME] % 2
    inverse = inverse_factor(whole_sum(core, own_ref, other_ref, 0) / total_rows)
    size = image_ref.shape[2]
    for j in range(image_ref.shape[0]):
        result_ref[:, j * size : (j + 1) * size] = jnp.dot(
            inverse, image_ref[j], precision=HIGHEST, preferred_element_type=jnp.float32
        )
    projected_ref[...] = whole_sum(core, own_ref, other_ref, 1) / total_rows


def spread_kernel(own_ref, given_ref, out_ref):
    chip = own_ref[...] + given_ref[...]
    for i in range(out_ref.shape[0]):
        out_ref[i] = chip


def total_kernel(parts_ref, out_ref):
    terms = [parts_ref[i] for i in range(parts_ref.shape[0])]
    while len(terms) > 1:
        terms = [a + b for a, b in zip(terms[::2], terms[1::2])] + terms[len(terms) // 2 * 2 :]
    out_ref[...] = terms[0]


def sum_over_devices(mine, given):
    swap = [(0, 1), (1, 0)]
    chips = lax.axis_size("rows")
    spread = pl.pallas_call(
        spread_kernel,
        out_shape=jax.ShapeDtypeStruct((chips,) + mine.shape, mine.dtype),
        in_specs=[VMEM] * 2,
        out_specs=VMEM,
        compiler_params=SMALL,
        name="spread",
    )(mine, lax.ppermute(given, "grp", swap))
    own = pl.pallas_call(
        total_kernel,
        out_shape=jax.ShapeDtypeStruct(mine.shape, mine.dtype),
        in_specs=[VMEM],
        out_specs=VMEM,
        compiler_params=SMALL,
        name="total",
    )(lax.all_to_all(spread, "rows", 0, 0, tiled=True))
    return own, lax.ppermute(own, "grp", swap)


def exchange(outgoing):
    return lax.all_to_all(outgoing, AXES, split_axis=0, concat_axis=0, tiled=True)


def on_device(start_basis, kernel_blocks, block_row, block_col, block_count):
    devices = lax.axis_size(AXES)
    me = lax.axis_index(AXES)
    slots, size, _ = kernel_blocks.shape
    own_rows, columns = start_basis.shape
    row_blocks = own_rows // size
    total_rows = own_rows * devices

    asked = pl.pallas_call(
        functools.partial(ask_kernel, row_blocks),
        out_shape=jax.ShapeDtypeStruct((devices, 1, 128), jnp.int32),
        in_specs=[SMEM, VMEM],
        out_specs=VMEM,
        compiler_params=SMALL,
        name="ask",
    )(block_count, block_col[None, :])
    wanted = exchange(asked)
    table = jnp.concatenate([me.reshape(1).astype(jnp.int32), block_count, block_row, block_col])

    params = pltpu.CompilerParams(vmem_limit_bytes=12 * MIB)
    tiles_shape = jax.ShapeDtypeStruct((row_blocks, columns, size), jnp.bfloat16)
    image_shape = jax.ShapeDtypeStruct((row_blocks, columns, size), jnp.float32)
    out_shape = jax.ShapeDtypeStruct((devices, columns, size), jnp.bfloat16)

    def image_of(tiles, arrived, blocks, with_projection):
        parts = 2 if with_projection else 1
        half = jax.ShapeDtypeStruct((1, (parts * ROWS + 1) * LANES), jnp.float32)
        turned = () if with_projection else (jax.ShapeDtypeStruct(blocks.shape, blocks.dtype),)
        return pl.pallas_call(
            functools.partial(image_kernel, with_projection),
            out_shape=(image_shape, half, half) + turned,
            in_specs=[SMEM] + [VMEM] * 4,
            out_specs=(VMEM,) * (3 + len(turned)),
            compiler_params=params,
            name="image",
        )(table, wanted, tiles, arrived, blocks)

    products, tiles = pl.pallas_call(
        first_kernel,
        out_shape=(jax.ShapeDtypeStruct((slots, columns, size), jnp.bfloat16), tiles_shape),
        in_specs=[SMEM] + [VMEM, ANY],
        out_specs=(VMEM, VMEM),
        scratch_shapes=[
            pltpu.VMEM(kernel_blocks.shape, kernel_blocks.dtype),
            pltpu.SemaphoreType.DMA((slots // CHUNK,)),
        ],
        compiler_params=LARGE,
        name="first",
    )(table, start_basis.T, kernel_blocks)
    outgoing = pl.pallas_call(
        place_kernel,
        out_shape=out_shape,
        in_specs=[SMEM] + [VMEM] * 3,
        out_specs=VMEM,
        compiler_params=params,
        name="place",
    )(table, wanted, tiles, products)
    image, own, given, turned = image_of(tiles, exchange(outgoing), kernel_blocks, False)
    own, other = sum_over_devices(own, given)
    outgoing, tiles = pl.pallas_call(
        functools.partial(normal_kernel, total_rows),
        out_shape=(out_shape, tiles_shape),
        in_specs=[SMEM] + [VMEM] * 5,
        out_specs=(VMEM, VMEM),
        compiler_params=params,
        name="normal",
    )(table, wanted, own, other, image, kernel_blocks)
    image, own, given = image_of(tiles, exchange(outgoing), turned, True)
    own, other = sum_over_devices(own, given)
    result, projected = pl.pallas_call(
        functools.partial(last_kernel, total_rows),
        out_shape=(
            jax.ShapeDtypeStruct((columns, own_rows), jnp.float32),
            jax.ShapeDtypeStruct((columns, columns), jnp.float32),
        ),
        in_specs=[SMEM] + [VMEM] * 3,
        out_specs=(VMEM, VMEM),
        compiler_params=params,
        name="last",
    )(table, own, other, image)
    return result.T, projected


def solution(mesh):
    in_specs = (
        P(AXES, None),
        P(AXES, None, None),
        P(AXES),
        P(AXES),
        P(AXES),
    )
    out_specs = (P(AXES, None), P())
    return jax.shard_map(
        on_device, mesh=mesh, in_specs=in_specs, out_specs=out_specs, check_vma=False
    )
```
